32 devices in a mesh: section: 2 (over core), dp: 8 (over z, x), tensor: 2 (over y).
Axes of the slice: x: 2, y: 2, z: 4, core: 2. Of those that a mesh axis runs over, the one named last changes fastest.
Arguments:
- inputs: bfloat16 [2, 4096, 768], P(None, 'dp', 'tensor'), may hold values from -6 to 6
- out_grads: bfloat16 [2, 4096, 768], P(None, 'dp', 'tensor'), may hold values from -6 to 6
- seq_blocks: int32 [2, 5], replicated, may hold values from 1 to 2, as said below
- ln1_gain: bfloat16 [768], P('tensor'), may hold values from 0.5 to 1.5
- ln1_shift: bfloat16 [768], P('tensor'), may hold values from -3 to 3
- qkv_weight: bfloat16 [768, 3, 768], P(None, None, 'tensor'), may hold values from -0.21875 to 0.21875
- qv_bias: bfloat16 [2, 768], P(None, 'tensor'), may hold values from -3 to 3
- out_weight: bfloat16 [768, 768], P('tensor'), may hold values from -1.25 to 1.25
- out_bias: bfloat16 [768], P('tensor'), may hold values from -3 to 3
- ln2_gain: bfloat16 [768], P('tensor'), may hold values from 0.5 to 1.5
- ln2_shift: bfloat16 [768], P('tensor'), may hold values from -3 to 3
- fc_weight: bfloat16 [768, 3072], P(None, 'tensor'), may hold values from -0.21875 to 0.21875
- fc_bias: bfloat16 [3072], P('tensor'), may hold values from -3 to 3
- proj_weight: bfloat16 [3072, 768], P('tensor'), may hold values from -0.109375 to 0.109375
- proj_bias: bfloat16 [768], P('tensor'), may hold values from -3 to 3
Outputs:
- acts: bfloat16 [2, 2, 4096, 768], P('section', None, 'dp', 'tensor')
- act_grads: float32 [2, 2, 4096, 768], P('section', None, 'dp', 'tensor')
- ln1_gain_grad: float32 [768], P('tensor')
- ln1_shift_grad: float32 [768], P('tensor')
- qkv_weight_grad: float32 [768, 3, 768], P(None, None, 'tensor')
- qv_bias_grad: float32 [2, 768], P(None, 'tensor')
- out_weight_grad: float32 [768, 768], P('tensor')
- out_bias_grad: float32 [768], P('tensor')
- ln2_gain_grad: float32 [768], P('tensor')
- ln2_shift_grad: float32 [768], P('tensor')
- fc_weight_grad: float32 [768, 3072], P(None, 'tensor')
- fc_bias_grad: float32 [3072], P('tensor')
- proj_weight_grad: float32 [3072, 768], P('tensor')
- proj_bias_grad: float32 [768], P('tensor')
The draws below stay inside these ranges and needn't reach their ends.
Inputs may be any that keep to these rules, and one draw needn't show every extreme that they name: `seq_blocks`: each row lists the lengths, in blocks of 512 tokens, of one micro-batch's sequences in order; each row sums to 8; in each row the first and the last entry are 2, and 3 entries are 2 in all.
All inputs are finite; a program needn't handle non-finite values.
Results may differ from the reference program's by a relative error of at most 0.019.
Values may be sent and summed in bfloat16 or wider, within the bound.
No kernel may reach another device: no remote copies, remote signals or barrier semaphores. Data moves between devices by JAX's collectives and lax.ppermute only.
A program may use at most 192 MiB of HBM per device.

```python
import jax
import jax.numpy as jnp
from jax import lax

D = 768
HEADS = 12
HEAD = 64
FF = 3072
BLOCK = 512
MICRO = 2
SEQROWS = 4096
SEQS = 5
N_DP = 8


def draw_seq_blocks(key, part):
    key = jax.random.fold_in(key, 11)
    middle_count = SEQS - 2
    long_middle = N_DP // 4 - 1
    row_keys = jax.random.split(key, MICRO)

    def one_row(row_key):
        shuffled = jax.random.permutation(row_key, middle_count)
        middle = jnp.where(shuffled < long_middle, 2, 1).astype(jnp.int32)
        edge_block = jnp.full((1,), 2, jnp.int32)
        return jnp.concatenate([edge_block, middle, edge_block])
    return jax.vmap(one_row)(row_keys)


def block_levels(stream_key, dims, pieces, low, largest):
    factor_of = 1.0
    for position, blocks in pieces:
        steps = jax.random.uniform(jax.random.fold_in(jax.random.fold_in(stream_key, 6), position), (blocks,), jnp.float32, low / len(pieces), largest / len(pieces))
        factor_of = factor_of * jnp.repeat(jnp.exp(steps), dims[position] // blocks).reshape((-1,) + (1,) * (len(dims) - 1 - position))
    return factor_of


def scatter_about(own_key, shape, deviation, bound, pieces=(), kind=jnp.bfloat16):
    drawn = deviation * jax.random.normal(own_key, shape, jnp.float32)
    if pieces:
        drawn = drawn * block_levels(own_key, shape, pieces, -0.22, 0.18)
    return jnp.clip(drawn, -bound, bound).astype(kind)


def setup_inputs(seed: int = 0) -> dict:
    streams_of = jax.random.split(jax.random.key(seed), 16)
    inputs = scatter_about(streams_of[0], (MICRO, SEQROWS, D), 1.0, 6.0, ((1, 8), (2, 2)))
    out_grads = scatter_about(streams_of[1], (MICRO, SEQROWS, D), 1.0, 6.0, ((1, 8), (2, 2)))
    seq_blocks = draw_seq_blocks(jax.random.fold_in(streams_of[15], 71), 0)
    ln1_gain = jnp.clip(1.0 + 0.1 * jax.random.normal(streams_of[3], (D,), jnp.float32), 0.5, 1.5).astype(jnp.bfloat16)
    ln1_shift = scatter_about(streams_of[4], (D,), 0.3, 3.0, ((0, 2),))
    qkv_weight = scatter_about(streams_of[5], (D, 3, D), D ** -0.5, 0.21875, ((2, 2),))
    qv_bias = scatter_about(streams_of[6], (2, D), 0.5, 3.0, ((1, 2),))
    out_weight = scatter_about(streams_of[7], (D, D), (D // 32) ** -0.5, 1.25, ((0, 2),))
    out_bias = scatter_about(streams_of[8], (D,), 0.3, 3.0, ((0, 2),))
    ln2_gain = jnp.clip(1.0 + 0.1 * jax.random.normal(streams_of[9], (D,), jnp.float32), 0.5, 1.5).astype(jnp.bfloat16)
    ln2_shift = scatter_about(streams_of[10], (D,), 0.3, 3.0, ((0, 2),))
    fc_weight = scatter_about(streams_of[11], (D, FF), D ** -0.5, 0.21875, ((1, 2),))
    fc_bias = scatter_about(streams_of[12], (FF,), 0.3, 3.0, ((0, 2),))
    proj_weight = scatter_about(streams_of[13], (FF, D), FF ** -0.5, 0.109375, ((0, 2),))
    proj_bias = scatter_about(streams_of[14], (D,), 0.3, 3.0, ((0, 2),))
    return dict(inputs=inputs, out_grads=out_grads, seq_blocks=seq_blocks, ln1_gain=ln1_gain, ln1_shift=ln1_shift, qkv_weight=qkv_weight, qv_bias=qv_bias, out_weight=out_weight, out_bias=out_bias, ln2_gain=ln2_gain, ln2_shift=ln2_shift, fc_weight=fc_weight, fc_bias=fc_bias, proj_weight=proj_weight, proj_bias=proj_bias)


@jax.custom_vjp
def low(v):
    return lax.optimization_barrier(v.astype(jnp.bfloat16)).astype(jnp.float32)

@jax.custom_vjp
def low_back(v):
    return v

def low_keep(v):
    return (low(v), None)

def low_pass(kept, grad):
    return (grad,)

def back_keep(v):
    return (v, None)

def back_low(kept, grad):
    return (low(grad),)
low.defvjp(low_keep, low_pass)
low_back.defvjp(back_keep, back_low)
NORM_EPSILON = 1e-05
HIGHEST = lax.Precision.HIGHEST

def layer_norm(residual, gain, shift):
    center = lax.optimization_barrier(jnp.mean(residual, axis=-1, keepdims=True))
    spread = lax.optimization_barrier(jnp.mean(residual * residual, axis=-1, keepdims=True)) - center * center
    return low((residual - center) * lax.rsqrt(spread + NORM_EPSILON) * gain + shift)

def attend_block(members):
    queries, prior_keys, prior_values, keys_own, values_own, continues = members
    all_keys = jnp.concatenate([prior_keys, keys_own], axis=0)
    all_values = jnp.concatenate([prior_values, values_own], axis=0)
    scores = jnp.einsum('qhd,khd->hqk', queries, all_keys, precision=HIGHEST) * HEAD ** (-0.5)
    scores = low_back(scores)
    row_index = jnp.arange(BLOCK)[:, None]
    col_index = jnp.arange(2 * BLOCK)[None, :]
    allowed = jnp.where(col_index < BLOCK, continues > 0, col_index - BLOCK <= row_index)
    scores = jnp.where(allowed[None], scores, -1e+30)
    row_max = lax.optimization_barrier(jnp.max(scores, axis=-1, keepdims=True))
    lifted = jnp.exp(scores - row_max)
    chances = low(lifted / lax.optimization_barrier(jnp.sum(lifted, axis=-1, keepdims=True)))
    return jnp.einsum('hqk,khd->qhd', chances, all_values, precision=HIGHEST)

def apply_layer(residual, continues, params):
    gain_one, shift_one, qkv_weight, qv_bias, out_weight, out_bias, gain_two, shift_two, fc_weight, fc_bias, proj_weight, proj_bias = params
    block_count = SEQROWS // BLOCK
    normed_one = layer_norm(residual, gain_one, shift_one)
    project = jnp.dot(normed_one, qkv_weight.reshape(D, 3 * D), precision=HIGHEST).reshape(SEQROWS, 3, D)
    queries = low(low_back(project[:, 0] + qv_bias[0]))
    keys_own = low(low_back(project[:, 1]))
    values_own = low(low_back(project[:, 2] + qv_bias[1]))
    block_shape = (block_count, BLOCK, HEADS, HEAD)
    queries = queries.reshape(block_shape)
    keys_own = keys_own.reshape(block_shape)
    values_own = values_own.reshape(block_shape)
    empty_block = jnp.zeros((1, BLOCK, HEADS, HEAD), jnp.float32)
    prior_keys = jnp.concatenate([empty_block, keys_own[:-1]], axis=0)
    prior_values = jnp.concatenate([empty_block, values_own[:-1]], axis=0)
    context = lax.map(jax.checkpoint(attend_block), (queries, prior_keys, prior_values, keys_own, values_own, continues))
    context = low(low_back(context.reshape(SEQROWS, D)))
    middle = residual + low_back(jnp.dot(context, out_weight, precision=HIGHEST) + out_bias)
    normed_two = layer_norm(middle, gain_two, shift_two)
    hidden_pre = low_back(jnp.dot(normed_two, fc_weight, precision=HIGHEST) + fc_bias)
    hidden = low(jax.nn.gelu(hidden_pre, approximate=True))
    return middle + low_back(jnp.dot(hidden, proj_weight, precision=HIGHEST) + proj_bias)

def reference(inputs, out_grads, seq_blocks, ln1_gain, ln1_shift, qkv_weight, qv_bias, out_weight, out_bias, ln2_gain, ln2_shift, fc_weight, fc_bias, proj_weight, proj_bias):
    params = tuple((member.astype(jnp.float32) for member in (ln1_gain, ln1_shift, qkv_weight, qv_bias, out_weight, out_bias, ln2_gain, ln2_shift, fc_weight, fc_bias, proj_weight, proj_bias)))
    block_ids = jnp.arange(SEQROWS // BLOCK, dtype=jnp.int32)
    totals = tuple((jnp.zeros_like(member) for member in params))
    first_acts, second_acts, first_grads, second_grads = ([], [], [], [])
    for micro_index in range(MICRO):
        lengths = seq_blocks[micro_index].astype(jnp.int32)
        starts = (jnp.cumsum(lengths) - lengths).astype(jnp.int32)
        continues = 1 - jnp.any(starts[:, None] == block_ids[None, :], axis=0).astype(jnp.int32)

        def run_layer(residual, weights):
            return apply_layer(residual, continues, weights)
        first_out, first_back = jax.vjp(run_layer, inputs[micro_index].astype(jnp.float32), params)
        middle = low(first_out)
        second_out, second_back = jax.vjp(run_layer, middle, params)
        grad_middle, grad_second = second_back(out_grads[micro_index].astype(jnp.float32))
        grad_middle = low(grad_middle)
        grad_input, grad_first = first_back(grad_middle)
        totals = tuple((running + one_grad + two_grad for running, one_grad, two_grad in zip(totals, grad_first, grad_second)))
        first_acts.append(middle)
        second_acts.append(second_out)
        first_grads.append(grad_input)
        second_grads.append(grad_middle)
    acts = jnp.stack([jnp.stack(first_acts), jnp.stack(second_acts)]).astype(jnp.bfloat16)
    act_grads = jnp.stack([jnp.stack(first_grads), jnp.stack(second_grads)])
    return (acts, act_grads, totals[0], totals[1], totals[2], totals[3], totals[4], totals[5], totals[6], totals[7], totals[8], totals[9], totals[10], totals[11])
```

```python
import jax
import jax.numpy as jnp
from jax import lax
from jax.sharding import PartitionSpec as P

D = 768
HEAD = 64
NORM_EPSILON = 1e-05
MASKED = -1e30
SCALE = HEAD ** (-0.5)
F32 = jnp.float32
BF16 = jnp.bfloat16


def dot(a, b, dims=((1,), (0,))):
    return lax.dot_general(a, b, (dims, ((), ())), preferred_element_type=F32)


def swap(array, axis):
    return lax.ppermute(array, axis, [(0, 1), (1, 0)])


def shift(array, by):
    count = lax.axis_size("dp")
    pairs = [(i, i + by) for i in range(count) if 0 <= i + by < count]
    return lax.ppermute(array, "dp", pairs)


def exchange(array, bit):
    count = lax.axis_size("dp")
    return lax.ppermute(array, "dp", [(i, i ^ bit) for i in range(count)])


def part(array, which, parts, axis=0):
    size = array.shape[axis] // parts
    return lax.dynamic_slice_in_dim(array, which * size, size, axis)


def ordered(first, mine, other, axis):
    ahead = jnp.concatenate([mine, other], axis=axis)
    behind = jnp.concatenate([other, mine], axis=axis)
    return jnp.where(first, ahead, behind)


def add_low(a, b):
    return (a.astype(F32) + b.astype(F32)).astype(BF16)


def reduce_grads(own, foreign):
    section = lax.axis_index("section")
    position = lax.axis_index("dp")
    both = jnp.stack([own, foreign])
    kept = add_low(part(both, section, 2, 1), swap(part(both, 1 - section, 2, 1), "section"))
    kept = add_low(kept[0], swap(kept[1], "tensor"))
    bit = 1
    while bit < lax.axis_size("dp"):
        side = (position // bit) % 2
        kept = add_low(part(kept, side, 2), exchange(part(kept, 1 - side, 2), bit))
        bit *= 2
    while bit > 1:
        bit //= 2
        side = (position // bit) % 2
        kept = ordered(side == 0, kept, exchange(kept, bit), 0)
    return ordered(section == 0, kept, swap(kept, "section"), 0)


def fetch_other(array):
    section = lax.axis_index("section")
    mine = swap(part(array, section, 2), "tensor")
    return ordered(section == 0, mine, swap(mine, "section"), 0)


def norm(rows, gain, shift_by):
    center = jnp.sum(rows, axis=1, keepdims=True) / D
    spread = jnp.sum(rows * rows, axis=1, keepdims=True) / D - center * center
    factor = lax.rsqrt(spread + NORM_EPSILON)
    normed = (rows - center) * factor
    return normed, factor, (normed * gain + shift_by).astype(BF16)


def norm_back(grad, normed, factor, gain):
    scaled = grad * gain
    mean = jnp.sum(scaled, axis=1, keepdims=True) / D
    along = jnp.sum(scaled * normed, axis=1, keepdims=True) / D
    return (
        factor * (scaled - mean - normed * along),
        jnp.sum(grad * normed, axis=0),
        jnp.sum(grad, axis=0),
    )


def heads(array):
    return array.reshape(array.shape[0], -1, HEAD)


def gather_rows(own):
    section = lax.axis_index("section")
    mate = swap(own, "section")
    block = ordered(section == 0, own, mate, 0)
    prior_mine = shift(own, 1)
    prior = ordered(section == 0, prior_mine, swap(prior_mine, "section"), 0)
    return jnp.concatenate([prior, block], axis=0)


def return_rows(grads):
    section = lax.axis_index("section")
    rows = grads.shape[0] // 4
    prior, block = grads[: 2 * rows], grads[2 * rows :]
    sent = jnp.concatenate([part(prior, 1 - section, 2), part(block, 1 - section, 2)], axis=0)
    mate = swap(sent.astype(BF16), "section").astype(F32)
    prior_sum = part(prior, section, 2) + mate[:rows]
    later = shift(prior_sum.astype(BF16), -1).astype(F32)
    return part(block, section, 2) + mate[rows:] + later


def layer_forward(rows, continues, p):
    section = lax.axis_index("section")
    count = rows.shape[0] // 4
    normed, factor, nrm = norm(rows.astype(F32), p["gain1"], p["shift1"])
    offset = 2 * count + section * count
    own = lambda a: lax.dynamic_slice_in_dim(a, offset, count, 0)
    nrm_own = own(nrm)
    q = (dot(nrm_own, p["wq"]) + p["bq"]).astype(BF16)
    k = dot(nrm, p["wk"]).astype(BF16)
    v = (dot(nrm, p["wv"]) + p["bv"]).astype(BF16)
    scores = jnp.einsum("qhd,khd->hqk", heads(q), heads(k), preferred_element_type=F32) * SCALE
    row = lax.broadcasted_iota(jnp.int32, (count, 4 * count), 0) + section * count
    col = lax.broadcasted_iota(jnp.int32, (count, 4 * count), 1)
    allowed = jnp.where(col < 2 * count, continues, col - 2 * count <= row)
    scores = jnp.where(allowed[None], scores, MASKED)
    lifted = jnp.exp(scores - jnp.max(scores, axis=-1, keepdims=True))
    chances = lifted / jnp.sum(lifted, axis=-1, keepdims=True)
    weights = chances.astype(BF16)
    o = jnp.einsum("hqk,khd->qhd", weights, heads(v), preferred_element_type=F32)
    o = o.reshape(count, -1).astype(BF16)
    h1 = own(rows).astype(F32) + (dot(o, p["wo"]) + p["bo"])
    normed2, factor2, nrm2 = norm(h1, p["gain2"], p["shift2"])
    f = dot(nrm2, p["wfc"]) + p["bfc"]
    u = jax.nn.gelu(f, approximate=True).astype(BF16)
    out = h1 + (dot(u, p["wp"]) + p["bp"])
    kept = (own(normed), own(factor), nrm, nrm_own, q, k, v, chances, weights, o)
    return out, kept + (normed2, factor2, nrm2, f, u)


def layer_backward(kept, p, dout):
    section = lax.axis_index("section")
    normed, factor, nrm, nrm_own, q, k, v, chances, weights, o, normed2, factor2, nrm2, f, u = kept
    count = dout.shape[0]
    gm = dout.astype(BF16)
    col = lambda a: jnp.sum(a.astype(F32), axis=0)
    g = {}
    g["wp"] = dot(u, gm, ((0,), (0,)))
    g["bp"] = col(gm)
    du = dot(gm, p["wp"], ((1,), (1,)))
    df = jax.vjp(lambda a: jax.nn.gelu(a, approximate=True), f)[1](du)[0].astype(BF16)
    g["wfc"] = dot(nrm2, df, ((0,), (0,)))
    g["bfc"] = col(df)
    dh, g["gain2"], g["shift2"] = norm_back(
        dot(df, p["wfc"], ((1,), (1,))), normed2, factor2, p["gain2"]
    )
    dh1 = dout + dh
    ga = dh1.astype(BF16)
    g["wo"] = dot(o, ga, ((0,), (0,)))
    g["bo"] = col(ga)
    do = dot(ga, p["wo"], ((1,), (1,))).astype(BF16)
    dpw = jnp.einsum("qhd,khd->hqk", heads(do), heads(v), preferred_element_type=F32)
    ds = (chances * (dpw - jnp.sum(chances * dpw, axis=-1, keepdims=True))).astype(BF16)
    flat = lambda a: a.reshape(a.shape[0], -1)
    dq = flat(jnp.einsum("hqk,khd->qhd", ds, heads(k), preferred_element_type=F32)) * SCALE
    dk = flat(jnp.einsum("hqk,qhd->khd", ds, heads(q), preferred_element_type=F32)) * SCALE
    dv = flat(jnp.einsum("hqk,qhd->khd", weights, heads(do), preferred_element_type=F32))
    dq, dk, dv = dq.astype(BF16), dk.astype(BF16), dv.astype(BF16)
    g["wq"] = dot(nrm_own, dq, ((0,), (0,)))
    g["wk"] = dot(nrm, dk, ((0,), (0,)))
    g["wv"] = dot(nrm, dv, ((0,), (0,)))
    g["bq"] = col(dq)
    g["bv"] = col(dv)
    dn_q = dot(dq, p["wq"], ((1,), (1,)))
    dn = dot(dk, p["wk"], ((1,), (1,))) + dot(dv, p["wv"], ((1,), (1,)))
    offset = 2 * count + section * count
    dn = lax.dynamic_update_slice_in_dim(
        dn, lax.dynamic_slice_in_dim(dn, offset, count, 0) + dn_q, offset, 0
    )
    dh, g["gain1"], g["shift1"] = norm_back(return_rows(dn), normed, factor, p["gain1"])
    return dh1 + dh, g


def local(
    inputs,
    out_grads,
    seq_blocks,
    ln1_gain,
    ln1_shift,
    qkv_weight,
    qv_bias,
    out_weight,
    out_bias,
    ln2_gain,
    ln2_shift,
    fc_weight,
    fc_bias,
    proj_weight,
    proj_bias,
):
    section = lax.axis_index("section")
    position = lax.axis_index("dp")
    tensor = lax.axis_index("tensor")
    half = D // 2
    block = inputs.shape[1]
    count = block // 2
    hidden = fc_weight.shape[1]
    first = tensor == 0

    def features(mine, other):
        return ordered(first, mine, other, mine.ndim - 1)

    micro = lambda a, which: lax.dynamic_index_in_dim(a, which, 0, keepdims=False)
    starts = jnp.cumsum(seq_blocks, axis=1) - seq_blocks
    continuing = jnp.logical_not(jnp.any(starts == position, axis=1))
    continues = micro(continuing, tensor)

    own_rows = lambda a, which: part(micro(a, which), section, 2)
    mine = features(own_rows(inputs, tensor), swap(own_rows(inputs, 1 - tensor), "tensor"))
    rows_one = gather_rows(mine)
    dout = features(own_rows(out_grads, tensor), swap(own_rows(out_grads, 1 - tensor), "tensor"))

    vectors = jnp.stack([ln1_gain, ln1_shift, out_bias, ln2_gain, ln2_shift, proj_bias])
    vectors = features(vectors, swap(vectors, "tensor")).astype(F32)
    names = ("gain1", "shift1", "bo", "gain2", "shift2", "bp")
    p = {name: vectors[i] for i, name in enumerate(names)}
    both = lambda a, other, axis: jnp.concatenate([a, other], axis=axis)
    qkv = both(qkv_weight, fetch_other(qkv_weight), 2)
    p["wq"], p["wk"], p["wv"] = qkv[:, 0], qkv[:, 1], qkv[:, 2]
    biases = both(qv_bias, swap(qv_bias, "tensor"), 1).astype(F32)
    p["bq"], p["bv"] = biases[0], biases[1]
    p["wo"] = both(out_weight, fetch_other(out_weight), 0)
    p["wfc"] = both(fc_weight, fetch_other(fc_weight), 1)
    p["bfc"] = both(fc_bias, swap(fc_bias, "tensor"), 0).astype(F32)
    p["wp"] = both(proj_weight, fetch_other(proj_weight), 0)

    out_one, kept_one = layer_forward(rows_one, continues, p)
    act_one = out_one.astype(BF16)
    out_two, kept_two = layer_forward(gather_rows(act_one), continues, p)
    act_two = out_two.astype(BF16)
    grad_two, g_two = layer_backward(kept_two, p, dout.astype(F32))
    grad_two = grad_two.astype(BF16)
    grad_one, g_one = layer_backward(kept_one, p, grad_two.astype(F32))
    grad_one = grad_one.astype(BF16)

    def spread(layers):
        both_layers = jnp.stack(layers)
        halves = lambda which: part(both_layers, which, 2, 2)
        mine = halves(tensor)
        theirs = swap(halves(1 - tensor), "tensor")
        per_micro = ordered(first, mine[:, None], theirs[:, None], 1)
        keep = lax.dynamic_index_in_dim(per_micro, section, 0, keepdims=False)
        mate = swap(lax.dynamic_index_in_dim(per_micro, 1 - section, 0, keepdims=False), "section")
        return ordered(section == 0, keep, mate, 1)[None]

    acts = spread([act_one, act_two])
    act_grads = spread([grad_one, grad_two]).astype(F32)

    g = {name: g_one[name] + g_two[name] for name in g_one}
    small = [g[n] for n in ("gain1", "shift1", "bo", "gain2", "shift2", "bp")]
    heads_order = lambda a: jnp.where(first, a, jnp.roll(a, a.shape[0] // 2))
    small += [heads_order(g["bq"]), heads_order(g["bv"]), heads_order(g["bfc"])]
    total = lax.psum(jnp.concatenate(small), ("section", "dp", "tensor"))
    cut = lambda start, size: lax.dynamic_slice_in_dim(
        total[start : start + 2 * size], tensor * size, size, 0
    )
    vec = {n: cut(D * i, half) for i, n in enumerate(names + ("bq", "bv"))}
    vec["bfc"] = cut(8 * D, hidden)

    def mlp_half(i):
        fc = g["wfc"][:, i * hidden : (i + 1) * hidden]
        proj = g["wp"][i * hidden : (i + 1) * hidden]
        return jnp.concatenate([proj, fc[:, :D], fc[:, D:]], axis=0).astype(BF16)

    def attn_half(i):
        cols = slice(i * half, (i + 1) * half)
        wo = g["wo"][cols]
        parts = [g["wq"][:, cols], g["wk"][:, cols], g["wv"][:, cols], wo[:, :half], wo[:, half:]]
        return jnp.concatenate(parts, axis=0).astype(BF16)

    mlp = reduce_grads(mlp_half(0), mlp_half(1)).astype(F32)
    attn = reduce_grads(attn_half(0), attn_half(1)).astype(F32)
    proj_grad = mlp[:hidden]
    fc_grad = jnp.concatenate([mlp[hidden : hidden + D], mlp[hidden + D :]], axis=1)
    qkv_grad = attn[: 3 * D].reshape(3, D, half).transpose(1, 0, 2)
    out_grad = jnp.concatenate([attn[3 * D : 3 * D + half], attn[3 * D + half :]], axis=1)
    return (
        acts,
        act_grads,
        vec["gain1"],
        vec["shift1"],
        qkv_grad,
        jnp.stack([vec["bq"], vec["bv"]]),
        out_grad,
        vec["bo"],
        vec["gain2"],
        vec["shift2"],
        fc_grad,
        vec["bfc"],
        proj_grad,
        vec["bp"],
    )


def solution(mesh):
    in_specs = (
        P(None, "dp", "tensor"),
        P(None, "dp", "tensor"),
        P(),
        P("tensor"),
        P("tensor"),
        P(None, None, "tensor"),
        P(None, "tensor"),
        P("tensor", None),
        P("tensor"),
        P("tensor"),
        P("tensor"),
        P(None, "tensor"),
        P("tensor"),
        P("tensor", None),
        P("tensor"),
    )
    out_specs = (
        P("section", None, "dp", "tensor"),
        P("section", None, "dp", "tensor"),
        P("tensor"),
        P("tensor"),
        P(None, None, "tensor"),
        P(None, "tensor"),
        P("tensor", None),
        P("tensor"),
        P("tensor"),
        P("tensor"),
        P(None, "tensor"),
        P("tensor"),
        P("tensor", None),
        P("tensor"),
    )
    return jax.shard_map(local, mesh=mesh, in_specs=in_specs, out_specs=out_specs, check_vma=False)
```

```python
import functools

import jax
import jax.numpy as jnp
from jax import lax
from jax.experimental import pallas as pl
from jax.experimental.pallas import tpu as pltpu
from jax.sharding import PartitionSpec as P

D = 768
HEAD = 64
NORM_EPSILON = 1e-05
MASKED = -1e30
SCALE = HEAD ** (-0.5)
F32 = jnp.float32
BF16 = jnp.bfloat16
LIMIT = 60 * 1024 * 1024
SMALL = 12 * 1024 * 1024


def dot(a, b, dims=((1,), (0,))):
    return lax.dot_general(a, b, (dims, ((), ())), preferred_element_type=F32)


def swap(array, axis):
    return lax.ppermute(array, axis, [(0, 1), (1, 0)])


def shift(array, by):
    count = lax.axis_size("dp")
    pairs = [(i, i + by) for i in range(count) if 0 <= i + by < count]
    return lax.ppermute(array, "dp", pairs)


def exchange(array, bit):
    count = lax.axis_size("dp")
    return lax.ppermute(array, "dp", [(i, i ^ bit) for i in range(count)])


def part(array, which, parts, axis=0):
    size = array.shape[axis] // parts
    return lax.dynamic_slice_in_dim(array, which * size, size, axis)


def ordered(first, mine, other, axis):
    return jnp.concatenate(
        [jnp.where(first, mine, other), jnp.where(first, other, mine)], axis=axis
    )


def add_low(a, b):
    return (a.astype(F32) + b.astype(F32)).astype(BF16)


def lasts(microseconds):
    return pl.CostEstimate(flops=int(microseconds * 1e3), bytes_accessed=1, transcendentals=0)


def params(limit):
    return pltpu.CompilerParams(vmem_limit_bytes=limit)


def after(dep):
    return ([], []) if dep is None else ([dep], [pl.BlockSpec(memory_space=pl.ANY)])


def sum_split(sets, side, dep=None):
    halves = [arrays[0].shape[0] // 2 for arrays in sets]
    if any(rows % 16 for rows in halves):
        totals = [sum(a.astype(F32) for a in arrays).astype(BF16) for arrays in sets]
        pick = lambda which: jnp.concatenate([part(t, which, 2) for t in totals], axis=0)
        return pick(side), pick(1 - side)
    width = sets[0][0].shape[1]
    extra, extra_specs = after(dep)
    operands, specs = [], []
    for arrays, rows in zip(sets, halves):
        for array in arrays:
            operands += [array, array]
            specs.append(pl.BlockSpec((rows, width), lambda j, which: (which[0], 0)))
            specs.append(pl.BlockSpec((rows, width), lambda j, which: (1 - which[0], 0)))

    def kernel(which, *refs):
        at, row = 0, 0
        for arrays, rows in zip(sets, halves):
            for out, first in ((refs[-2], at), (refs[-1], at + 1)):
                total = refs[first][...].astype(F32)
                for i in range(1, len(arrays)):
                    total += refs[first + 2 * i][...].astype(F32)
                out[row : row + rows, :] = total.astype(BF16)
            at, row = at + 2 * len(arrays), row + rows

    block = (sum(halves), width)
    flat = pl.BlockSpec(block, lambda j, which: (0, 0))
    return pl.pallas_call(
        kernel,
        grid_spec=pltpu.PrefetchScalarGridSpec(
            num_scalar_prefetch=1,
            grid=(1,),
            in_specs=specs + extra_specs,
            out_specs=[flat] * 2,
        ),
        out_shape=[jax.ShapeDtypeStruct(block, BF16)] * 2,
        compiler_params=params(SMALL),
        cost_estimate=lasts(1.2),
        name="sum_split",
    )(side.reshape(1), *operands, *extra)


def sum_rows(arrays, dep=None):
    rows, width = arrays[0].shape
    kind = arrays[0].dtype
    if rows % 16:
        return add_low(*arrays)
    extra, extra_specs = after(dep)

    def kernel(a, b, *rest):
        rest[-1][...] = (a[...].astype(F32) + b[...].astype(F32)).astype(kind)

    return pl.pallas_call(
        kernel,
        in_specs=[pl.BlockSpec(memory_space=pltpu.VMEM)] * 2 + extra_specs,
        out_shape=jax.ShapeDtypeStruct((rows, width), kind),
        compiler_params=params(SMALL),
        cost_estimate=lasts(0.7),
        name="sum_rows",
    )(*arrays, *extra)


def put_rows(side, mine, other, dep=None):
    rows, width = mine.shape
    if rows % 16:
        return ordered(side == 0, mine, other, 0)
    extra, extra_specs = after(dep)

    def kernel(which, a, b, *rest):
        out = rest[-1]
        out[pl.ds(pl.multiple_of(which[0] * rows, rows), rows), :] = a[...]
        out[pl.ds(pl.multiple_of((1 - which[0]) * rows, rows), rows), :] = b[...]

    return pl.pallas_call(
        kernel,
        in_specs=[pl.BlockSpec(memory_space=pltpu.SMEM)]
        + [pl.BlockSpec(memory_space=pltpu.VMEM)] * 2
        + extra_specs,
        out_shape=jax.ShapeDtypeStruct((2 * rows, width), BF16),
        compiler_params=params(SMALL),
        cost_estimate=lasts(0.7),
        name="put_rows",
    )(side.reshape(1), mine, other, *extra)


def gradient(where, terms, which, added=(), dep=None):
    arrays, specs, plan = [], [], []
    for term in terms:
        plan.append(len(term))
        for a, a_block, a_index, b, b_block, b_index in term:
            for array, block, index in ((a, a_block, a_index), (b, b_block, b_index)):
                arrays.append(array)
                specs.append(
                    pl.BlockSpec(block, lambda j, w, index=index: index(w[0], w[0] ^ which))
                )
    rows, width = terms[0][0][1][1], terms[0][0][4][1]
    total = rows * len(terms)
    last = len(arrays)
    for cuts in added:
        for array in cuts:
            arrays.append(array)
            specs.append(pl.BlockSpec(array.shape, lambda j, w: (0, 0)))
    extra, extra_specs = after(dep)

    def kernel(w, *refs):
        out, at = refs[-1], 0
        for i, layers in enumerate(plan):
            value = None
            for _ in range(layers):
                one = dot(refs[at][...], refs[at + 1][...], ((0,), (0,)))
                value = one if value is None else value + one
                at += 2
            span = slice(i * rows, (i + 1) * rows)
            place = last
            for cuts in added:
                each = total // len(cuts)
                taken = []
                for cut in range(len(cuts)):
                    low, high = max(span.start, cut * each), min(span.stop, (cut + 1) * each)
                    if low < high:
                        taken.append(refs[place + cut][low - cut * each : high - cut * each, :])
                value += jnp.concatenate([t.astype(F32) for t in taken], axis=0)
                place += len(cuts)
            out[span, :] = value.astype(BF16)

    return pl.pallas_call(
        kernel,
        grid_spec=pltpu.PrefetchScalarGridSpec(
            num_scalar_prefetch=1,
            grid=(1,),
            in_specs=specs + extra_specs,
            out_specs=pl.BlockSpec((total, width), lambda j, w: (0, 0)),
        ),
        out_shape=jax.ShapeDtypeStruct((total, width), BF16),
        compiler_params=params(SMALL),
        cost_estimate=lasts(1 + sum(plan) * 0.35),
        name="gradient",
    )(where, *arrays, *extra)


class Reduction:
    def __init__(self, where, terms_of, early=False):
        self.where, self.terms_of = where, terms_of
        self.bit = 1
        self.early = early
        self.partial = {}

    def first_layer(self, dep):
        for half in (1, 0):
            for which in (1, 0):
                terms = [term[:1] for term in self.terms_of(half)]
                dep = self.partial[half, which] = gradient(self.where, terms, which, dep=dep)
        return dep

    def piece(self, half, which, mate, dep):
        terms, added = self.terms_of(half), [] if mate is None else [mate]
        added = [a if isinstance(a, list) else [a] for a in added]
        if self.early:
            terms = [term[1:] for term in terms]
            added.append([self.partial[half, which]])
        return gradient(self.where, terms, which, added, dep)

    def theirs_foreign(self, dep):
        theirs = self.piece(1, 1, None, dep)
        self.mate_foreign = self.to_mate(theirs)
        return theirs

    def theirs_own(self, dep):
        theirs = self.piece(0, 1, None, dep)
        self.mate_own = self.to_mate(theirs)
        return theirs

    def to_mate(self, theirs):
        rows = theirs.shape[0] // 2
        return [swap(theirs[i * rows : (i + 1) * rows], "section") for i in range(2)]

    def foreign(self, dep):
        foreign = self.piece(1, 0, self.mate_foreign, dep)
        self.across = swap(foreign, "tensor")
        return foreign

    def own(self, dep):
        own = self.piece(0, 0, self.mate_own, dep)
        self.arrays = [own, self.across]
        return own

    def side(self):
        return (lax.axis_index("dp") // self.bit) % 2

    def split(self, dep, other=None):
        sets = [self.arrays] if other is None else [self.arrays, other.arrays]
        kept, sent = sum_split(sets, self.side(), dep)
        self.arrays = [kept, exchange(sent, self.bit)]
        self.bit *= 2
        return kept

    def sum(self, dep):
        self.kept = sum_rows(self.arrays, dep)
        self.send_back()
        return self.kept

    def send_back(self):
        self.bit //= 2
        self.other = swap(self.kept, "section") if self.bit == 0 else exchange(self.kept, self.bit)

    def join(self, dep):
        self.kept = put_rows(self.side(), self.kept, self.other, dep)
        self.send_back()
        return self.kept


class SmallSum:
    def __init__(self, array):
        bits = []
        while 2 ** len(bits) < lax.axis_size("dp"):
            bits.append(2 ** len(bits))
        self.moves = [lambda a: swap(a, "section"), lambda a: swap(a, "tensor")]
        self.moves += [lambda a, bit=bit: exchange(a, bit) for bit in bits]
        self.array = array
        self.other = self.moves.pop(0)(array)

    def step(self, dep):
        if self.other is None:
            return dep
        self.array = sum_rows([self.array, self.other], dep)
        self.other = self.moves.pop(0)(self.array) if self.moves else None
        return self.array


def widen(section, kept, other, shape, place, dep):
    extra, extra_specs = after(dep)

    def kernel(which, a, b, *rest):
        for value in range(2):

            @pl.when(which[0] == value)
            def _():
                place(rest[-1], a, value)
                place(rest[-1], b, 1 - value)

    return pl.pallas_call(
        kernel,
        in_specs=[pl.BlockSpec(memory_space=pltpu.SMEM)]
        + [pl.BlockSpec(memory_space=pltpu.VMEM)] * 2
        + extra_specs,
        out_shape=jax.ShapeDtypeStruct(shape, F32),
        compiler_params=params(2 * SMALL),
        cost_estimate=lasts(2),
        name="widen",
    )(section.reshape(1), kept, other, *extra)


def take_rows(array, which, parts, dep):
    rows, width = array.shape[0] // parts, array.shape[1]
    extra, extra_specs = after(dep)

    def kernel(w, a, *rest):
        rest[-1][...] = a[...]

    return pl.pallas_call(
        kernel,
        grid_spec=pltpu.PrefetchScalarGridSpec(
            num_scalar_prefetch=1,
            grid=(1,),
            in_specs=[pl.BlockSpec((rows, width), lambda j, w: (w[0], 0))] + extra_specs,
            out_specs=pl.BlockSpec((rows, width), lambda j, w: (0, 0)),
        ),
        out_shape=jax.ShapeDtypeStruct((rows, width), array.dtype),
        compiler_params=params(SMALL),
        cost_estimate=lasts(0.7),
        name="take_rows",
    )(which.reshape(1), array, *extra)


class Fetch:
    def __init__(self, array, bit):
        self.array, self.bit = array, bit
        self.section = lax.axis_index("section")
        self.side = (lax.axis_index("dp") // bit) % 2

    def start(self, dep):
        piece = take_rows(self.array, self.section * 2 + self.side, 4, dep)
        self.mine = swap(piece, "tensor")
        self.other = exchange(self.mine, self.bit)
        return piece

    def join(self, dep):
        self.mine = put_rows(self.side, self.mine, self.other, dep)
        self.other = swap(self.mine, "section")
        return self.mine

    def finish(self, dep):
        self.whole = put_rows(self.section, self.mine, self.other, dep)
        return self.whole


def standard(rows):
    center = jnp.sum(rows, axis=1, keepdims=True) / D
    spread = jnp.sum(rows * rows, axis=1, keepdims=True) / D - center * center
    factor = lax.rsqrt(spread + NORM_EPSILON)
    return (rows - center) * factor, factor


def norm(rows, gain, shift_by):
    return (standard(rows)[0] * gain + shift_by).astype(BF16)


def norm_back(grad, normed, factor, gain):
    scaled = grad * gain
    mean = jnp.sum(scaled, axis=1, keepdims=True) / D
    along = jnp.sum(scaled * normed, axis=1, keepdims=True) / D
    return factor * (scaled - mean - normed * along)


def total_rows(array):
    return jnp.sum(array.astype(F32), axis=0, keepdims=True)


def only_head(array, which):
    lane = lax.broadcasted_iota(jnp.int32, array.shape, 1)
    return jnp.where((lane >= HEAD) == (which == 1), array, jnp.zeros_like(array))


GELU_A = 0.7978845608028654
GELU_B = 0.044715
PAIR = 2 * HEAD
CHUNK = 768


class Call:
    def __init__(self):
        self.names, self.arrays, self.in_specs = [], [], []
        self.out_names, self.out_specs, self.out_shape = [], [], []

    def take(self, name, array, block=None, index=None):
        self.names.append(name)
        self.arrays.append(array)
        if block is None:
            block, index = array.shape, lambda j: (0,) * array.ndim
        self.in_specs.append(pl.BlockSpec(block, index))

    def scalars(self, name, array):
        self.names.append(name)
        self.arrays.append(array)
        self.in_specs.append(pl.BlockSpec(memory_space=pltpu.SMEM))

    def give(self, name, shape, dtype, block=None, index=None):
        self.out_names.append(name)
        self.out_shape.append(jax.ShapeDtypeStruct(shape, dtype))
        if block is None:
            block, index = shape, lambda j: (0,) * len(shape)
        self.out_specs.append(pl.BlockSpec(block, index))

    def run(self, body, grid, scratch, name, time, dep=None):
        extra, extra_specs = after(dep)
        names = self.names + ["dep"] * len(extra) + self.out_names + [n for n, _ in scratch]

        def kernel(*refs):
            body(dict(zip(names, refs)))

        outs = pl.pallas_call(
            kernel,
            grid=(grid,),
            in_specs=self.in_specs + extra_specs,
            out_specs=self.out_specs,
            out_shape=self.out_shape,
            scratch_shapes=[shape for _, shape in scratch],
            compiler_params=params(LIMIT),
            cost_estimate=lasts(time),
            name=name,
        )(*self.arrays, *extra)
        return dict(zip(self.out_names, outs))


def within(first, size):
    return lambda j: jnp.clip(j - first, 0, size - 1)


class Half:
    def __init__(self, refs, half):
        self.refs, self.half = refs, half

    def __getitem__(self, name):
        return self.refs[f"{name}{self.half}"]


def each_half(refs, halves, step, first, per):
    def run(body):
        for place, half in enumerate(halves):
            start = first + place * per

            @pl.when((step >= start) & (step < start + per))
            def _(half=half):
                body(Half(refs, half))

    return run


def forward_part(
    where, vec, weights, attn, mlp, rows=None, nrm=None, nrm2=None, carried=None, dep=None
):
    c = Call()
    c.scalars("where", where)
    c.take("vec", vec)
    if rows is not None:
        c.take("rows", rows)
    if nrm is not None:
        c.take("nrm", nrm)
    if nrm2 is not None:
        c.take("nrm2", nrm2)
    if carried is not None:
        c.take("carried", carried)
    full = (rows if rows is not None else nrm if nrm is not None else None)
    count = carried.shape[0] if full is None else full.shape[0] // 4
    width = weights[0]["wo"].shape[0]
    hidden = weights[0]["wp"].shape[0]
    per, per_chunk = width // PAIR, hidden // CHUNK
    pairs, chunks = per * len(attn), per_chunk * len(mlp)
    for place, half in enumerate(attn):
        w = weights[half]
        at = within(place * per, per)
        for index, name in enumerate(("wq", "wk", "wv")):
            c.take(f"{name}{half}", w["wqkv"], (D, PAIR), lambda j, i=index, at=at: (i, at(j)))
        c.take(f"bqv{half}", w["bqv"], (2, PAIR), lambda j, at=at: (0, at(j)))
        c.take(f"wo{half}", w["wo"], (PAIR, D), lambda j, at=at: (at(j), 0))
    for place, half in enumerate(mlp):
        w = weights[half]
        at = within(pairs + place * per_chunk, per_chunk)
        c.take(f"wfc{half}", w["wfc"], (D, CHUNK), lambda j, at=at: (0, at(j)))
        c.take(f"bfc{half}", w["bfc"], (1, CHUNK), lambda j, at=at: (0, at(j)))
        c.take(f"wp{half}", w["wp"], (CHUNK, D), lambda j, at=at: (at(j), 0))
    if rows is not None:
        c.give("nrm", (4 * count, D), BF16)
    for place, half in enumerate(attn):
        at = within(place * per, per)
        for name, n in (("q", count), ("k", 4 * count), ("v", 4 * count), ("o", count)):
            c.give(f"{name}{half}", (n, width), BF16, (n, PAIR), lambda j, at=at: (0, at(j)))
        block = (2, count, 4 * count)
        c.give(f"p{half}", (2 * per, count, 4 * count), BF16, block, lambda j, at=at: (at(j), 0, 0))
    middle = bool(attn) and bool(mlp)
    if middle:
        c.give("h1", (count, D), F32)
        c.give("nrm2", (count, D), BF16)
    for place, half in enumerate(mlp):
        at = within(pairs + place * per_chunk, per_chunk)
        for name, kind in (("f", F32), ("u", BF16)):
            c.give(f"{name}{half}", (count, hidden), kind, (count, CHUNK), lambda j, at=at: (0, at(j)))
    final = 1 in mlp
    if final:
        c.give("act", (count, D), BF16)
    else:
        c.give("sum", (count, D), F32)
    scratch = []
    if final:
        scratch.append(("sum", pltpu.VMEM((count, D), F32)))
    if attn:
        scratch.append(("mask", pltpu.VMEM((count, 4 * count), F32)))

    def body(r):
        step = pl.program_id(0)
        total = r["sum"]
        flags = r["where"]
        vec = r["vec"]
        span = pl.ds(pl.multiple_of(2 * count + flags[0] * count, count), count)

        @pl.when(step == 0)
        def _():
            if rows is not None:
                r["nrm"][...] = norm(r["rows"][...].astype(F32), vec[0:1, :], vec[1:2, :])
                total[...] = r["rows"][span, :].astype(F32) + vec[2:3, :]
            else:
                total[...] = r["carried"][...]
            if attn:
                mask = r["mask"]
                row = lax.broadcasted_iota(jnp.int32, mask.shape, 0) + flags[0] * count
                col = lax.broadcasted_iota(jnp.int32, mask.shape, 1)
                limit = jnp.where(col < 2 * count, flags[1] * (4 * count) - 1, row + 2 * count)
                mask[...] = jnp.where(col <= limit, 0.0, MASKED)

        if attn:

            @each_half(r, attn, step, 0, per)
            def _(h):
                nrm_ref = r["nrm"]
                q = (dot(nrm_ref[span, :], h["wq"][...]) + h["bqv"][0:1, :]).astype(BF16)
                h["q"][...] = q
                kv = dot(nrm_ref[...], jnp.concatenate([h["wk"][...], h["wv"][...]], axis=1))
                k = kv[:, :PAIR].astype(BF16)
                h["k"][...] = k
                v = (kv[:, PAIR:] + h["bqv"][1:2, :]).astype(BF16)
                h["v"][...] = v
                scaled = q * jnp.asarray(SCALE, BF16)
                sides = []
                for which in range(2):
                    scores = dot(only_head(scaled, which), k, ((1,), (1,))) + r["mask"][...]
                    lifted = jnp.exp(scores - jnp.max(scores, axis=1, keepdims=True))
                    low = (lifted * (1.0 / jnp.sum(lifted, axis=1, keepdims=True))).astype(BF16)
                    h["p"][which] = low
                    sides.append(dot(low, v))
                lane = lax.broadcasted_iota(jnp.int32, sides[0].shape, 1)
                o = jnp.where(lane < HEAD, sides[0], sides[1]).astype(BF16)
                h["o"][...] = o
                total[...] += dot(o, h["wo"][...])

        if middle:

            @pl.when(step == pairs - 1)
            def _():
                r["h1"][...] = total[...]
                r["nrm2"][...] = norm(total[...], vec[3:4, :], vec[4:5, :])
                total[...] += vec[5:6, :]

        if mlp:

            @each_half(r, mlp, step, pairs, per_chunk)
            def _(h):
                pre = dot(r["nrm2"][...], h["wfc"][...]) + h["bfc"][...]
                h["f"][...] = pre
                inner = jnp.tanh(GELU_A * (pre + GELU_B * pre * pre * pre))
                hidden_low = (0.5 * pre * (1.0 + inner)).astype(BF16)
                h["u"][...] = hidden_low
                total[...] += dot(hidden_low, h["wp"][...])

        if final:

            @pl.when(step == pairs + chunks - 1)
            def _():
                r["act"][...] = total[...].astype(BF16)

    return c.run(body, pairs + chunks, scratch, "forward", 4.2 * pairs + 2 * chunks, dep)


def backward_mlp(vec, weights, kept, dout, dep=None):
    c = Call()
    count = dout.shape[0]
    hidden = weights[0]["wp"].shape[0]
    per = hidden // CHUNK
    steps = 2 * per
    c.take("vec", vec)
    c.take("dout", dout)
    c.take("h1", kept["h1"])
    for half in range(2):
        at = within(half * per, per)
        w = weights[half]
        c.take(f"f{half}", kept[f"f{half}"], (count, CHUNK), lambda j, at=at: (0, at(j)))
        c.take(f"wp{half}", w["wp"], (CHUNK, D), lambda j, at=at: (at(j), 0))
        c.take(f"wfc{half}", w["wfc"], (D, CHUNK), lambda j, at=at: (0, at(j)))
    for half in range(2):
        at = within(half * per, per)
        c.give(f"df{half}", (count, hidden), BF16, (count, CHUNK), lambda j, at=at: (0, at(j)))
        c.give(f"bfc{half}", (1, hidden), F32, (1, CHUNK), lambda j, at=at: (0, at(j)))
    c.give("ga", (count, D), BF16)
    c.give("dh1", (count, D), F32)
    c.give("small", (8, D), F32)

    def body(r):
        step = pl.program_id(0)
        vec, dout, dn2 = r["vec"], r["dout"], r["dn2"]

        @pl.when(step == 0)
        def _():
            dn2[...] = jnp.zeros_like(dn2)

        @each_half(r, (0, 1), step, 0, per)
        def _(h):
            du = dot(dout[...], h["wp"][...], ((1,), (1,)))
            pre = h["f"][...]
            square = pre * pre
            inner = jnp.tanh(GELU_A * (pre + GELU_B * square * pre))
            slope = 0.5 * (1.0 + inner) + (0.5 * GELU_A) * pre * (1.0 - inner * inner) * (
                1.0 + 3.0 * GELU_B * square
            )
            low = (du * slope).astype(BF16)
            h["df"][...] = low
            h["bfc"][...] = total_rows(low)
            dn2[...] += dot(low, h["wfc"][...], ((1,), (1,)))

        @pl.when(step == steps - 1)
        def _():
            normed, factor = standard(r["h1"][...])
            back = dn2[...]
            grad = dout[...].astype(F32) + norm_back(back, normed, factor, vec[3:4, :])
            r["dh1"][...] = grad
            low = grad.astype(BF16)
            r["ga"][...] = low
            sums = [total_rows(x) for x in (back * normed, back, low, dout[...])]
            r["small"][...] = jnp.concatenate(sums + [jnp.zeros((4, D), F32)], axis=0)

    return c.run(body, steps, [("dn2", pltpu.VMEM((count, D), F32))], "backward_mlp", 10, dep)


def backward_attn(where, weights, kept, ga, dep=None):
    c = Call()
    count = ga.shape[0]
    width = weights[0]["wo"].shape[0]
    per = width // PAIR
    steps = 2 * per
    c.scalars("where", where)
    c.take("ga", ga)
    for half in range(2):
        at = within(half * per, per)
        w = weights[half]
        for index, name in enumerate(("wq", "wk", "wv")):
            c.take(f"{name}{half}", w["wqkv"], (D, PAIR), lambda j, i=index, at=at: (i, at(j)))
        c.take(f"wo{half}", w["wo"], (PAIR, D), lambda j, at=at: (at(j), 0))
        for name, n in (("q", count), ("k", 4 * count), ("v", 4 * count)):
            c.take(f"{name}{half}", kept[f"{name}{half}"], (n, PAIR), lambda j, at=at: (0, at(j)))
        block = (2, count, 4 * count)
        c.take(f"p{half}", kept[f"p{half}"], block, lambda j, at=at: (at(j), 0, 0))
    for half in range(2):
        at = within(half * per, per)
        for name, n in (("dq", count), ("dk", 4 * count), ("dv", 4 * count)):
            c.give(f"{name}{half}", (n, width), BF16, (n, PAIR), lambda j, at=at: (0, at(j)))
        c.give(f"bqv{half}", (8, width), F32, (8, PAIR), lambda j, at=at: (0, at(j)))
    c.give("sent", (2 * count, D), BF16)
    c.give("prior", (count, D), BF16)
    c.give("own", (count, D), F32)

    def body(r):
        step = pl.program_id(0)
        flags, dn = r["where"], r["dn"]
        span = pl.ds(pl.multiple_of(2 * count + flags[0] * count, count), count)

        @pl.when(step == 0)
        def _():
            dn[...] = jnp.zeros_like(dn)

        @each_half(r, (0, 1), step, 0, per)
        def _(h):
            do = dot(r["ga"][...], h["wo"][...], ((1,), (1,))).astype(BF16)
            v = h["v"][...]
            scaled_q = h["q"][...] * jnp.asarray(SCALE, BF16)
            scaled_k = h["k"][...] * jnp.asarray(SCALE, BF16)
            grads = []
            for which in range(2):
                do_head = only_head(do, which)
                low = h["p"][which]
                dpw = dot(do_head, v, ((1,), (1,)))
                chances = low.astype(F32)
                center = jnp.sum(chances * dpw, axis=1, keepdims=True)
                ds = (chances * (dpw - center)).astype(BF16)
                grads.append(
                    (
                        dot(ds, scaled_k),
                        dot(ds, only_head(scaled_q, which), ((0,), (0,))),
                        dot(low, do_head, ((0,), (0,))),
                    )
                )
            (dq0, dk0, dv0), (dq1, dk1, dv1) = grads
            lane = lax.broadcasted_iota(jnp.int32, dq0.shape, 1)
            dq = jnp.where(lane < HEAD, dq0, dq1).astype(BF16)
            dk = (dk0 + dk1).astype(BF16)
            dv = (dv0 + dv1).astype(BF16)
            h["dq"][...] = dq
            h["dk"][...] = dk
            h["dv"][...] = dv
            sums = [total_rows(dq), total_rows(dv), jnp.zeros((6, PAIR), F32)]
            h["bqv"][...] = jnp.concatenate(sums, axis=0)
            dn[...] += dot(
                jnp.concatenate([dk, dv], axis=1),
                jnp.concatenate([h["wk"][...], h["wv"][...]], axis=1),
                ((1,), (1,)),
            )
            dn[span, :] += dot(dq, h["wq"][...], ((1,), (1,)))

        @pl.when(step == steps - 1)
        def _():
            at = lambda base, which: pl.ds(pl.multiple_of(base + which * count, count), count)
            mine, other = flags[0], 1 - flags[0]
            r["sent"][:count, :] = dn[at(0, other), :].astype(BF16)
            r["sent"][count:, :] = dn[at(2 * count, other), :].astype(BF16)
            r["prior"][...] = dn[at(0, mine), :].astype(BF16)
            r["own"][...] = dn[at(2 * count, mine), :]

    return c.run(body, steps, [("dn", pltpu.VMEM((4 * count, D), F32))], "backward_attn", 26, dep)


def norm_kernel(rows, vec, own, mate, later, dh1, low, small):
    back = own[...] + mate[...].astype(F32) + later[...].astype(F32)
    normed, factor = standard(rows[...].astype(F32))
    low[...] = (dh1[...] + norm_back(back, normed, factor, vec[0:1, :])).astype(BF16)
    small[...] = jnp.concatenate(
        [total_rows(back * normed), total_rows(back), jnp.zeros((6, D), F32)], axis=0
    )


class NormBack:
    def __init__(self, rows, vec, back, dh1):
        self.rows, self.vec, self.back, self.dh1 = rows, vec, back, dh1
        self.mate = swap(back["sent"], "section")

    def send(self, dep):
        count = self.rows.shape[0]
        prior = sum_rows([self.back["prior"], self.mate[:count]], dep)
        self.later = shift(prior, -1)
        return prior

    def finish(self, dep):
        shape = jax.ShapeDtypeStruct
        extra, extra_specs = after(dep)
        count = self.rows.shape[0]
        operands = [
            self.rows, self.vec, self.back["own"], self.mate[count:], self.later, self.dh1,
        ]

        def kernel(*refs):
            norm_kernel(*refs[: len(operands)], *refs[-2:])

        return pl.pallas_call(
            kernel,
            in_specs=[pl.BlockSpec(memory_space=pltpu.VMEM)] * len(operands) + extra_specs,
            out_shape=[shape(self.dh1.shape, BF16), shape((8, D), F32)],
            name="first_norm_back",
            compiler_params=params(SMALL),
            cost_estimate=lasts(1),
        )(*operands, *extra)


def gather_small(where, norms, mlps, attns, dep):
    halves = [m[f"bfc{i}"] for m in mlps for i in range(2)]
    halves += [a[f"bqv{i}"] for a in attns for i in range(2)]
    operands = list(norms) + [m["small"] for m in mlps] + halves
    extra, extra_specs = after(dep)

    def kernel(flags, norm_a, norm_b, mlp_a, mlp_b, f0, f1, g0, g1, a0, a1, b0, b1, *rest):
        out = rest[-1]
        out[...] = jnp.zeros_like(out)
        out[0:2, :] = norm_a[0:2, :] + norm_b[0:2, :]
        out[2:6, :] = mlp_a[0:4, :] + mlp_b[0:4, :]
        bqv = (a0[0:2, :] + b0[0:2, :], a1[0:2, :] + b1[0:2, :])
        bfc = (f0[...] + g0[...], f1[...] + g1[...])
        for value in range(2):

            @pl.when(flags[2] == value)
            def _():
                out[6:8, :] = jnp.concatenate([bqv[value], bqv[1 - value]], axis=1)
                for place in range(2):
                    row = 8 + 2 * (place if value == 0 else 1 - place)
                    out[row : row + 1, :] = bfc[place][:, :D]
                    out[row + 1 : row + 2, :] = bfc[place][:, D:]

    return pl.pallas_call(
        kernel,
        in_specs=[pl.BlockSpec(memory_space=pltpu.SMEM)]
        + [pl.BlockSpec(memory_space=pltpu.VMEM)] * len(operands)
        + extra_specs,
        out_shape=jax.ShapeDtypeStruct((16, D), F32),
        compiler_params=params(SMALL),
        cost_estimate=lasts(1),
        name="gather_small",
    )(where, *operands, *extra)


class Spread:
    def __init__(self, section, tensor):
        self.section, self.tensor = section, tensor

    def add(self, layers, dep):
        rows, width = layers[0].shape[0], layers[0].shape[1] // 2
        extra, extra_specs = after(dep)

        def kernel(which, a, b, *rest):
            for value in range(2):

                @pl.when(which[0] == value)
                def _():
                    for layer, ref in enumerate((a, b)):
                        rest[-2][layer] = ref[:, value * width : (value + 1) * width]
                        rest[-1][layer] = ref[:, (1 - value) * width : (2 - value) * width]

        shape = jax.ShapeDtypeStruct((2, rows, width), layers[0].dtype)
        self.mine, theirs = pl.pallas_call(
            kernel,
            in_specs=[pl.BlockSpec(memory_space=pltpu.SMEM)]
            + [pl.BlockSpec(memory_space=pltpu.VMEM)] * 2
            + extra_specs,
            out_shape=[shape, shape],
            compiler_params=params(SMALL),
            cost_estimate=lasts(0.7),
            name="spread",
        )(self.tensor.reshape(1), *layers, *extra)
        self.theirs = swap(theirs, "tensor")
        return self.mine

    def turn(self, dep):
        extra, extra_specs = after(dep)

        def kernel(which, a, b, *rest):
            for section in range(2):
                for tensor in range(2):

                    @pl.when((which[0] == section) & (which[1] == tensor))
                    def _():
                        for out, layer in ((rest[-2], section), (rest[-1], 1 - section)):
                            out[tensor] = a[layer]
                            out[1 - tensor] = b[layer]

        shape = jax.ShapeDtypeStruct(self.mine.shape, self.mine.dtype)
        self.kept, sent = pl.pallas_call(
            kernel,
            in_specs=[pl.BlockSpec(memory_space=pltpu.SMEM)]
            + [pl.BlockSpec(memory_space=pltpu.VMEM)] * 2
            + extra_specs,
            out_shape=[shape, shape],
            compiler_params=params(SMALL),
            cost_estimate=lasts(0.7),
            name="turn",
        )(jnp.stack([self.section, self.tensor]), self.mine, self.theirs, *extra)
        self.mate = swap(sent, "section")
        return self.kept

    def finish(self, kind, dep):
        _, rows, width = self.kept.shape
        extra, extra_specs = after(dep)

        def kernel(which, mine, mate, *rest):
            out = rest[-1]
            for value in range(2):

                @pl.when(which[0] == value)
                def _():
                    for micro in range(2):
                        here = slice(value * rows, (value + 1) * rows)
                        there = slice((1 - value) * rows, (2 - value) * rows)
                        out[micro, here, :] = mine[micro].astype(kind)
                        out[micro, there, :] = mate[micro].astype(kind)

        return pl.pallas_call(
            kernel,
            in_specs=[pl.BlockSpec(memory_space=pltpu.SMEM)]
            + [pl.BlockSpec(memory_space=pltpu.VMEM)] * 2
            + extra_specs,
            out_shape=jax.ShapeDtypeStruct((2, 2 * rows, width), kind),
            compiler_params=params(SMALL),
            cost_estimate=lasts(1),
            name="spread_out",
        )(self.section.reshape(1), self.kept, self.mate, *extra)


def pack_vectors(vectors, qv_bias, fc_bias):
    half = vectors[0].shape[0]
    more = fc_bias.shape[0] // half

    def kernel(*refs):
        out = refs[-1]
        out[...] = jnp.zeros_like(out)
        for i in range(len(vectors)):
            out[i : i + 1, :] = refs[i][...].astype(F32)
        out[6:8, :] = refs[-3][...].astype(F32)
        for i in range(more):
            out[8 + i : 9 + i, :] = refs[-2][:, i * half : (i + 1) * half].astype(F32)

    return pl.pallas_call(
        kernel,
        out_shape=jax.ShapeDtypeStruct((16, half), F32),
        compiler_params=params(SMALL),
        cost_estimate=lasts(1),
        name="pack_vectors",
    )(*[v.reshape(1, half) for v in vectors], qv_bias, fc_bias.reshape(1, -1))


def unpack_vectors(tensor, mine, other):
    half = mine.shape[1]

    def kernel(which, a, b, vec, bqv0, bqv1, bfc0, bfc1):
        for value in range(2):

            @pl.when(which[0] == value)
            def _():
                order = (a, b) if value == 0 else (b, a)
                vec[:, :half] = order[0][0:8, :]
                vec[:, half:] = order[1][0:8, :]

        for ref, bqv, bfc in ((a, bqv0, bfc0), (b, bqv1, bfc1)):
            bqv[...] = ref[6:8, :]
            for i in range(4):
                bfc[:, i * half : (i + 1) * half] = ref[8 + i : 9 + i, :]

    shape = lambda *s: jax.ShapeDtypeStruct(s, F32)
    pair = [shape(2, half)] * 2 + [shape(1, 4 * half)] * 2
    return pl.pallas_call(
        kernel,
        in_specs=[pl.BlockSpec(memory_space=pltpu.SMEM)]
        + [pl.BlockSpec(memory_space=pltpu.VMEM)] * 2,
        out_shape=[shape(8, 2 * half)] + pair,
        compiler_params=params(SMALL),
        cost_estimate=lasts(1),
        name="unpack_vectors",
    )(tensor.reshape(1), mine, other)


def assemble(where, own, arrived, mate):
    count = arrived.shape[0] // 3
    half = own.shape[1]

    def kernel(which, own_ref, arrived_ref, mate_ref, out, mine):
        for section in range(2):
            for tensor in range(2):

                @pl.when((which[0] == section) & (which[2] == tensor))
                def _():
                    here = slice(tensor * half, (tensor + 1) * half)
                    there = slice((1 - tensor) * half, (2 - tensor) * half)
                    out[2 * count :, here] = own_ref[...]
                    for place in range(2):
                        ref = arrived_ref if place == section else mate_ref
                        rows = slice(place * count, (place + 1) * count)
                        later = slice((2 + place) * count, (3 + place) * count)
                        out[later, there] = ref[:count, :]
                        out[rows, here] = ref[count : 2 * count, :]
                        out[rows, there] = ref[2 * count :, :]
                    rows = slice((2 + section) * count, (3 + section) * count)
                    mine[...] = out[rows, :]

    return pl.pallas_call(
        kernel,
        in_specs=[pl.BlockSpec(memory_space=pltpu.SMEM)]
        + [pl.BlockSpec(memory_space=pltpu.VMEM)] * 3,
        out_shape=[
            jax.ShapeDtypeStruct((4 * count, 2 * half), BF16),
            jax.ShapeDtypeStruct((count, 2 * half), BF16),
        ],
        compiler_params=params(SMALL),
        cost_estimate=lasts(1),
        name="assemble",
    )(where, own, arrived, mate)


def gather_rows(own):
    section = lax.axis_index("section")
    mate = swap(own, "section")
    prior_mine = shift(own, 1)
    prior_mate = swap(prior_mine, "section")
    first = section == 0
    pick = lambda a, b: [jnp.where(first, a, b), jnp.where(first, b, a)]
    return jnp.concatenate(pick(prior_mine, prior_mate) + pick(own, mate), axis=0)


def local(
    inputs,
    out_grads,
    seq_blocks,
    ln1_gain,
    ln1_shift,
    qkv_weight,
    qv_bias,
    out_weight,
    out_bias,
    ln2_gain,
    ln2_shift,
    fc_weight,
    fc_bias,
    proj_weight,
    proj_bias,
):
    section = lax.axis_index("section")
    position = lax.axis_index("dp")
    tensor = lax.axis_index("tensor")
    half = D // 2
    block = inputs.shape[1]
    count = block // 2
    hidden = fc_weight.shape[1]
    first = tensor == 0

    def features(mine, other):
        return ordered(first, mine, other, mine.ndim - 1)

    micro = lambda a, which: lax.dynamic_index_in_dim(a, which, 0, keepdims=False)
    starts = jnp.cumsum(seq_blocks, axis=1) - seq_blocks
    continuing = jnp.logical_not(jnp.any(starts == position, axis=1))
    continues = micro(continuing, tensor)
    where = jnp.stack([section, continues.astype(jnp.int32), tensor])

    own_rows = lambda a, which: part(micro(a, which), section, 2)
    here, there = own_rows(inputs, tensor), own_rows(inputs, 1 - tensor)
    count_dp = lax.axis_size("dp")
    ahead = [(2 * i + j, 2 * i + 2 + 1 - j) for i in range(count_dp - 1) for j in range(2)]
    across = swap(there, "tensor")
    before_here = shift(here, 1)
    before_there = lax.ppermute(there, ("dp", "tensor"), ahead)
    arrived = jnp.concatenate([across, before_here, before_there], axis=0)
    mate = swap(arrived, "section")
    rows_one, mine = assemble(where, micro(inputs, tensor), arrived, mate)
    vectors = pack_vectors(
        [ln1_gain, ln1_shift, out_bias, ln2_gain, ln2_shift, proj_bias], qv_bias, fc_bias
    )
    vec, *biases = unpack_vectors(tensor, vectors, swap(vectors, "tensor"))
    qkv_weight = jnp.concatenate([qkv_weight[:, n] for n in range(3)], axis=0)
    fetch_qkv, fetch_out = Fetch(qkv_weight, 1), Fetch(out_weight, 1)
    fetch_fc, fetch_proj = Fetch(fc_weight, 2), Fetch(proj_weight, 2)
    weights = [
        dict(wqkv=qkv_weight, wo=out_weight, wfc=fc_weight, wp=proj_weight),
        {},
    ]
    for half_index in range(2):
        weights[half_index].update(bqv=biases[half_index], bfc=biases[2 + half_index])
    dep = fetch_qkv.start(across)
    dep = fetch_out.start(dep)
    dep = fetch_fc.start(dep)
    one = forward_part(where, vec, weights, (0,), (), rows=rows_one, dep=dep)
    dep = fetch_proj.start(one["sum"])
    dep = fetch_qkv.join(dep)
    dep = fetch_out.join(dep)
    dep = fetch_qkv.finish(dep)
    dep = fetch_out.finish(dep)
    dep = fetch_fc.join(dep)
    weights[1].update(wqkv=fetch_qkv.whole, wo=fetch_out.whole)
    one_b = forward_part(
        where, vec, weights, (1,), (0,), nrm=one["nrm"], carried=one["sum"], dep=dep
    )
    dep = fetch_proj.join(one_b["sum"])
    dep = fetch_fc.finish(dep)
    dep = fetch_proj.finish(dep)
    weights[1].update(wfc=fetch_fc.whole, wp=fetch_proj.whole)
    one_c = forward_part(
        where, vec, weights, (), (1,), nrm2=one_b["nrm2"], carried=one_b["sum"], dep=dep
    )
    one = {**one, **one_b, **one_c}
    dout = features(own_rows(out_grads, tensor), swap(own_rows(out_grads, 1 - tensor), "tensor"))
    two = forward_part(where, vec, weights, (0, 1), (0, 1), rows=gather_rows(one["act"]))
    acts = Spread(section, tensor)
    dep = acts.add([one["act"], two["act"]], two["act"])
    mlp_two = backward_mlp(vec, weights, two, dout, dep)
    attn_two = backward_attn(where, weights, two, mlp_two["ga"])
    norm_two = NormBack(one["act"], vec, attn_two, mlp_two["dh1"])
    dep = norm_two.send(attn_two["prior"])
    layers = [[two, mlp_two, attn_two, dout], [one, None, None, None]]
    flat = lambda s, piece: (0, 0)
    by_piece = lambda s, piece: (0, piece)
    own_piece = lambda s, piece: (2 + s, piece)
    square, tall, narrow, thin = (count, D), (4 * count, half), (count, half), (4 * count, half)

    def proj_terms(i):
        return [[(f[f"u{i}"], square, by_piece, g, square, flat) for f, _, _, g in layers]]

    def fc_terms(i):
        return [
            [(f["nrm2"], square, flat, m[f"df{i}"], square, by_piece) for f, m, _, _ in layers]
        ]

    def attn_terms(i):
        return [
            [(f["nrm"], narrow, own_piece, a[f"dq{i}"], narrow, flat) for f, _, a, _ in layers if a],
            [(f["nrm"], tall, by_piece, a[f"dk{i}"], thin, flat) for f, _, a, _ in layers if a],
            [(f["nrm"], tall, by_piece, a[f"dv{i}"], thin, flat) for f, _, a, _ in layers if a],
            [(f[f"o{i}"], narrow, flat, m["ga"], narrow, by_piece) for f, m, a, _ in layers if a],
        ]

    proj, fc = Reduction(where, proj_terms), Reduction(where, fc_terms)
    attn = Reduction(where, attn_terms, True)
    dep = acts.turn(dep)
    dep = attn.first_layer(dep)
    low_two, small_two = norm_two.finish(dep)
    layers[1][3] = low_two
    dep = proj.theirs_foreign(low_two)
    dep = proj.theirs_own(dep)
    dep = acts_out = acts.finish(BF16, dep)
    dep = proj.foreign(dep)
    mlp_one = layers[1][1] = backward_mlp(vec, weights, one, low_two, dep)
    dep = proj.own(mlp_one["ga"])
    dep = fc.theirs_foreign(dep)
    dep = fc.theirs_own(dep)
    dep = proj.split(dep)
    dep = fc.foreign(dep)
    dep = fc.own(dep)
    attn_one = layers[1][2] = backward_attn(where, weights, one, mlp_one["ga"], dep)
    norm_one = NormBack(mine, vec, attn_one, mlp_one["dh1"])
    sums = grads = None
    low_one, small_one = None, None
    levels = 0
    while 2 ** (levels + 1) < count_dp:
        levels += 1
    dep = attn.theirs_foreign(attn_one["own"])
    dep = attn.theirs_own(dep)
    dep = proj.split(dep)
    dep = attn.foreign(dep)
    dep = fc.split(dep)
    dep = norm_one.send(dep)
    for level in range(1, levels):
        dep = proj.split(dep)
    dep = attn.own(dep)
    dep = proj.sum(dep)
    dep = fc.split(dep)
    low_one, small_one = norm_one.finish(dep)
    norms, mlps, attns = (small_one, small_two), (mlp_one, mlp_two), (attn_one, attn_two)
    dep = gather_small(where, norms, mlps, attns, low_one)
    sums = SmallSum(dep)
    for level in range(1, levels):
        dep = proj.join(dep)
    dep = attn.split(dep)
    dep = sums.step(dep)
    for level in range(1, levels):
        dep = fc.split(dep)
        dep = sums.step(dep)
    dep = attn.split(dep)
    dep = fc.sum(dep)
    dep = proj.join(dep)
    for level in range(1, levels):
        dep = attn.split(dep)
        dep = fc.join(dep)
        dep = sums.step(dep)
    dep = attn.sum(dep)
    dep = fc.join(dep)
    dep = proj.join(dep)
    dep = sums.step(dep)
    dep = attn.join(dep)
    grads = Spread(section, tensor)
    dep = grads.add([low_one, low_two], dep)
    count_rows = hidden // 2

    def place_proj(out, piece, core):
        out[core * count_rows : (core + 1) * count_rows, :] = piece[...].astype(F32)

    def place_fc(out, piece, core):
        out[:, core * count_rows : (core + 1) * count_rows] = piece[...].astype(F32)

    dep = proj_grad = widen(section, proj.kept, proj.other, (hidden, D), place_proj, dep)
    for level in range(1, levels):
        dep = attn.join(dep)
    dep = sums.step(dep)
    dep = fc.join(dep)
    dep = grads.turn(dep)
    dep = fc_grad = widen(section, fc.kept, fc.other, (D, hidden), place_fc, dep)
    dep = grads_out = grads.finish(F32, dep)
    dep = attn.join(dep)

    def place_out(out, piece, core):
        value = piece[3 * half : 4 * half, :].astype(F32)
        out[:, core * half : (core + 1) * half] = value

    while sums.other is not None:
        dep = sums.step(dep)
    out_grad = widen(section, attn.kept, attn.other, (half, D), place_out, dep)
    sides = lambda n: [a[n * half : (n + 1) * half] for a in (attn.kept, attn.other)]
    qkv_grad = jnp.stack([ordered(section == 0, *sides(n), 0) for n in range(3)], axis=1)
    qkv_grad = qkv_grad.astype(F32)
    rows_here = part(sums.array[:8], tensor, 2, 1)
    bfc_grad = part(sums.array[8:12], tensor, 2).reshape(hidden)
    return (
        acts_out[None],
        grads_out[None],
        rows_here[0],
        rows_here[1],
        qkv_grad,
        rows_here[6:8],
        out_grad,
        rows_here[4],
        rows_here[2],
        rows_here[3],
        fc_grad,
        bfc_grad,
        proj_grad,
        rows_here[5],
    )


def solution(mesh):
    in_specs = (
        P(None, "dp", "tensor"),
        P(None, "dp", "tensor"),
        P(),
        P("tensor"),
        P("tensor"),
        P(None, None, "tensor"),
        P(None, "tensor"),
        P("tensor", None),
        P("tensor"),
        P("tensor"),
        P("tensor"),
        P(None, "tensor"),
        P("tensor"),
        P("tensor", None),
        P("tensor"),
    )
    out_specs = (
        P("section", None, "dp", "tensor"),
        P("section", None, "dp", "tensor"),
        P("tensor"),
        P("tensor"),
        P(None, None, "tensor"),
        P(None, "tensor"),
        P("tensor", None),
        P("tensor"),
        P("tensor"),
        P("tensor"),
        P(None, "tensor"),
        P("tensor"),
        P("tensor", None),
        P("tensor"),
    )
    return jax.shard_map(local, mesh=mesh, in_specs=in_specs, out_specs=out_specs, check_vma=False)
```

```python
import functools

import jax
import jax.numpy as jnp
from jax import lax
from jax.experimental import pallas as pl
from jax.experimental.pallas import tpu as pltpu
from jax.sharding import PartitionSpec as P

D = 768
HEAD = 64
NORM_EPSILON = 1e-05
MASKED = -1e30
SCALE = HEAD ** (-0.5)
F32 = jnp.float32
BF16 = jnp.bfloat16
LIMIT = 60 * 1024 * 1024
SMALL = 12 * 1024 * 1024


def dot(a, b, dims=((1,), (0,))):
    return lax.dot_general(a, b, (dims, ((), ())), preferred_element_type=F32)


def swap(array, axis):
    return lax.ppermute(array, axis, [(0, 1), (1, 0)])


def shift(array, by):
    count = lax.axis_size("dp")
    pairs = [(i, i + by) for i in range(count) if 0 <= i + by < count]
    return lax.ppermute(array, "dp", pairs)


def exchange(array, bit):
    count = lax.axis_size("dp")
    return lax.ppermute(array, "dp", [(i, i ^ bit) for i in range(count)])


def part(array, which, parts, axis=0):
    size = array.shape[axis] // parts
    return lax.dynamic_slice_in_dim(array, which * size, size, axis)


def ordered(first, mine, other, axis):
    return jnp.concatenate(
        [jnp.where(first, mine, other), jnp.where(first, other, mine)], axis=axis
    )


def add_low(a, b):
    return (a.astype(F32) + b.astype(F32)).astype(BF16)


def lasts(microseconds):
    return pl.CostEstimate(flops=int(microseconds * 2e7), bytes_accessed=1, transcendentals=0)


def params(limit):
    return pltpu.CompilerParams(vmem_limit_bytes=limit)


def after(dep):
    return ([], []) if dep is None else ([dep], [pl.BlockSpec(memory_space=pl.ANY)])


def sum_split(sets, side, dep=None):
    halves = [arrays[0].shape[0] // 2 for arrays in sets]
    if any(rows % 16 for rows in halves):
        totals = [sum(a.astype(F32) for a in arrays).astype(BF16) for arrays in sets]
        pick = lambda which: jnp.concatenate([part(t, which, 2) for t in totals], axis=0)
        return pick(side), pick(1 - side)
    width = sets[0][0].shape[1]
    extra, extra_specs = after(dep)
    operands, specs = [], []
    for arrays, rows in zip(sets, halves):
        for array in arrays:
            operands += [array, array]
            specs.append(pl.BlockSpec((rows, width), lambda j, which: (which[0], 0)))
            specs.append(pl.BlockSpec((rows, width), lambda j, which: (1 - which[0], 0)))

    def kernel(which, *refs):
        at, row = 0, 0
        for arrays, rows in zip(sets, halves):
            for out, first in ((refs[-2], at), (refs[-1], at + 1)):
                total = refs[first][...].astype(F32)
                for i in range(1, len(arrays)):
                    total += refs[first + 2 * i][...].astype(F32)
                out[row : row + rows, :] = total.astype(BF16)
            at, row = at + 2 * len(arrays), row + rows

    block = (sum(halves), width)
    flat = pl.BlockSpec(block, lambda j, which: (0, 0))
    return pl.pallas_call(
        kernel,
        grid_spec=pltpu.PrefetchScalarGridSpec(
            num_scalar_prefetch=1,
            grid=(1,),
            in_specs=specs + extra_specs,
            out_specs=[flat] * 2,
        ),
        out_shape=[jax.ShapeDtypeStruct(block, BF16)] * 2,
        compiler_params=params(SMALL),
        cost_estimate=lasts(1.2),
        name="sum_split",
    )(side.reshape(1), *operands, *extra)


def sum_rows(arrays, dep=None):
    rows, width = arrays[0].shape
    kind = arrays[0].dtype
    if rows % 16:
        return add_low(*arrays)
    extra, extra_specs = after(dep)

    def kernel(a, b, *rest):
        rest[-1][...] = (a[...].astype(F32) + b[...].astype(F32)).astype(kind)

    return pl.pallas_call(
        kernel,
        in_specs=[pl.BlockSpec(memory_space=pltpu.VMEM)] * 2 + extra_specs,
        out_shape=jax.ShapeDtypeStruct((rows, width), kind),
        compiler_params=params(SMALL),
        cost_estimate=lasts(0.7),
        name="sum_rows",
    )(*arrays, *extra)


def put_rows(side, mine, other, dep=None):
    rows, width = mine.shape
    if rows % 16:
        return ordered(side == 0, mine, other, 0)
    extra, extra_specs = after(dep)

    def kernel(which, a, b, *rest):
        out = rest[-1]
        out[pl.ds(pl.multiple_of(which[0] * rows, rows), rows), :] = a[...]
        out[pl.ds(pl.multiple_of((1 - which[0]) * rows, rows), rows), :] = b[...]

    return pl.pallas_call(
        kernel,
        in_specs=[pl.BlockSpec(memory_space=pltpu.SMEM)]
        + [pl.BlockSpec(memory_space=pltpu.VMEM)] * 2
        + extra_specs,
        out_shape=jax.ShapeDtypeStruct((2 * rows, width), BF16),
        compiler_params=params(SMALL),
        cost_estimate=lasts(0.7),
        name="put_rows",
    )(side.reshape(1), mine, other, *extra)


def gradient(where, terms, which, added=(), dep=None):
    arrays, specs, plan = [], [], []
    for term in terms:
        plan.append(len(term))
        for a, a_block, a_index, b, b_block, b_index in term:
            for array, block, index in ((a, a_block, a_index), (b, b_block, b_index)):
                arrays.append(array)
                specs.append(
                    pl.BlockSpec(block, lambda j, w, index=index: index(w[0], w[0] ^ which))
                )
    rows, width = terms[0][0][1][1], terms[0][0][4][1]
    total = rows * len(terms)
    last = len(arrays)
    for cuts in added:
        for array in cuts:
            arrays.append(array)
            specs.append(pl.BlockSpec(array.shape, lambda j, w: (0, 0)))
    extra, extra_specs = after(dep)

    def kernel(w, *refs):
        out, at = refs[-1], 0
        for i, layers in enumerate(plan):
            value = None
            for _ in range(layers):
                one = dot(refs[at][...], refs[at + 1][...], ((0,), (0,)))
                value = one if value is None else value + one
                at += 2
            span = slice(i * rows, (i + 1) * rows)
            place = last
            for cuts in added:
                each = total // len(cuts)
                taken = []
                for cut in range(len(cuts)):
                    low, high = max(span.start, cut * each), min(span.stop, (cut + 1) * each)
                    if low < high:
                        taken.append(refs[place + cut][low - cut * each : high - cut * each, :])
                value += jnp.concatenate([t.astype(F32) for t in taken], axis=0)
                place += len(cuts)
            out[span, :] = value.astype(BF16)

    return pl.pallas_call(
        kernel,
        grid_spec=pltpu.PrefetchScalarGridSpec(
            num_scalar_prefetch=1,
            grid=(1,),
            in_specs=specs + extra_specs,
            out_specs=pl.BlockSpec((total, width), lambda j, w: (0, 0)),
        ),
        out_shape=jax.ShapeDtypeStruct((total, width), BF16),
        compiler_params=params(SMALL),
        cost_estimate=lasts(1 + sum(plan) * 0.35),
        name="gradient",
    )(where, *arrays, *extra)


class Reduction:
    def __init__(self, where, terms_of, early=False):
        self.where, self.terms_of = where, terms_of
        self.bit = 1
        self.early = early
        self.partial = {}

    def first_layer(self, dep):
        for half in (1, 0):
            for which in (1, 0):
                terms = [term[:1] for term in self.terms_of(half)]
                dep = self.partial[half, which] = gradient(self.where, terms, which, dep=dep)
        return dep

    def piece(self, half, which, mate, dep):
        terms, added = self.terms_of(half), [] if mate is None else [mate]
        added = [a if isinstance(a, list) else [a] for a in added]
        if self.early:
            terms = [term[1:] for term in terms]
            added.append([self.partial[half, which]])
        return gradient(self.where, terms, which, added, dep)

    def theirs_foreign(self, dep):
        theirs = self.piece(1, 1, None, dep)
        self.mate_foreign = self.to_mate(theirs)
        return theirs

    def theirs_own(self, dep):
        theirs = self.piece(0, 1, None, dep)
        self.mate_own = self.to_mate(theirs)
        return theirs

    def to_mate(self, theirs):
        rows = theirs.shape[0] // 2
        return [swap(theirs[i * rows : (i + 1) * rows], "section") for i in range(2)]

    def foreign(self, dep):
        foreign = self.piece(1, 0, self.mate_foreign, dep)
        self.across = swap(foreign, "tensor")
        return foreign

    def own(self, dep):
        own = self.piece(0, 0, self.mate_own, dep)
        self.arrays = [own, self.across]
        return own

    def side(self):
        return (lax.axis_index("dp") // self.bit) % 2

    def split(self, dep, other=None):
        sets = [self.arrays] if other is None else [self.arrays, other.arrays]
        kept, sent = sum_split(sets, self.side(), dep)
        self.arrays = [kept, exchange(sent, self.bit)]
        self.bit *= 2
        return kept

    def sum(self, dep):
        self.kept = sum_rows(self.arrays, dep)
        self.send_back()
        return self.kept

    def send_back(self):
        self.bit //= 2
        self.other = swap(self.kept, "section") if self.bit == 0 else exchange(self.kept, self.bit)

    def join(self, dep):
        self.kept = put_rows(self.side(), self.kept, self.other, dep)
        self.send_back()
        return self.kept


class SmallSum:
    def __init__(self, array):
        bits = []
        while 2 ** len(bits) < lax.axis_size("dp"):
            bits.append(2 ** len(bits))
        self.moves = [lambda a: swap(a, "section"), lambda a: swap(a, "tensor")]
        self.moves += [lambda a, bit=bit: exchange(a, bit) for bit in bits]
        self.array = array
        self.other = self.moves.pop(0)(array)

    def step(self, dep):
        if self.other is None:
            return dep
        self.array = sum_rows([self.array, self.other], dep)
        self.other = self.moves.pop(0)(self.array) if self.moves else None
        return self.array


def widen(section, kept, other, shape, place, dep):
    extra, extra_specs = after(dep)

    def kernel(which, a, b, *rest):
        for value in range(2):

            @pl.when(which[0] == value)
            def _():
                place(rest[-1], a, value)
                place(rest[-1], b, 1 - value)

    return pl.pallas_call(
        kernel,
        in_specs=[pl.BlockSpec(memory_space=pltpu.SMEM)]
        + [pl.BlockSpec(memory_space=pltpu.VMEM)] * 2
        + extra_specs,
        out_shape=jax.ShapeDtypeStruct(shape, F32),
        compiler_params=params(2 * SMALL),
        cost_estimate=lasts(2),
        name="widen",
    )(section.reshape(1), kept, other, *extra)


def take_rows(array, which, parts, dep):
    rows, width = array.shape[0] // parts, array.shape[1]
    extra, extra_specs = after(dep)

    def kernel(w, a, *rest):
        rest[-1][...] = a[...]

    return pl.pallas_call(
        kernel,
        grid_spec=pltpu.PrefetchScalarGridSpec(
            num_scalar_prefetch=1,
            grid=(1,),
            in_specs=[pl.BlockSpec((rows, width), lambda j, w: (w[0], 0))] + extra_specs,
            out_specs=pl.BlockSpec((rows, width), lambda j, w: (0, 0)),
        ),
        out_shape=jax.ShapeDtypeStruct((rows, width), array.dtype),
        compiler_params=params(SMALL),
        cost_estimate=lasts(0.7),
        name="take_rows",
    )(which.reshape(1), array, *extra)


class Fetch:
    def __init__(self, array, bit):
        self.array, self.bit = array, bit
        self.section = lax.axis_index("section")
        self.side = (lax.axis_index("dp") // bit) % 2

    def start(self, dep):
        piece = take_rows(self.array, self.section * 2 + self.side, 4, dep)
        self.mine = swap(piece, "tensor")
        self.other = exchange(self.mine, self.bit)
        return piece

    def join(self, dep):
        self.mine = put_rows(self.side, self.mine, self.other, dep)
        self.other = swap(self.mine, "section")
        return self.mine

    def finish(self, dep):
        self.whole = put_rows(self.section, self.mine, self.other, dep)
        return self.whole


def standard(rows):
    center = jnp.sum(rows, axis=1, keepdims=True) / D
    spread = jnp.sum(rows * rows, axis=1, keepdims=True) / D - center * center
    factor = lax.rsqrt(spread + NORM_EPSILON)
    return (rows - center) * factor, factor


def norm(rows, gain, shift_by):
    return (standard(rows)[0] * gain + shift_by).astype(BF16)


def norm_back(grad, normed, factor, gain):
    scaled = grad * gain
    mean = jnp.sum(scaled, axis=1, keepdims=True) / D
    along = jnp.sum(scaled * normed, axis=1, keepdims=True) / D
    return factor * (scaled - mean - normed * along)


def total_rows(array):
    return jnp.sum(array.astype(F32), axis=0, keepdims=True)


def only_head(array, which):
    lane = lax.broadcasted_iota(jnp.int32, array.shape, 1)
    return jnp.where((lane >= HEAD) == (which == 1), array, jnp.zeros_like(array))


GELU_A = 0.7978845608028654
GELU_B = 0.044715
PAIR = 2 * HEAD
CHUNK = 768


class Call:
    def __init__(self):
        self.names, self.arrays, self.out_names, self.out_shape, self.scratch = [], [], [], [], []

    def take(self, name, array):
        self.names.append(name)
        self.arrays.append(array)

    def give(self, name, shape, dtype):
        self.out_names.append(name)
        self.out_shape.append(jax.ShapeDtypeStruct(shape, dtype))

    def keep(self, name, shape, dtype):
        self.scratch.append((name, pltpu.VMEM(shape, dtype)))

    def run(self, body, flags, name, time, dep=None):
        extra, extra_specs = after(dep)
        taken, given = len(self.names), len(self.out_names)
        memory = [pltpu.VMEM(a.shape, a.dtype) for a in self.arrays]
        memory += [pltpu.VMEM(o.shape, o.dtype) for o in self.out_shape]
        memory += [shape for _, shape in self.scratch]
        memory.append(pltpu.SemaphoreType.DMA((taken + given,)))

        def kernel(flags_ref, *refs):
            far = list(refs[:taken]) + list(refs[taken + len(extra) : taken + len(extra) + given])
            near = refs[taken + len(extra) + given :]
            names = self.names + self.out_names + [n for n, _ in self.scratch]
            held = dict(zip(names, near[: len(names)]))
            sems = near[-1]
            copies = {}
            for i, key in enumerate(self.names):
                copies[key] = pltpu.make_async_copy(far[i], held[key], sems.at[i])
                copies[key].start()
            waiting = dict(copies)
            leaving = []

            def get(key):
                if key in waiting:
                    waiting.pop(key).wait()
                return held[key]

            def send(*keys):
                for key in keys:
                    if key not in self.out_names:
                        continue
                    i = taken + self.out_names.index(key)
                    copy = pltpu.make_async_copy(held[key], far[i], sems.at[i])
                    copy.start()
                    leaving.append(copy)

            body(flags_ref, get, send)
            for key in list(waiting):
                waiting.pop(key).wait()
            for copy in leaving:
                copy.wait()

        anywhere = pl.BlockSpec(memory_space=pl.ANY)
        outs = pl.pallas_call(
            kernel,
            in_specs=[pl.BlockSpec(memory_space=pltpu.SMEM)] + [anywhere] * taken + extra_specs,
            out_specs=[anywhere] * given,
            out_shape=self.out_shape,
            scratch_shapes=memory,
            compiler_params=params(LIMIT),
            cost_estimate=lasts(time),
            name=name,
        )(flags, *self.arrays, *extra)
        return dict(zip(self.out_names, outs))


def each_pair(count, body):
    for i in range(count):
        body(slice(i * PAIR, (i + 1) * PAIR), i)


def forward_part(
    where, vec, weights, attn, mlp, rows=None, nrm=None, nrm2=None, carried=None, dep=None
):
    c = Call()
    c.take("vec", vec)
    if rows is not None:
        c.take("rows", rows)
    if nrm is not None:
        c.take("nrm", nrm)
    if carried is not None:
        c.take("carried", carried)
    if nrm2 is not None:
        c.take("nrm2", nrm2)
    full = rows if rows is not None else nrm
    count = carried.shape[0] if full is None else full.shape[0] // 4
    width = weights[0]["wo"].shape[0]
    hidden = weights[0]["wp"].shape[0]
    for half in attn:
        for name in ("bqv", "wqkv", "wo"):
            c.take(f"{name}{half}", weights[half][name])
    for half in mlp:
        for name in ("bfc", "wfc", "wp"):
            c.take(f"{name}{half}", weights[half][name])
    if rows is not None:
        c.give("nrm", (4 * count, D), BF16)
    for half in attn:
        for name, n, kind in (
            ("q", count, BF16), ("k", 4 * count, BF16), ("v", 4 * count, BF16),
            ("o", count, BF16), ("of", count, F32), ("rl", count, F32),
        ):
            c.give(f"{name}{half}", (n, width), kind)
        c.give(f"p{half}", (2 * width // PAIR, count, 4 * count), BF16)
    middle = bool(attn) and bool(mlp)
    if middle:
        c.give("h1", (count, D), F32)
        c.give("nrm2", (count, D), BF16)
    for half in mlp:
        c.give(f"f{half}", (count, hidden), F32)
        c.give(f"u{half}", (count, hidden), BF16)
    final = 1 in mlp
    if final:
        c.give("act", (count, D), BF16)
        c.keep("sum", (count, D), F32)
    else:
        c.give("sum", (count, D), F32)
    if attn:
        c.keep("mask", (count, 4 * count), F32)

    body = forward_body(attn, mlp, count, width, hidden, rows is not None)
    return c.run(body, where, "forward", 12 * len(attn) + 3 * len(mlp), dep)


def forward_body(attn, mlp, count, width, hidden, first):
    def body(flags, get, send):
        total = get("sum")
        vec = get("vec")
        span = pl.ds(pl.multiple_of(2 * count + flags[0] * count, count), count)
        if first:
            rows_ref = get("rows")
            get("nrm")[...] = norm(rows_ref[...].astype(F32), vec[0:1, :], vec[1:2, :])
            total[...] = rows_ref[span, :].astype(F32) + vec[2:3, :]
            send("nrm")
        else:
            total[...] = get("carried")[...]
        if attn:
            mask = get("mask")
            row = lax.broadcasted_iota(jnp.int32, mask.shape, 0) + flags[0] * count
            col = lax.broadcasted_iota(jnp.int32, mask.shape, 1)
            limit = jnp.where(col < 2 * count, flags[1] * (4 * count) - 1, row + 2 * count)
            mask[...] = jnp.where(col <= limit, 0.0, MASKED)
            nrm_ref = get("nrm")
        for half in attn:
            here = lambda name, half=half: get(f"{name}{half}")
            bqv, wqkv = here("bqv"), here("wqkv")

            def pair(lanes, i, here=here, bqv=bqv, wqkv=wqkv):
                wq, wk, wv = [wqkv[n * D : (n + 1) * D, lanes] for n in range(3)]
                q = (dot(nrm_ref[span, :], wq) + bqv[0:1, lanes]).astype(BF16)
                here("q")[:, lanes] = q
                kv = dot(nrm_ref[...], jnp.concatenate([wk, wv], axis=1))
                k = kv[:, :PAIR].astype(BF16)
                here("k")[:, lanes] = k
                v = (kv[:, PAIR:] + bqv[1:2, lanes]).astype(BF16)
                here("v")[:, lanes] = v
                scaled = q * jnp.asarray(SCALE, BF16)
                both = jnp.concatenate([only_head(scaled, 0), only_head(scaled, 1)], axis=0)
                scores = dot(both, k, ((1,), (1,)))
                lows, factors = [], []
                for which in range(2):
                    masked = scores[which * count : (which + 1) * count, :] + mask[...]
                    lifted = jnp.exp(masked - jnp.max(masked, axis=1, keepdims=True))
                    lows.append(lifted.astype(BF16))
                    here("p")[2 * i + which] = lows[which]
                    factors.append(1.0 / jnp.sum(lifted, axis=1, keepdims=True))
                sides = dot(jnp.concatenate(lows, axis=0), v)
                lane = lax.broadcasted_iota(jnp.int32, q.shape, 1)
                factor = jnp.where(lane < HEAD, factors[0], factors[1])
                here("rl")[:, lanes] = factor
                o = jnp.where(lane < HEAD, sides[:count], sides[count:]) * factor
                here("of")[:, lanes] = o
                here("o")[:, lanes] = o.astype(BF16)

            each_pair(width // PAIR, pair)
            send(*[f"{name}{half}" for name in ("q", "k", "v", "p", "o", "of", "rl")])
            total[...] += dot(here("o")[...], here("wo")[...])
        if attn and mlp:
            get("h1")[...] = total[...]
            get("nrm2")[...] = norm(total[...], vec[3:4, :], vec[4:5, :])
            total[...] += vec[5:6, :]
            send("h1", "nrm2")
        for half in mlp:
            here = lambda name, half=half: get(f"{name}{half}")
            wfc, bfc = here("wfc"), here("bfc")
            for i in range(hidden // CHUNK):
                lanes = slice(i * CHUNK, (i + 1) * CHUNK)
                pre = dot(get("nrm2")[...], wfc[:, lanes]) + bfc[:, lanes]
                here("f")[:, lanes] = pre
                inner = jnp.tanh(GELU_A * (pre + GELU_B * pre * pre * pre))
                hidden_low = (0.5 * pre * (1.0 + inner)).astype(BF16)
                here("u")[:, lanes] = hidden_low
                total[...] += dot(hidden_low, here("wp")[lanes, :])
            send(f"f{half}", f"u{half}")
        if 1 in mlp:
            get("act")[...] = total[...].astype(BF16)
            send("act")
        else:
            send("sum")

    return body


def backward_mlp(vec, weights, kept, dout, where, dep=None):
    c = Call()
    count = dout.shape[0]
    hidden = weights[0]["wp"].shape[0]
    c.take("dout", dout)
    for half in range(2):
        c.take(f"wp{half}", weights[half]["wp"])
        c.take(f"f{half}", kept[f"f{half}"])
        c.take(f"wfc{half}", weights[half]["wfc"])
    c.take("h1", kept["h1"])
    c.take("vec", vec)
    for half in range(2):
        c.give(f"df{half}", (count, hidden), BF16)
        c.give(f"gfc{half}", (1, hidden), F32)
    c.give("ga", (count, D), BF16)
    c.give("dh1", (count, D), F32)
    c.give("small", (8, D), F32)
    return c.run(mlp_body(hidden), where, "backward_mlp", 7, dep)


def mlp_body(hidden):
    def body(flags, get, send):
        dout = get("dout")
        back = None
        for half in range(2):
            wp, f, wfc = get(f"wp{half}"), get(f"f{half}"), get(f"wfc{half}")
            for i in range(hidden // CHUNK):
                lanes = slice(i * CHUNK, (i + 1) * CHUNK)
                du = dot(dout[...], wp[lanes, :], ((1,), (1,)))
                pre = f[:, lanes]
                square = pre * pre
                inner = jnp.tanh(GELU_A * (pre + GELU_B * square * pre))
                slope = 0.5 * (1.0 + inner) + (0.5 * GELU_A) * pre * (1.0 - inner * inner) * (
                    1.0 + 3.0 * GELU_B * square
                )
                low = (du * slope).astype(BF16)
                get(f"df{half}")[:, lanes] = low
                get(f"gfc{half}")[:, lanes] = total_rows(low)
                one = dot(low, wfc[:, lanes], ((1,), (1,)))
                back = one if back is None else back + one
            send(f"df{half}", f"gfc{half}")
        vec = get("vec")
        normed, factor = standard(get("h1")[...])
        grad = dout[...].astype(F32) + norm_back(back, normed, factor, vec[3:4, :])
        get("dh1")[...] = grad
        low = grad.astype(BF16)
        get("ga")[...] = low
        sums = [total_rows(x) for x in (back * normed, back, low, dout[...])]
        get("small")[...] = jnp.concatenate(sums + [jnp.zeros((4, D), F32)], axis=0)
        send("ga", "dh1", "small")

    return body


def backward_attn(where, weights, kept, ga, dep=None):
    c = Call()
    count = ga.shape[0]
    width = weights[0]["wo"].shape[0]
    c.take("ga", ga)
    for half in range(2):
        c.take(f"wo{half}", weights[half]["wo"])
        for name in ("rl", "of", "q", "v", "p", "k"):
            c.take(f"{name}{half}", kept[f"{name}{half}"])
        c.take(f"wqkv{half}", weights[half]["wqkv"])
    for half in range(2):
        for name, n in (("dq", count), ("dk", 4 * count), ("dv", 4 * count)):
            c.give(f"{name}{half}", (n, width), BF16)
        c.give(f"gqv{half}", (8, width), F32)
    c.give("sent", (2 * count, D), BF16)
    c.give("prior", (count, D), BF16)
    c.give("own", (count, D), F32)
    c.keep("dn", (4 * count, D), F32)
    return c.run(attn_body(count, width), where, "backward_attn", 15, dep)


def attn_body(count, width):
    def body(flags, get, send):
        dn = get("dn")
        span = pl.ds(pl.multiple_of(2 * count + flags[0] * count, count), count)
        ga = get("ga")
        for half in range(2):
            here = lambda name, half=half: get(f"{name}{half}")
            do_all = dot(ga[...], here("wo")[...], ((1,), (1,)))
            refs = {name: here(name) for name in ("rl", "of", "q", "v", "p", "k")}

            def pair(lanes, i, here=here, do_all=do_all, refs=refs):
                by_head = lambda a: jnp.concatenate([only_head(a, 0), only_head(a, 1)], axis=0)
                do = (do_all[:, lanes] * refs["rl"][:, lanes]).astype(BF16)
                product = do.astype(F32) * refs["of"][:, lanes]
                center = jnp.sum(by_head(product), axis=1, keepdims=True)
                do_both = by_head(do)
                scaled_q = by_head(refs["q"][:, lanes] * jnp.asarray(SCALE, BF16))
                scaled_k = refs["k"][:, lanes] * jnp.asarray(SCALE, BF16)
                lifted = refs["p"][2 * i : 2 * i + 2].reshape(2 * count, 4 * count)
                dpw = dot(do_both, refs["v"][:, lanes], ((1,), (1,)))
                ds = (lifted.astype(F32) * (dpw - center)).astype(BF16)
                dq_both = dot(ds, scaled_k)
                lane = lax.broadcasted_iota(jnp.int32, do.shape, 1)
                dq = jnp.where(lane < HEAD, dq_both[:count], dq_both[count:]).astype(BF16)
                dk = dot(ds, scaled_q, ((0,), (0,))).astype(BF16)
                dv = dot(lifted, do_both, ((0,), (0,))).astype(BF16)
                here("dq")[:, lanes] = dq
                here("dk")[:, lanes] = dk
                here("dv")[:, lanes] = dv
                sums = [total_rows(dq), total_rows(dv), jnp.zeros((6, PAIR), F32)]
                here("gqv")[:, lanes] = jnp.concatenate(sums, axis=0)

            each_pair(width // PAIR, pair)
            send(*[f"{name}{half}" for name in ("dq", "dk", "dv", "gqv")])
            wqkv = here("wqkv")
            back = dot(here("dk")[...], wqkv[D : 2 * D, :], ((1,), (1,)))
            back += dot(here("dv")[...], wqkv[2 * D :, :], ((1,), (1,)))
            if half == 0:
                dn[...] = back
            else:
                dn[...] += back
            dn[span, :] += dot(here("dq")[...], wqkv[:D, :], ((1,), (1,)))
        at = lambda base, which: pl.ds(pl.multiple_of(base + which * count, count), count)
        mine, other = flags[0], 1 - flags[0]
        get("sent")[:count, :] = dn[at(0, other), :].astype(BF16)
        get("sent")[count:, :] = dn[at(2 * count, other), :].astype(BF16)
        send("sent")
        get("prior")[...] = dn[at(0, mine), :].astype(BF16)
        get("own")[...] = dn[at(2 * count, mine), :]
        send("prior", "own")

    return body


def last_layer(where, vec, weights, rows, dout, dep=None):
    c = Call()
    count = rows.shape[0] // 4
    width = weights[0]["wo"].shape[0]
    hidden = weights[0]["wp"].shape[0]
    c.take("vec", vec)
    c.take("rows", rows)
    for name in ("bqv", "wqkv", "wo"):
        for half in range(2):
            c.take(f"{name}{half}", weights[half][name])
    for half in range(2):
        for name in ("bfc", "wfc", "wp"):
            c.take(f"{name}{half}", weights[half][name])
    c.take("dout", dout)
    c.give("nrm", (4 * count, D), BF16)
    c.give("nrm2", (count, D), BF16)
    c.give("act", (count, D), BF16)
    c.give("ga", (count, D), BF16)
    c.give("dh1", (count, D), F32)
    c.give("small", (8, D), F32)
    c.give("sent", (2 * count, D), BF16)
    c.give("prior", (count, D), BF16)
    c.give("own", (count, D), F32)
    for half in range(2):
        c.give(f"o{half}", (count, width), BF16)
        c.give(f"u{half}", (count, hidden), BF16)
        c.give(f"df{half}", (count, hidden), BF16)
        c.give(f"gfc{half}", (1, hidden), F32)
        for name, n in (("dq", count), ("dk", 4 * count), ("dv", 4 * count)):
            c.give(f"{name}{half}", (n, width), BF16)
        c.give(f"gqv{half}", (8, width), F32)
    for half in range(2):
        for name, n, kind in (
            ("q", count, BF16), ("k", 4 * count, BF16), ("v", 4 * count, BF16),
            ("of", count, F32), ("rl", count, F32),
        ):
            c.keep(f"{name}{half}", (n, width), kind)
        c.keep(f"p{half}", (2 * width // PAIR, count, 4 * count), BF16)
        c.keep(f"f{half}", (count, hidden), F32)
    c.keep("h1", (count, D), F32)
    c.keep("sum", (count, D), F32)
    c.keep("mask", (count, 4 * count), F32)
    c.keep("dn", (4 * count, D), F32)

    def body(flags, get, send):
        forward_body((0, 1), (0, 1), count, width, hidden, True)(flags, get, send)
        mlp_body(hidden)(flags, get, send)
        attn_body(count, width)(flags, get, send)

    return c.run(body, where, "last_layer", 40, dep)


def norm_kernel(rows, vec, own, mate, later, dh1, low, small):
    back = own[...] + mate[...].astype(F32) + later[...].astype(F32)
    normed, factor = standard(rows[...].astype(F32))
    low[...] = (dh1[...] + norm_back(back, normed, factor, vec[0:1, :])).astype(BF16)
    small[...] = jnp.concatenate(
        [total_rows(back * normed), total_rows(back), jnp.zeros((6, D), F32)], axis=0
    )


class NormBack:
    def __init__(self, rows, vec, back, dh1):
        self.rows, self.vec, self.back, self.dh1 = rows, vec, back, dh1
        self.mate = swap(back["sent"], "section")

    def send(self, dep):
        count = self.rows.shape[0]
        prior = sum_rows([self.back["prior"], self.mate[:count]], dep)
        self.later = shift(prior, -1)
        return prior

    def finish(self, dep):
        shape = jax.ShapeDtypeStruct
        extra, extra_specs = after(dep)
        count = self.rows.shape[0]
        operands = [
            self.rows, self.vec, self.back["own"], self.mate[count:], self.later, self.dh1,
        ]

        def kernel(*refs):
            norm_kernel(*refs[: len(operands)], *refs[-2:])

        return pl.pallas_call(
            kernel,
            in_specs=[pl.BlockSpec(memory_space=pltpu.VMEM)] * len(operands) + extra_specs,
            out_shape=[shape(self.dh1.shape, BF16), shape((8, D), F32)],
            name="first_norm_back",
            compiler_params=params(SMALL),
            cost_estimate=lasts(1),
        )(*operands, *extra)


def gather_small(where, norms, mlps, attns, dep):
    halves = [m[f"gfc{i}"] for m in mlps for i in range(2)]
    halves += [a[f"gqv{i}"] for a in attns for i in range(2)]
    operands = list(norms) + [m["small"] for m in mlps] + halves
    extra, extra_specs = after(dep)

    def kernel(flags, norm_a, norm_b, mlp_a, mlp_b, f0, f1, g0, g1, a0, a1, b0, b1, *rest):
        out = rest[-1]
        out[...] = jnp.zeros_like(out)
        out[0:2, :] = norm_a[0:2, :] + norm_b[0:2, :]
        out[2:6, :] = mlp_a[0:4, :] + mlp_b[0:4, :]
        bqv = (a0[0:2, :] + b0[0:2, :], a1[0:2, :] + b1[0:2, :])
        bfc = (f0[...] + g0[...], f1[...] + g1[...])
        for value in range(2):

            @pl.when(flags[2] == value)
            def _():
                out[6:8, :] = jnp.concatenate([bqv[value], bqv[1 - value]], axis=1)
                for place in range(2):
                    row = 8 + 2 * (place if value == 0 else 1 - place)
                    out[row : row + 1, :] = bfc[place][:, :D]
                    out[row + 1 : row + 2, :] = bfc[place][:, D:]

    return pl.pallas_call(
        kernel,
        in_specs=[pl.BlockSpec(memory_space=pltpu.SMEM)]
        + [pl.BlockSpec(memory_space=pltpu.VMEM)] * len(operands)
        + extra_specs,
        out_shape=jax.ShapeDtypeStruct((16, D), F32),
        compiler_params=params(SMALL),
        cost_estimate=lasts(1),
        name="gather_small",
    )(where, *operands, *extra)


class Spread:
    def __init__(self, section, tensor):
        self.section, self.tensor = section, tensor

    def add(self, layers, dep):
        rows, width = layers[0].shape[0], layers[0].shape[1] // 2
        extra, extra_specs = after(dep)

        def kernel(which, a, b, *rest):
            for value in range(2):

                @pl.when(which[0] == value)
                def _():
                    for layer, ref in enumerate((a, b)):
                        rest[-2][layer] = ref[:, value * width : (value + 1) * width]
                        rest[-1][layer] = ref[:, (1 - value) * width : (2 - value) * width]

        shape = jax.ShapeDtypeStruct((2, rows, width), layers[0].dtype)
        self.mine, theirs = pl.pallas_call(
            kernel,
            in_specs=[pl.BlockSpec(memory_space=pltpu.SMEM)]
            + [pl.BlockSpec(memory_space=pltpu.VMEM)] * 2
            + extra_specs,
            out_shape=[shape, shape],
            compiler_params=params(SMALL),
            cost_estimate=lasts(0.7),
            name="spread",
        )(self.tensor.reshape(1), *layers, *extra)
        self.theirs = swap(theirs, "tensor")
        return self.mine

    def turn(self, dep):
        extra, extra_specs = after(dep)

        def kernel(which, a, b, *rest):
            for section in range(2):
                for tensor in range(2):

                    @pl.when((which[0] == section) & (which[1] == tensor))
                    def _():
                        for out, layer in ((rest[-2], section), (rest[-1], 1 - section)):
                            out[tensor] = a[layer]
                            out[1 - tensor] = b[layer]

        shape = jax.ShapeDtypeStruct(self.mine.shape, self.mine.dtype)
        self.kept, sent = pl.pallas_call(
            kernel,
            in_specs=[pl.BlockSpec(memory_space=pltpu.SMEM)]
            + [pl.BlockSpec(memory_space=pltpu.VMEM)] * 2
            + extra_specs,
            out_shape=[shape, shape],
            compiler_params=params(SMALL),
            cost_estimate=lasts(0.7),
            name="turn",
        )(jnp.stack([self.section, self.tensor]), self.mine, self.theirs, *extra)
        self.mate = swap(sent, "section")
        return self.kept

    def finish(self, kind, dep):
        _, rows, width = self.kept.shape
        extra, extra_specs = after(dep)

        def kernel(which, mine, mate, *rest):
            out = rest[-1]
            for value in range(2):

                @pl.when(which[0] == value)
                def _():
                    for micro in range(2):
                        here = slice(value * rows, (value + 1) * rows)
                        there = slice((1 - value) * rows, (2 - value) * rows)
                        out[micro, here, :] = mine[micro].astype(kind)
                        out[micro, there, :] = mate[micro].astype(kind)

        return pl.pallas_call(
            kernel,
            in_specs=[pl.BlockSpec(memory_space=pltpu.SMEM)]
            + [pl.BlockSpec(memory_space=pltpu.VMEM)] * 2
            + extra_specs,
            out_shape=jax.ShapeDtypeStruct((2, 2 * rows, width), kind),
            compiler_params=params(SMALL),
            cost_estimate=lasts(1),
            name="spread_out",
        )(self.section.reshape(1), self.kept, self.mate, *extra)


def pack_vectors(vectors, qv_bias, fc_bias):
    half = vectors[0].shape[0]
    more = fc_bias.shape[0] // half

    def kernel(*refs):
        out = refs[-1]
        out[...] = jnp.zeros_like(out)
        for i in range(len(vectors)):
            out[i : i + 1, :] = refs[i][...].astype(F32)
        out[6:8, :] = refs[-3][...].astype(F32)
        for i in range(more):
            out[8 + i : 9 + i, :] = refs[-2][:, i * half : (i + 1) * half].astype(F32)

    return pl.pallas_call(
        kernel,
        out_shape=jax.ShapeDtypeStruct((16, half), F32),
        compiler_params=params(SMALL),
        cost_estimate=lasts(1),
        name="pack_vectors",
    )(*[v.reshape(1, half) for v in vectors], qv_bias, fc_bias.reshape(1, -1))


def unpack_vectors(tensor, mine, other):
    half = mine.shape[1]

    def kernel(which, a, b, vec, bqv0, bqv1, bfc0, bfc1):
        for value in range(2):

            @pl.when(which[0] == value)
            def _():
                order = (a, b) if value == 0 else (b, a)
                vec[:, :half] = order[0][0:8, :]
                vec[:, half:] = order[1][0:8, :]

        for ref, bqv, bfc in ((a, bqv0, bfc0), (b, bqv1, bfc1)):
            bqv[...] = ref[6:8, :]
            for i in range(4):
                bfc[:, i * half : (i + 1) * half] = ref[8 + i : 9 + i, :]

    shape = lambda *s: jax.ShapeDtypeStruct(s, F32)
    pair = [shape(2, half)] * 2 + [shape(1, 4 * half)] * 2
    return pl.pallas_call(
        kernel,
        in_specs=[pl.BlockSpec(memory_space=pltpu.SMEM)]
        + [pl.BlockSpec(memory_space=pltpu.VMEM)] * 2,
        out_shape=[shape(8, 2 * half)] + pair,
        compiler_params=params(SMALL),
        cost_estimate=lasts(1),
        name="unpack_vectors",
    )(tensor.reshape(1), mine, other)


def assemble(where, own, arrived, mate):
    count = arrived.shape[0] // 3
    half = own.shape[1]

    def kernel(which, own_ref, arrived_ref, mate_ref, out, mine):
        for section in range(2):
            for tensor in range(2):

                @pl.when((which[0] == section) & (which[2] == tensor))
                def _():
                    here = slice(tensor * half, (tensor + 1) * half)
                    there = slice((1 - tensor) * half, (2 - tensor) * half)
                    out[2 * count :, here] = own_ref[...]
                    for place in range(2):
                        ref = arrived_ref if place == section else mate_ref
                        rows = slice(place * count, (place + 1) * count)
                        later = slice((2 + place) * count, (3 + place) * count)
                        out[later, there] = ref[:count, :]
                        out[rows, here] = ref[count : 2 * count, :]
                        out[rows, there] = ref[2 * count :, :]
                    rows = slice((2 + section) * count, (3 + section) * count)
                    mine[...] = out[rows, :]

    return pl.pallas_call(
        kernel,
        in_specs=[pl.BlockSpec(memory_space=pltpu.SMEM)]
        + [pl.BlockSpec(memory_space=pltpu.VMEM)] * 3,
        out_shape=[
            jax.ShapeDtypeStruct((4 * count, 2 * half), BF16),
            jax.ShapeDtypeStruct((count, 2 * half), BF16),
        ],
        compiler_params=params(SMALL),
        cost_estimate=lasts(1),
        name="assemble",
    )(where, own, arrived, mate)


def gather_rows(own):
    section = lax.axis_index("section")
    mate = swap(own, "section")
    prior_mine = shift(own, 1)
    prior_mate = swap(prior_mine, "section")
    first = section == 0
    pick = lambda a, b: [jnp.where(first, a, b), jnp.where(first, b, a)]
    return jnp.concatenate(pick(prior_mine, prior_mate) + pick(own, mate), axis=0)


def local(
    inputs,
    out_grads,
    seq_blocks,
    ln1_gain,
    ln1_shift,
    qkv_weight,
    qv_bias,
    out_weight,
    out_bias,
    ln2_gain,
    ln2_shift,
    fc_weight,
    fc_bias,
    proj_weight,
    proj_bias,
):
    section = lax.axis_index("section")
    position = lax.axis_index("dp")
    tensor = lax.axis_index("tensor")
    half = D // 2
    block = inputs.shape[1]
    count = block // 2
    hidden = fc_weight.shape[1]
    first = tensor == 0

    def features(mine, other):
        return ordered(first, mine, other, mine.ndim - 1)

    micro = lambda a, which: lax.dynamic_index_in_dim(a, which, 0, keepdims=False)
    starts = jnp.cumsum(seq_blocks, axis=1) - seq_blocks
    continuing = jnp.logical_not(jnp.any(starts == position, axis=1))
    continues = micro(continuing, tensor)
    where = jnp.stack([section, continues.astype(jnp.int32), tensor])

    own_rows = lambda a, which: part(micro(a, which), section, 2)
    here, there = own_rows(inputs, tensor), own_rows(inputs, 1 - tensor)
    count_dp = lax.axis_size("dp")
    ahead = [(2 * i + j, 2 * i + 2 + 1 - j) for i in range(count_dp - 1) for j in range(2)]
    across = swap(there, "tensor")
    before_here = shift(here, 1)
    before_there = lax.ppermute(there, ("dp", "tensor"), ahead)
    arrived = jnp.concatenate([across, before_here, before_there], axis=0)
    mate = swap(arrived, "section")
    rows_one, mine = assemble(where, micro(inputs, tensor), arrived, mate)
    vectors = pack_vectors(
        [ln1_gain, ln1_shift, out_bias, ln2_gain, ln2_shift, proj_bias], qv_bias, fc_bias
    )
    vec, *biases = unpack_vectors(tensor, vectors, swap(vectors, "tensor"))
    qkv_weight = jnp.concatenate([qkv_weight[:, n] for n in range(3)], axis=0)
    fetch_qkv, fetch_out = Fetch(qkv_weight, 1), Fetch(out_weight, 1)
    fetch_fc, fetch_proj = Fetch(fc_weight, 2), Fetch(proj_weight, 2)
    weights = [
        dict(wqkv=qkv_weight, wo=out_weight, wfc=fc_weight, wp=proj_weight),
        {},
    ]
    for half_index in range(2):
        weights[half_index].update(bqv=biases[half_index], bfc=biases[2 + half_index])
    dep = fetch_qkv.start(across)
    dep = fetch_out.start(dep)
    dep = fetch_fc.start(dep)
    one = forward_part(where, vec, weights, (0,), (), rows=rows_one, dep=dep)
    dep = fetch_proj.start(one["sum"])
    dep = fetch_qkv.join(dep)
    dep = fetch_out.join(dep)
    dep = fetch_qkv.finish(dep)
    dep = fetch_out.finish(dep)
    dep = fetch_fc.join(dep)
    weights[1].update(wqkv=fetch_qkv.whole, wo=fetch_out.whole)
    one_b = forward_part(
        where, vec, weights, (1,), (0,), nrm=one["nrm"], carried=one["sum"], dep=dep
    )
    dep = fetch_proj.join(one_b["sum"])
    dep = fetch_fc.finish(dep)
    dep = fetch_proj.finish(dep)
    weights[1].update(wfc=fetch_fc.whole, wp=fetch_proj.whole)
    one_c = forward_part(
        where, vec, weights, (), (1,), nrm2=one_b["nrm2"], carried=one_b["sum"], dep=dep
    )
    one = {**one, **one_b, **one_c}
    dout = features(own_rows(out_grads, tensor), swap(own_rows(out_grads, 1 - tensor), "tensor"))
    two = last_layer(where, vec, weights, gather_rows(one["act"]), dout)
    norm_two = NormBack(one["act"], vec, two, two["dh1"])
    acts = Spread(section, tensor)
    dep = norm_two.send(two["prior"])
    dep = acts.add([one["act"], two["act"]], dep)
    layers = [[two, two, two, dout], [one, None, None, None]]
    flat = lambda s, piece: (0, 0)
    by_piece = lambda s, piece: (0, piece)
    own_piece = lambda s, piece: (2 + s, piece)
    square, tall, narrow, thin = (count, D), (4 * count, half), (count, half), (4 * count, half)

    def proj_terms(i):
        return [[(f[f"u{i}"], square, by_piece, g, square, flat) for f, _, _, g in layers]]

    def fc_terms(i):
        return [
            [(f["nrm2"], square, flat, m[f"df{i}"], square, by_piece) for f, m, _, _ in layers]
        ]

    def attn_terms(i):
        return [
            [(f["nrm"], narrow, own_piece, a[f"dq{i}"], narrow, flat) for f, _, a, _ in layers if a],
            [(f["nrm"], tall, by_piece, a[f"dk{i}"], thin, flat) for f, _, a, _ in layers if a],
            [(f["nrm"], tall, by_piece, a[f"dv{i}"], thin, flat) for f, _, a, _ in layers if a],
            [(f[f"o{i}"], narrow, flat, m["ga"], narrow, by_piece) for f, m, a, _ in layers if a],
        ]

    proj, fc = Reduction(where, proj_terms), Reduction(where, fc_terms)
    attn = Reduction(where, attn_terms, True)
    dep = attn.first_layer(dep)
    low_two, small_two = norm_two.finish(dep)
    layers[1][3] = low_two
    dep = proj.theirs_foreign(low_two)
    dep = proj.theirs_own(dep)
    dep = acts.turn(dep)
    dep = proj.foreign(dep)
    mlp_one = layers[1][1] = backward_mlp(vec, weights, one, low_two, where, dep)
    dep = acts_out = acts.finish(BF16, mlp_one["ga"])
    dep = proj.own(dep)
    dep = fc.theirs_foreign(dep)
    dep = fc.theirs_own(dep)
    dep = proj.split(dep)
    dep = fc.foreign(dep)
    dep = fc.own(dep)
    attn_one = layers[1][2] = backward_attn(where, weights, one, mlp_one["ga"], dep)
    norm_one = NormBack(mine, vec, attn_one, mlp_one["dh1"])
    sums = grads = None
    low_one, small_one = None, None
    levels = 0
    while 2 ** (levels + 1) < count_dp:
        levels += 1
    dep = attn.theirs_foreign(attn_one["own"])
    dep = attn.theirs_own(dep)
    dep = proj.split(dep)
    dep = attn.foreign(dep)
    dep = fc.split(dep)
    dep = norm_one.send(dep)
    for level in range(1, levels):
        dep = proj.split(dep)
    dep = attn.own(dep)
    dep = proj.sum(dep)
    dep = fc.split(dep)
    low_one, small_one = norm_one.finish(dep)
    norms, mlps, attns = (small_one, small_two), (mlp_one, two), (attn_one, two)
    dep = gather_small(where, norms, mlps, attns, low_one)
    sums = SmallSum(dep)
    for level in range(1, levels):
        dep = proj.join(dep)
    dep = attn.split(dep)
    dep = sums.step(dep)
    for level in range(1, levels):
        dep = fc.split(dep)
        dep = sums.step(dep)
    dep = attn.split(dep)
    dep = fc.sum(dep)
    dep = proj.join(dep)
    for level in range(1, levels):
        dep = attn.split(dep)
        dep = fc.join(dep)
        dep = sums.step(dep)
    dep = attn.sum(dep)
    dep = fc.join(dep)
    dep = proj.join(dep)
    dep = sums.step(dep)
    dep = attn.join(dep)
    grads = Spread(section, tensor)
    dep = grads.add([low_one, low_two], dep)
    count_rows = hidden // 2

    def place_proj(out, piece, core):
        out[core * count_rows : (core + 1) * count_rows, :] = piece[...].astype(F32)

    def place_fc(out, piece, core):
        out[:, core * count_rows : (core + 1) * count_rows] = piece[...].astype(F32)

    dep = proj_grad = widen(section, proj.kept, proj.other, (hidden, D), place_proj, dep)
    for level in range(1, levels):
        dep = attn.join(dep)
    dep = sums.step(dep)
    dep = fc.join(dep)
    dep = grads.turn(dep)
    dep = fc_grad = widen(section, fc.kept, fc.other, (D, hidden), place_fc, dep)
    dep = grads_out = grads.finish(F32, dep)
    dep = attn.join(dep)

    def place_out(out, piece, core):
        value = piece[3 * half : 4 * half, :].astype(F32)
        out[:, core * half : (core + 1) * half] = value

    while sums.other is not None:
        dep = sums.step(dep)
    out_grad = widen(section, attn.kept, attn.other, (half, D), place_out, dep)
    sides = lambda n: [a[n * half : (n + 1) * half] for a in (attn.kept, attn.other)]
    qkv_grad = jnp.stack([ordered(section == 0, *sides(n), 0) for n in range(3)], axis=1)
    qkv_grad = qkv_grad.astype(F32)
    rows_here = part(sums.array[:8], tensor, 2, 1)
    bfc_grad = part(sums.array[8:12], tensor, 2).reshape(hidden)
    return (
        acts_out[None],
        grads_out[None],
        rows_here[0],
        rows_here[1],
        qkv_grad,
        rows_here[6:8],
        out_grad,
        rows_here[4],
        rows_here[2],
        rows_here[3],
        fc_grad,
        bfc_grad,
        proj_grad,
        rows_here[5],
    )


def solution(mesh):
    in_specs = (
        P(None, "dp", "tensor"),
        P(None, "dp", "tensor"),
        P(),
        P("tensor"),
        P("tensor"),
        P(None, None, "tensor"),
        P(None, "tensor"),
        P("tensor", None),
        P("tensor"),
        P("tensor"),
        P("tensor"),
        P(None, "tensor"),
        P("tensor"),
        P("tensor", None),
        P("tensor"),
    )
    out_specs = (
        P("section", None, "dp", "tensor"),
        P("section", None, "dp", "tensor"),
        P("tensor"),
        P("tensor"),
        P(None, None, "tensor"),
        P(None, "tensor"),
        P("tensor", None),
        P("tensor"),
        P("tensor"),
        P("tensor"),
        P(None, "tensor"),
        P("tensor"),
        P("tensor", None),
        P("tensor"),
    )
    return jax.shard_map(local, mesh=mesh, in_specs=in_specs, out_specs=out_specs, check_vma=False)
```

```python
import math

import jax
import jax.numpy as jnp
from jax import lax
from jax.experimental import pallas as pl
from jax.experimental.pallas import tpu as pltpu
from jax.sharding import PartitionSpec as P

SECTION, TENSOR = "section", "tensor"
D = 768
HEAD = 64
NORM_EPSILON = 1e-05
MASKED = -1e30
SCALE = HEAD ** (-0.5)
F32 = jnp.float32
BF16 = jnp.bfloat16
LIMIT = 60 * 1024 * 1024
SMALL = 12 * 1024 * 1024
SPARE = 12 * 1024 * 1024


def dot(a, b, dims=((1,), (0,))):
    return lax.dot_general(a, b, (dims, ((), ())), preferred_element_type=F32)


def swap(array, axis):
    return lax.ppermute(array, axis, [(0, 1), (1, 0)])


def shift(array, by):
    count = lax.axis_size("dp")
    pairs = [(i, i + by) for i in range(count) if 0 <= i + by < count]
    return lax.ppermute(array, "dp", pairs)


def exchange(array, bit):
    count = lax.axis_size("dp")
    return lax.ppermute(array, "dp", [(i, i ^ bit) for i in range(count)])


def part(array, which, parts, axis=0):
    size = array.shape[axis] // parts
    return lax.dynamic_slice_in_dim(array, which * size, size, axis)


def ordered(first, mine, other, axis):
    return jnp.concatenate(
        [jnp.where(first, mine, other), jnp.where(first, other, mine)], axis=axis
    )


def add_low(a, b):
    return (a.astype(F32) + b.astype(F32)).astype(BF16)


def lasts(microseconds):
    return pl.CostEstimate(flops=int(microseconds * 2e7), bytes_accessed=1, transcendentals=0)


def params(limit):
    return pltpu.CompilerParams(vmem_limit_bytes=limit)


def after(dep):
    return ([], []) if dep is None else ([dep], [pl.BlockSpec(memory_space=pl.ANY)])


def sum_split(sets, side, dep=None):
    halves = [arrays[0].shape[0] // 2 for arrays in sets]
    if any(rows % 16 for rows in halves):
        totals = [sum(a.astype(F32) for a in arrays).astype(BF16) for arrays in sets]
        pick = lambda which: jnp.concatenate([part(t, which, 2) for t in totals], axis=0)
        return pick(side), pick(1 - side)
    width = sets[0][0].shape[1]
    extra, extra_specs = after(dep)
    operands, specs = [], []
    for arrays, rows in zip(sets, halves):
        for array in arrays:
            operands += [array, array]
            specs.append(pl.BlockSpec((rows, width), lambda j, which: (which[0], 0)))
            specs.append(pl.BlockSpec((rows, width), lambda j, which: (1 - which[0], 0)))

    def kernel(which, *refs):
        at, row = 0, 0
        for arrays, rows in zip(sets, halves):
            for out, first in ((refs[-2], at), (refs[-1], at + 1)):
                total = refs[first][...].astype(F32)
                for i in range(1, len(arrays)):
                    total += refs[first + 2 * i][...].astype(F32)
                out[row : row + rows, :] = total.astype(BF16)
            at, row = at + 2 * len(arrays), row + rows

    block = (sum(halves), width)
    flat = pl.BlockSpec(block, lambda j, which: (0, 0))
    return pl.pallas_call(
        kernel,
        grid_spec=pltpu.PrefetchScalarGridSpec(
            num_scalar_prefetch=1,
            grid=(1,),
            in_specs=specs + extra_specs,
            out_specs=[flat] * 2,
        ),
        out_shape=[jax.ShapeDtypeStruct(block, BF16)] * 2,
        compiler_params=params(SMALL),
        cost_estimate=lasts(1.2),
        name="sum_split",
    )(side.reshape(1), *operands, *extra)


def sum_rows(arrays, dep=None):
    rows, width = arrays[0].shape
    kind = arrays[0].dtype
    if rows % 16:
        return add_low(*arrays)
    extra, extra_specs = after(dep)

    def kernel(a, b, *rest):
        rest[-1][...] = (a[...].astype(F32) + b[...].astype(F32)).astype(kind)

    return pl.pallas_call(
        kernel,
        in_specs=[pl.BlockSpec(memory_space=pltpu.VMEM)] * 2 + extra_specs,
        out_shape=jax.ShapeDtypeStruct((rows, width), kind),
        compiler_params=params(SMALL),
        cost_estimate=lasts(0.7),
        name="sum_rows",
    )(*arrays, *extra)


def put_rows(side, mine, other, dep=None):
    rows, width = mine.shape
    if rows % 16:
        return ordered(side == 0, mine, other, 0)
    extra, extra_specs = after(dep)

    def kernel(which, a, b, *rest):
        out = rest[-1]
        out[pl.ds(pl.multiple_of(which[0] * rows, rows), rows), :] = a[...]
        out[pl.ds(pl.multiple_of((1 - which[0]) * rows, rows), rows), :] = b[...]

    return pl.pallas_call(
        kernel,
        in_specs=[pl.BlockSpec(memory_space=pltpu.SMEM)]
        + [pl.BlockSpec(memory_space=pltpu.VMEM)] * 2
        + extra_specs,
        out_shape=jax.ShapeDtypeStruct((2 * rows, width), BF16),
        compiler_params=params(SMALL),
        cost_estimate=lasts(0.7),
        name="put_rows",
    )(side.reshape(1), mine, other, *extra)


def gradient(where, terms, which, added=(), dep=None, cuts=1):
    arrays, specs, plan = [], [], []
    for term in terms:
        plan.append(len(term))
        for a, a_block, a_index, b, b_block, b_index in term:
            for array, block, index in ((a, a_block, a_index), (b, b_block, b_index)):
                arrays.append(array)
                specs.append(
                    pl.BlockSpec(block, lambda j, w, index=index: index(w[0], w[0] ^ which))
                )
    rows, width = terms[0][0][1][1], terms[0][0][4][1]
    total = rows * len(terms)
    last = len(arrays)
    for pieces in added:
        for array in pieces:
            arrays.append(array)
            specs.append(pl.BlockSpec(array.shape, lambda j, w: (0, 0)))
    extra, extra_specs = after(dep)

    def kernel(w, *refs):
        outs, at = refs[len(refs) - cuts :], 0
        for i, layers in enumerate(plan):
            value = None
            for _ in range(layers):
                one = dot(refs[at][...], refs[at + 1][...], ((0,), (0,)))
                value = one if value is None else value + one
                at += 2
            span = slice(i * rows, (i + 1) * rows)
            place = last
            for pieces in added:
                each = total // len(pieces)
                taken = []
                for cut in range(len(pieces)):
                    low, high = max(span.start, cut * each), min(span.stop, (cut + 1) * each)
                    if low < high:
                        taken.append(refs[place + cut][low - cut * each : high - cut * each, :])
                value += jnp.concatenate([t.astype(F32) for t in taken], axis=0)
                place += len(pieces)
            each = total // cuts
            for cut in range(cuts):
                low, high = max(span.start, cut * each), min(span.stop, (cut + 1) * each)
                if low < high:
                    taken = value[low - span.start : high - span.start, :]
                    outs[cut][low - cut * each : high - cut * each, :] = taken.astype(BF16)

    outs = pl.pallas_call(
        kernel,
        grid_spec=pltpu.PrefetchScalarGridSpec(
            num_scalar_prefetch=1,
            grid=(1,),
            in_specs=specs + extra_specs,
            out_specs=[pl.BlockSpec((total // cuts, width), lambda j, w: (0, 0))] * cuts,
        ),
        out_shape=[jax.ShapeDtypeStruct((total // cuts, width), BF16)] * cuts,
        compiler_params=params(SMALL),
        cost_estimate=lasts(1 + sum(plan) * 0.35),
        name="gradient",
    )(where, *arrays, *extra)
    return outs[0] if cuts == 1 else outs


class Reduction:
    def __init__(self, where, terms_of, early=False):
        self.where, self.terms_of = where, terms_of
        self.bit = 1
        self.early = early
        self.partial = {}

    def first_layer(self, dep):
        for half in (1, 0):
            for which in (1, 0):
                terms = [term[:1] for term in self.terms_of(half)]
                dep = self.partial[half, which] = gradient(self.where, terms, which, dep=dep)
        return dep

    def piece(self, half, which, mate, dep, cuts=1):
        terms, added = self.terms_of(half), [] if mate is None else [mate]
        added = [a if isinstance(a, list) else [a] for a in added]
        if self.early:
            terms = [term[1:] for term in terms]
            added.append([self.partial[half, which]])
        return gradient(self.where, terms, which, added, dep, cuts)

    def theirs_foreign(self, dep):
        theirs = self.piece(1, 1, None, dep, 2)
        self.mate_foreign = [swap(cut, SECTION) for cut in theirs]
        return theirs[0]

    def theirs_own(self, dep):
        theirs = self.piece(0, 1, None, dep, 2)
        self.mate_own = [swap(cut, SECTION) for cut in theirs]
        return theirs[0]

    def foreign(self, dep):
        foreign = self.piece(1, 0, self.mate_foreign, dep)
        self.across = swap(foreign, TENSOR)
        return foreign

    def own(self, dep):
        own = self.piece(0, 0, self.mate_own, dep)
        self.arrays = [own, self.across]
        return own

    def side(self):
        return (lax.axis_index("dp") // self.bit) % 2

    def split(self, dep, other=None):
        sets = [self.arrays] if other is None else [self.arrays, other.arrays]
        kept, sent = sum_split(sets, self.side(), dep)
        self.arrays = [kept, exchange(sent, self.bit)]
        self.bit *= 2
        return kept

    def sum(self, dep):
        self.kept = sum_rows(self.arrays, dep)
        self.send_back()
        return self.kept

    def send_back(self):
        self.bit //= 2
        self.other = swap(self.kept, SECTION) if self.bit == 0 else exchange(self.kept, self.bit)

    def join(self, dep):
        self.kept = put_rows(self.side(), self.kept, self.other, dep)
        self.send_back()
        return self.kept


class SmallSum:
    def __init__(self, array):
        bits = []
        while 2 ** len(bits) < lax.axis_size("dp"):
            bits.append(2 ** len(bits))
        self.moves = [lambda a: swap(a, SECTION), lambda a: swap(a, TENSOR)]
        self.moves += [lambda a, bit=bit: exchange(a, bit) for bit in bits]
        self.array = array
        self.other = self.moves.pop(0)(array)

    def step(self, dep):
        if self.other is None:
            return dep
        self.array = sum_rows([self.array, self.other], dep)
        self.other = self.moves.pop(0)(self.array) if self.moves else None
        return self.array


def widen(section, kept, other, shape, place, dep):
    extra, extra_specs = after(dep)
    plan = [place(core) for core in range(2)]
    steps = len(plan[0])

    def kernel(which, a, b, *rest):
        out, token, held, sems = rest[-4:]
        token[...] = jnp.zeros_like(token)
        for value in range(2):

            @pl.when(which[0] == value)
            def _():
                copies = []
                for core, ref in ((value, a), (1 - value, b)):
                    for step, (rows, block) in enumerate(plan[core]):
                        held[block] = ref[rows, :].astype(F32)
                        copy = pltpu.make_async_copy(
                            held.at[block], out.at[block], sems.at[core * steps + step]
                        )
                        copy.start()
                        copies.append(copy)
                for copy in copies:
                    copy.wait()

    return pl.pallas_call(
        kernel,
        in_specs=[pl.BlockSpec(memory_space=pltpu.SMEM)]
        + [pl.BlockSpec(memory_space=pltpu.VMEM)] * 2
        + extra_specs,
        out_specs=[pl.BlockSpec(memory_space=pltpu.HBM), pl.BlockSpec(memory_space=pltpu.VMEM)],
        out_shape=[jax.ShapeDtypeStruct(shape, F32), jax.ShapeDtypeStruct((8, 128), F32)],
        scratch_shapes=[pltpu.VMEM(shape, F32), pltpu.SemaphoreType.DMA((2 * steps,))],
        compiler_params=params(SMALL),
        cost_estimate=lasts(2),
        name="widen",
    )(section.reshape(1), kept, other, *extra)


def take_rows(array, which, parts, dep):
    rows, width = array.shape[0] // parts, array.shape[1]
    extra, extra_specs = after(dep)

    def kernel(w, a, *rest):
        rest[-1][...] = a[...]

    return pl.pallas_call(
        kernel,
        grid_spec=pltpu.PrefetchScalarGridSpec(
            num_scalar_prefetch=1,
            grid=(1,),
            in_specs=[pl.BlockSpec((rows, width), lambda j, w: (w[0], 0))] + extra_specs,
            out_specs=pl.BlockSpec((rows, width), lambda j, w: (0, 0)),
        ),
        out_shape=jax.ShapeDtypeStruct((rows, width), array.dtype),
        compiler_params=params(SMALL),
        cost_estimate=lasts(0.7),
        name="take_rows",
    )(which.reshape(1), array, *extra)


class Fetch:
    def __init__(self, array, bit):
        self.array, self.bit = array, bit
        self.section = lax.axis_index(SECTION)
        self.side = (lax.axis_index("dp") // bit) % 2

    def start(self, dep):
        piece = take_rows(self.array, self.section * 2 + self.side, 4, dep)
        self.mine = swap(piece, TENSOR)
        self.other = exchange(self.mine, self.bit)
        return piece

    def join(self, dep):
        self.mine = put_rows(self.side, self.mine, self.other, dep)
        self.other = swap(self.mine, SECTION)
        return self.mine

    def finish(self, dep):
        self.whole = put_rows(self.section, self.mine, self.other, dep)
        return self.whole


def standard(rows):
    center = jnp.sum(rows, axis=1, keepdims=True) / D
    spread = jnp.sum(rows * rows, axis=1, keepdims=True) / D - center * center
    factor = lax.rsqrt(spread + NORM_EPSILON)
    return (rows - center) * factor, factor


def norm(rows, gain, shift_by):
    return (standard(rows)[0] * gain + shift_by).astype(BF16)


def norm_back(grad, normed, factor, gain):
    scaled = grad * gain
    mean = jnp.sum(scaled, axis=1, keepdims=True) / D
    along = jnp.sum(scaled * normed, axis=1, keepdims=True) / D
    return factor * (scaled - mean - normed * along)


def total_rows(array):
    return jnp.sum(array.astype(F32), axis=0, keepdims=True)


def only_head(array, which):
    lane = lax.broadcasted_iota(jnp.int32, array.shape, 1)
    return jnp.where((lane >= HEAD) == (which == 1), array, jnp.zeros_like(array))


GELU_A = 0.7978845608028654
GELU_B = 0.044715
PAIR = 2 * HEAD
CHUNK = 768


class Call:
    def __init__(self):
        self.names, self.arrays, self.out_names, self.out_shape, self.scratch = [], [], [], [], []

    def take(self, name, array):
        self.names.append(name)
        self.arrays.append(array)

    def give(self, name, shape, dtype):
        self.out_names.append(name)
        self.out_shape.append(jax.ShapeDtypeStruct(shape, dtype))

    def keep(self, name, shape, dtype):
        self.scratch.append((name, pltpu.VMEM(shape, dtype)))

    def run(self, body, flags, name, time, dep=None):
        extra, extra_specs = after(dep)
        taken, given = len(self.names), len(self.out_names)
        memory = [pltpu.VMEM(a.shape, a.dtype) for a in self.arrays]
        memory += [pltpu.VMEM(o.shape, o.dtype) for o in self.out_shape]
        memory += [shape for _, shape in self.scratch]
        size = sum(math.prod(m.shape) * jnp.dtype(m.dtype).itemsize for m in memory)
        memory.append(pltpu.SemaphoreType.DMA((taken + given,)))

        def kernel(flags_ref, *refs):
            far = list(refs[:taken]) + list(refs[taken + len(extra) : taken + len(extra) + given])
            near = refs[taken + len(extra) + given :]
            names = self.names + self.out_names + [n for n, _ in self.scratch]
            held = dict(zip(names, near[: len(names)]))
            sems = near[-1]
            copies = {}
            for i, key in enumerate(self.names):
                copies[key] = pltpu.make_async_copy(far[i], held[key], sems.at[i])
                copies[key].start()
            waiting = dict(copies)
            leaving = []

            def get(key):
                if key in waiting:
                    waiting.pop(key).wait()
                return held[key]

            def send(*keys):
                for key in keys:
                    if key not in self.out_names:
                        continue
                    i = taken + self.out_names.index(key)
                    copy = pltpu.make_async_copy(held[key], far[i], sems.at[i])
                    copy.start()
                    leaving.append(copy)

            body(flags_ref, get, send)
            for key in list(waiting):
                waiting.pop(key).wait()
            for copy in leaving:
                copy.wait()

        anywhere = pl.BlockSpec(memory_space=pltpu.HBM)
        outs = pl.pallas_call(
            kernel,
            in_specs=[pl.BlockSpec(memory_space=pltpu.SMEM)] + [anywhere] * taken + extra_specs,
            out_specs=[anywhere] * given,
            out_shape=self.out_shape,
            scratch_shapes=memory,
            compiler_params=params(min(size + SPARE, LIMIT)),
            cost_estimate=lasts(time),
            name=name,
        )(flags, *self.arrays, *extra)
        return dict(zip(self.out_names, outs))


def each_pair(count, body):
    for i in range(count):
        body(slice(i * PAIR, (i + 1) * PAIR), i)


def forward_part(
    where, vec, weights, attn, mlp, rows=None, nrm=None, nrm2=None, carried=None, dep=None
):
    c = Call()
    c.take("vec", vec)
    if rows is not None:
        c.take("rows", rows)
    if nrm is not None:
        c.take("nrm", nrm)
    if carried is not None:
        c.take("carried", carried)
    if nrm2 is not None:
        c.take("nrm2", nrm2)
    full = rows if rows is not None else nrm
    count = carried.shape[0] if full is None else full.shape[0] // 4
    width = weights[0]["wo"].shape[0]
    hidden = weights[0]["wp"].shape[0]
    for half in attn:
        for name in ("bqv", "wqkv", "wo"):
            c.take(f"{name}{half}", weights[half][name])
    for half in mlp:
        for name in ("bfc", "wfc", "wp"):
            c.take(f"{name}{half}", weights[half][name])
    if rows is not None:
        c.give("nrm", (4 * count, D), BF16)
    for half in attn:
        for name, n, kind in (
            ("q", count, BF16), ("k", 4 * count, BF16), ("v", 4 * count, BF16),
            ("o", count, BF16), ("of", count, F32), ("rl", count, F32),
        ):
            c.give(f"{name}{half}", (n, width), kind)
        c.give(f"p{half}", (2 * width // PAIR, count, 4 * count), BF16)
    middle = bool(attn) and bool(mlp)
    if middle:
        c.give("h1", (count, D), F32)
        c.give("nrm2", (count, D), BF16)
    for half in mlp:
        c.give(f"f{half}", (count, hidden), F32)
        c.give(f"u{half}", (count, hidden), BF16)
    final = 1 in mlp
    if final:
        c.give("act", (count, D), BF16)
        c.keep("sum", (count, D), F32)
    else:
        c.give("sum", (count, D), F32)
    if attn:
        c.keep("mask", (count, 4 * count), F32)

    body = forward_body(attn, mlp, count, width, hidden, rows is not None)
    return c.run(body, where, "forward", 12 * len(attn) + 3 * len(mlp), dep)


def forward_body(attn, mlp, count, width, hidden, first):
    def body(flags, get, send):
        total = get("sum")
        vec = get("vec")
        span = pl.ds(pl.multiple_of(2 * count + flags[0] * count, count), count)
        if first:
            rows_ref = get("rows")
            get("nrm")[...] = norm(rows_ref[...].astype(F32), vec[0:1, :], vec[1:2, :])
            total[...] = rows_ref[span, :].astype(F32) + vec[2:3, :]
            send("nrm")
        else:
            total[...] = get("carried")[...]
        if attn:
            mask = get("mask")
            row = lax.broadcasted_iota(jnp.int32, mask.shape, 0) + flags[0] * count
            col = lax.broadcasted_iota(jnp.int32, mask.shape, 1)
            limit = jnp.where(col < 2 * count, flags[1] * (4 * count) - 1, row + 2 * count)
            mask[...] = jnp.where(col <= limit, 0.0, MASKED)
            nrm_ref = get("nrm")
        for half in attn:
            here = lambda name, half=half: get(f"{name}{half}")
            bqv, wqkv = here("bqv"), here("wqkv")

            def pair(lanes, i, here=here, bqv=bqv, wqkv=wqkv):
                wq, wk, wv = [wqkv[n * D : (n + 1) * D, lanes] for n in range(3)]
                q = (dot(nrm_ref[span, :], wq) + bqv[0:1, lanes]).astype(BF16)
                here("q")[:, lanes] = q
                kv = dot(nrm_ref[...], jnp.concatenate([wk, wv], axis=1))
                k = kv[:, :PAIR].astype(BF16)
                here("k")[:, lanes] = k
                v = (kv[:, PAIR:] + bqv[1:2, lanes]).astype(BF16)
                here("v")[:, lanes] = v
                scaled = q * jnp.asarray(SCALE, BF16)
                both = jnp.concatenate([only_head(scaled, 0), only_head(scaled, 1)], axis=0)
                scores = dot(both, k, ((1,), (1,)))
                lows, factors = [], []
                for which in range(2):
                    masked = scores[which * count : (which + 1) * count, :] + mask[...]
                    lifted = jnp.exp(masked - jnp.max(masked, axis=1, keepdims=True))
                    lows.append(lifted.astype(BF16))
                    here("p")[2 * i + which] = lows[which]
                    factors.append(1.0 / jnp.sum(lifted, axis=1, keepdims=True))
                sides = dot(jnp.concatenate(lows, axis=0), v)
                lane = lax.broadcasted_iota(jnp.int32, q.shape, 1)
                factor = jnp.where(lane < HEAD, factors[0], factors[1])
                here("rl")[:, lanes] = factor
                o = jnp.where(lane < HEAD, sides[:count], sides[count:]) * factor
                here("of")[:, lanes] = o
                here("o")[:, lanes] = o.astype(BF16)

            each_pair(width // PAIR, pair)
            send(*[f"{name}{half}" for name in ("q", "k", "v", "p", "o", "of", "rl")])
            total[...] += dot(here("o")[...], here("wo")[...])
        if attn and mlp:
            get("h1")[...] = total[...]
            get("nrm2")[...] = norm(total[...], vec[3:4, :], vec[4:5, :])
            total[...] += vec[5:6, :]
            send("h1", "nrm2")
        for half in mlp:
            here = lambda name, half=half: get(f"{name}{half}")
            wfc, bfc = here("wfc"), here("bfc")
            for i in range(hidden // CHUNK):
                lanes = slice(i * CHUNK, (i + 1) * CHUNK)
                pre = dot(get("nrm2")[...], wfc[:, lanes]) + bfc[:, lanes]
                here("f")[:, lanes] = pre
                inner = jnp.tanh(GELU_A * (pre + GELU_B * pre * pre * pre))
                hidden_low = (0.5 * pre * (1.0 + inner)).astype(BF16)
                here("u")[:, lanes] = hidden_low
                total[...] += dot(hidden_low, here("wp")[lanes, :])
            send(f"f{half}", f"u{half}")
        if 1 in mlp:
            get("act")[...] = total[...].astype(BF16)
            send("act")
        else:
            send("sum")

    return body


def backward_mlp(vec, weights, kept, dout, where, dep=None):
    c = Call()
    count = dout.shape[0]
    hidden = weights[0]["wp"].shape[0]
    c.take("dout", dout)
    for half in range(2):
        c.take(f"wp{half}", weights[half]["wp"])
        c.take(f"f{half}", kept[f"f{half}"])
        c.take(f"wfc{half}", weights[half]["wfc"])
    c.take("h1", kept["h1"])
    c.take("vec", vec)
    for half in range(2):
        c.give(f"df{half}", (count, hidden), BF16)
        c.give(f"gfc{half}", (1, hidden), F32)
    c.give("ga", (count, D), BF16)
    c.give("dh1", (count, D), F32)
    c.give("small", (8, D), F32)
    return c.run(mlp_body(hidden), where, "backward_mlp", 7, dep)


def mlp_body(hidden):
    def body(flags, get, send):
        dout = get("dout")
        back = None
        for half in range(2):
            wp, f, wfc = get(f"wp{half}"), get(f"f{half}"), get(f"wfc{half}")
            for i in range(hidden // CHUNK):
                lanes = slice(i * CHUNK, (i + 1) * CHUNK)
                du = dot(dout[...], wp[lanes, :], ((1,), (1,)))
                pre = f[:, lanes]
                square = pre * pre
                inner = jnp.tanh(GELU_A * (pre + GELU_B * square * pre))
                slope = 0.5 * (1.0 + inner) + (0.5 * GELU_A) * pre * (1.0 - inner * inner) * (
                    1.0 + 3.0 * GELU_B * square
                )
                low = (du * slope).astype(BF16)
                get(f"df{half}")[:, lanes] = low
                get(f"gfc{half}")[:, lanes] = total_rows(low)
                one = dot(low, wfc[:, lanes], ((1,), (1,)))
                back = one if back is None else back + one
            send(f"df{half}", f"gfc{half}")
        vec = get("vec")
        normed, factor = standard(get("h1")[...])
        grad = dout[...].astype(F32) + norm_back(back, normed, factor, vec[3:4, :])
        get("dh1")[...] = grad
        low = grad.astype(BF16)
        get("ga")[...] = low
        sums = [total_rows(x) for x in (back * normed, back, low, dout[...])]
        get("small")[...] = jnp.concatenate(sums + [jnp.zeros((4, D), F32)], axis=0)
        send("ga", "dh1", "small")

    return body


def backward_attn(where, weights, kept, ga, dep=None):
    c = Call()
    count = ga.shape[0]
    width = weights[0]["wo"].shape[0]
    c.take("ga", ga)
    for half in range(2):
        c.take(f"wo{half}", weights[half]["wo"])
        for name in ("rl", "of", "q", "v", "p", "k"):
            c.take(f"{name}{half}", kept[f"{name}{half}"])
        c.take(f"wqkv{half}", weights[half]["wqkv"])
    for half in range(2):
        for name, n in (("dq", count), ("dk", 4 * count), ("dv", 4 * count)):
            c.give(f"{name}{half}", (n, width), BF16)
        c.give(f"gqv{half}", (8, width), F32)
    c.give("sent", (2 * count, D), BF16)
    c.give("prior", (count, D), BF16)
    c.give("own", (count, D), F32)
    c.keep("dn", (4 * count, D), F32)
    return c.run(attn_body(count, width), where, "backward_attn", 15, dep)


def attn_body(count, width):
    def body(flags, get, send):
        dn = get("dn")
        span = pl.ds(pl.multiple_of(2 * count + flags[0] * count, count), count)
        ga = get("ga")
        for half in range(2):
            here = lambda name, half=half: get(f"{name}{half}")
            do_all = dot(ga[...], here("wo")[...], ((1,), (1,)))
            refs = {name: here(name) for name in ("rl", "of", "q", "v", "p", "k")}

            def pair(lanes, i, here=here, do_all=do_all, refs=refs):
                by_head = lambda a: jnp.concatenate([only_head(a, 0), only_head(a, 1)], axis=0)
                do = (do_all[:, lanes] * refs["rl"][:, lanes]).astype(BF16)
                product = do.astype(F32) * refs["of"][:, lanes]
                center = jnp.sum(by_head(product), axis=1, keepdims=True)
                do_both = by_head(do)
                scaled_q = by_head(refs["q"][:, lanes] * jnp.asarray(SCALE, BF16))
                scaled_k = refs["k"][:, lanes] * jnp.asarray(SCALE, BF16)
                lifted = refs["p"][2 * i : 2 * i + 2].reshape(2 * count, 4 * count)
                dpw = dot(do_both, refs["v"][:, lanes], ((1,), (1,)))
                ds = (lifted.astype(F32) * (dpw - center)).astype(BF16)
                dq_both = dot(ds, scaled_k)
                lane = lax.broadcasted_iota(jnp.int32, do.shape, 1)
                dq = jnp.where(lane < HEAD, dq_both[:count], dq_both[count:]).astype(BF16)
                dk = dot(ds, scaled_q, ((0,), (0,))).astype(BF16)
                dv = dot(lifted, do_both, ((0,), (0,))).astype(BF16)
                here("dq")[:, lanes] = dq
                here("dk")[:, lanes] = dk
                here("dv")[:, lanes] = dv
                sums = [total_rows(dq), total_rows(dv), jnp.zeros((6, PAIR), F32)]
                here("gqv")[:, lanes] = jnp.concatenate(sums, axis=0)

            each_pair(width // PAIR, pair)
            send(*[f"{name}{half}" for name in ("dq", "dk", "dv", "gqv")])
            wqkv = here("wqkv")
            back = dot(here("dk")[...], wqkv[D : 2 * D, :], ((1,), (1,)))
            back += dot(here("dv")[...], wqkv[2 * D :, :], ((1,), (1,)))
            if half == 0:
                dn[...] = back
            else:
                dn[...] += back
            dn[span, :] += dot(here("dq")[...], wqkv[:D, :], ((1,), (1,)))
        at = lambda base, which: pl.ds(pl.multiple_of(base + which * count, count), count)
        mine, other = flags[0], 1 - flags[0]
        get("sent")[:count, :] = dn[at(0, other), :].astype(BF16)
        get("sent")[count:, :] = dn[at(2 * count, other), :].astype(BF16)
        send("sent")
        get("prior")[...] = dn[at(0, mine), :].astype(BF16)
        get("own")[...] = dn[at(2 * count, mine), :]
        send("prior", "own")

    return body


def last_layer(where, vec, weights, rows, dout, dep=None):
    c = Call()
    count = rows.shape[0] // 4
    width = weights[0]["wo"].shape[0]
    hidden = weights[0]["wp"].shape[0]
    c.take("vec", vec)
    c.take("rows", rows)
    for name in ("bqv", "wqkv", "wo"):
        for half in range(2):
            c.take(f"{name}{half}", weights[half][name])
    for half in range(2):
        for name in ("bfc", "wfc", "wp"):
            c.take(f"{name}{half}", weights[half][name])
    c.take("dout", dout)
    c.give("nrm", (4 * count, D), BF16)
    c.give("nrm2", (count, D), BF16)
    c.give("act", (count, D), BF16)
    c.give("ga", (count, D), BF16)
    c.give("dh1", (count, D), F32)
    c.give("small", (8, D), F32)
    c.give("sent", (2 * count, D), BF16)
    c.give("prior", (count, D), BF16)
    c.give("own", (count, D), F32)
    for half in range(2):
        c.give(f"o{half}", (count, width), BF16)
        c.give(f"u{half}", (count, hidden), BF16)
        c.give(f"df{half}", (count, hidden), BF16)
        c.give(f"gfc{half}", (1, hidden), F32)
        for name, n in (("dq", count), ("dk", 4 * count), ("dv", 4 * count)):
            c.give(f"{name}{half}", (n, width), BF16)
        c.give(f"gqv{half}", (8, width), F32)
    for half in range(2):
        for name, n, kind in (
            ("q", count, BF16), ("k", 4 * count, BF16), ("v", 4 * count, BF16),
            ("of", count, F32), ("rl", count, F32),
        ):
            c.keep(f"{name}{half}", (n, width), kind)
        c.keep(f"p{half}", (2 * width // PAIR, count, 4 * count), BF16)
        c.keep(f"f{half}", (count, hidden), F32)
    c.keep("h1", (count, D), F32)
    c.keep("sum", (count, D), F32)
    c.keep("mask", (count, 4 * count), F32)
    c.keep("dn", (4 * count, D), F32)

    def body(flags, get, send):
        forward_body((0, 1), (0, 1), count, width, hidden, True)(flags, get, send)
        mlp_body(hidden)(flags, get, send)
        attn_body(count, width)(flags, get, send)

    return c.run(body, where, "last_layer", 40, dep)


def norm_kernel(rows, vec, own, mate, later, dh1, low, small):
    back = own[...] + mate[...].astype(F32) + later[...].astype(F32)
    normed, factor = standard(rows[...].astype(F32))
    low[...] = (dh1[...] + norm_back(back, normed, factor, vec[0:1, :])).astype(BF16)
    small[...] = jnp.concatenate(
        [total_rows(back * normed), total_rows(back), jnp.zeros((6, D), F32)], axis=0
    )


class NormBack:
    def __init__(self, rows, vec, back, dh1):
        self.rows, self.vec, self.back, self.dh1 = rows, vec, back, dh1
        self.mate = swap(back["sent"], SECTION)

    def send(self, dep):
        count = self.rows.shape[0]
        prior = sum_rows([self.back["prior"], self.mate[:count]], dep)
        self.later = shift(prior, -1)
        return prior

    def finish(self, dep):
        shape = jax.ShapeDtypeStruct
        extra, extra_specs = after(dep)
        count = self.rows.shape[0]
        operands = [
            self.rows, self.vec, self.back["own"], self.mate[count:], self.later, self.dh1,
        ]

        def kernel(*refs):
            norm_kernel(*refs[: len(operands)], *refs[-2:])

        return pl.pallas_call(
            kernel,
            in_specs=[pl.BlockSpec(memory_space=pltpu.VMEM)] * len(operands) + extra_specs,
            out_shape=[shape(self.dh1.shape, BF16), shape((8, D), F32)],
            name="first_norm_back",
            compiler_params=params(SMALL),
            cost_estimate=lasts(1),
        )(*operands, *extra)


def gather_small(where, norms, mlps, attns, dep):
    halves = [m[f"gfc{i}"] for m in mlps for i in range(2)]
    halves += [a[f"gqv{i}"] for a in attns for i in range(2)]
    operands = list(norms) + [m["small"] for m in mlps] + halves
    extra, extra_specs = after(dep)

    def kernel(flags, norm_a, norm_b, mlp_a, mlp_b, f0, f1, g0, g1, a0, a1, b0, b1, *rest):
        out = rest[-1]
        out[...] = jnp.zeros_like(out)
        out[0:2, :] = norm_a[0:2, :] + norm_b[0:2, :]
        out[2:6, :] = mlp_a[0:4, :] + mlp_b[0:4, :]
        bqv = (a0[0:2, :] + b0[0:2, :], a1[0:2, :] + b1[0:2, :])
        bfc = (f0[...] + g0[...], f1[...] + g1[...])
        for value in range(2):

            @pl.when(flags[2] == value)
            def _():
                out[6:8, :] = jnp.concatenate([bqv[value], bqv[1 - value]], axis=1)
                for place in range(2):
                    row = 8 + 2 * (place if value == 0 else 1 - place)
                    out[row : row + 1, :] = bfc[place][:, :D]
                    out[row + 1 : row + 2, :] = bfc[place][:, D:]

    return pl.pallas_call(
        kernel,
        in_specs=[pl.BlockSpec(memory_space=pltpu.SMEM)]
        + [pl.BlockSpec(memory_space=pltpu.VMEM)] * len(operands)
        + extra_specs,
        out_shape=jax.ShapeDtypeStruct((16, D), F32),
        compiler_params=params(SMALL),
        cost_estimate=lasts(1),
        name="gather_small",
    )(where, *operands, *extra)


class Spread:
    def __init__(self, section, tensor):
        self.section, self.tensor = section, tensor

    def add(self, layers, dep):
        rows, width = layers[0].shape[0], layers[0].shape[1] // 2
        extra, extra_specs = after(dep)

        def kernel(which, a, b, *rest):
            for value in range(2):

                @pl.when(which[0] == value)
                def _():
                    for layer, ref in enumerate((a, b)):
                        rest[-2][layer] = ref[:, value * width : (value + 1) * width]
                        rest[-1][layer] = ref[:, (1 - value) * width : (2 - value) * width]

        shape = jax.ShapeDtypeStruct((2, rows, width), layers[0].dtype)
        self.mine, theirs = pl.pallas_call(
            kernel,
            in_specs=[pl.BlockSpec(memory_space=pltpu.SMEM)]
            + [pl.BlockSpec(memory_space=pltpu.VMEM)] * 2
            + extra_specs,
            out_shape=[shape, shape],
            compiler_params=params(SMALL),
            cost_estimate=lasts(0.7),
            name="spread",
        )(self.tensor.reshape(1), *layers, *extra)
        self.theirs = swap(theirs, TENSOR)
        return self.mine

    def turn(self, dep):
        extra, extra_specs = after(dep)

        def kernel(which, a, b, *rest):
            for section in range(2):
                for tensor in range(2):

                    @pl.when((which[0] == section) & (which[1] == tensor))
                    def _():
                        for out, layer in ((rest[-2], section), (rest[-1], 1 - section)):
                            out[tensor] = a[layer]
                            out[1 - tensor] = b[layer]

        shape = jax.ShapeDtypeStruct(self.mine.shape, self.mine.dtype)
        self.kept, sent = pl.pallas_call(
            kernel,
            in_specs=[pl.BlockSpec(memory_space=pltpu.SMEM)]
            + [pl.BlockSpec(memory_space=pltpu.VMEM)] * 2
            + extra_specs,
            out_shape=[shape, shape],
            compiler_params=params(SMALL),
            cost_estimate=lasts(0.7),
            name="turn",
        )(jnp.stack([self.section, self.tensor]), self.mine, self.theirs, *extra)
        self.mate = swap(sent, SECTION)
        return self.kept

    def finish(self, kind, dep):
        _, rows, width = self.kept.shape
        extra, extra_specs = after(dep)

        def kernel(which, mine, mate, *rest):
            out = rest[-1]
            for value in range(2):

                @pl.when(which[0] == value)
                def _():
                    for micro in range(2):
                        here = slice(value * rows, (value + 1) * rows)
                        there = slice((1 - value) * rows, (2 - value) * rows)
                        out[micro, here, :] = mine[micro].astype(kind)
                        out[micro, there, :] = mate[micro].astype(kind)

        return pl.pallas_call(
            kernel,
            in_specs=[pl.BlockSpec(memory_space=pltpu.SMEM)]
            + [pl.BlockSpec(memory_space=pltpu.VMEM)] * 2
            + extra_specs,
            out_shape=jax.ShapeDtypeStruct((2, 2 * rows, width), kind),
            compiler_params=params(SMALL),
            cost_estimate=lasts(1),
            name="spread_out",
        )(self.section.reshape(1), self.kept, self.mate, *extra)


def pack_vectors(vectors, qv_bias, fc_bias):
    half = vectors[0].shape[0]
    more = fc_bias.shape[0] // half

    def kernel(*refs):
        out = refs[-1]
        out[...] = jnp.zeros_like(out)
        for i in range(len(vectors)):
            out[i : i + 1, :] = refs[i][...].astype(F32)
        out[6:8, :] = refs[-3][...].astype(F32)
        for i in range(more):
            out[8 + i : 9 + i, :] = refs[-2][:, i * half : (i + 1) * half].astype(F32)

    return pl.pallas_call(
        kernel,
        out_shape=jax.ShapeDtypeStruct((16, half), F32),
        compiler_params=params(SMALL),
        cost_estimate=lasts(1),
        name="pack_vectors",
    )(*[v.reshape(1, half) for v in vectors], qv_bias, fc_bias.reshape(1, -1))


def unpack_vectors(tensor, mine, other):
    half = mine.shape[1]

    def kernel(which, a, b, vec, bqv0, bqv1, bfc0, bfc1):
        for value in range(2):

            @pl.when(which[0] == value)
            def _():
                order = (a, b) if value == 0 else (b, a)
                vec[:, :half] = order[0][0:8, :]
                vec[:, half:] = order[1][0:8, :]

        for ref, bqv, bfc in ((a, bqv0, bfc0), (b, bqv1, bfc1)):
            bqv[...] = ref[6:8, :]
            for i in range(4):
                bfc[:, i * half : (i + 1) * half] = ref[8 + i : 9 + i, :]

    shape = lambda *s: jax.ShapeDtypeStruct(s, F32)
    pair = [shape(2, half)] * 2 + [shape(1, 4 * half)] * 2
    return pl.pallas_call(
        kernel,
        in_specs=[pl.BlockSpec(memory_space=pltpu.SMEM)]
        + [pl.BlockSpec(memory_space=pltpu.VMEM)] * 2,
        out_shape=[shape(8, 2 * half)] + pair,
        compiler_params=params(SMALL),
        cost_estimate=lasts(1),
        name="unpack_vectors",
    )(tensor.reshape(1), mine, other)


def assemble(where, own, arrived, mate):
    count = arrived.shape[0] // 3
    half = own.shape[1]

    def kernel(which, own_ref, arrived_ref, mate_ref, out, mine):
        for section in range(2):
            for tensor in range(2):

                @pl.when((which[0] == section) & (which[2] == tensor))
                def _():
                    here = slice(tensor * half, (tensor + 1) * half)
                    there = slice((1 - tensor) * half, (2 - tensor) * half)
                    out[2 * count :, here] = own_ref[...]
                    for place in range(2):
                        ref = arrived_ref if place == section else mate_ref
                        rows = slice(place * count, (place + 1) * count)
                        later = slice((2 + place) * count, (3 + place) * count)
                        out[later, there] = ref[:count, :]
                        out[rows, here] = ref[count : 2 * count, :]
                        out[rows, there] = ref[2 * count :, :]
                    rows = slice((2 + section) * count, (3 + section) * count)
                    mine[...] = out[rows, :]

    return pl.pallas_call(
        kernel,
        in_specs=[pl.BlockSpec(memory_space=pltpu.SMEM)]
        + [pl.BlockSpec(memory_space=pltpu.VMEM)] * 3,
        out_shape=[
            jax.ShapeDtypeStruct((4 * count, 2 * half), BF16),
            jax.ShapeDtypeStruct((count, 2 * half), BF16),
        ],
        compiler_params=params(SMALL),
        cost_estimate=lasts(1),
        name="assemble",
    )(where, own, arrived, mate)


def gather_rows(own):
    section = lax.axis_index(SECTION)
    mate = swap(own, SECTION)
    prior_mine = shift(own, 1)
    prior_mate = swap(prior_mine, SECTION)
    first = section == 0
    pick = lambda a, b: [jnp.where(first, a, b), jnp.where(first, b, a)]
    return jnp.concatenate(pick(prior_mine, prior_mate) + pick(own, mate), axis=0)


def local(
    inputs,
    out_grads,
    seq_blocks,
    ln1_gain,
    ln1_shift,
    qkv_weight,
    qv_bias,
    out_weight,
    out_bias,
    ln2_gain,
    ln2_shift,
    fc_weight,
    fc_bias,
    proj_weight,
    proj_bias,
):
    section = lax.axis_index(SECTION)
    position = lax.axis_index("dp")
    tensor = lax.axis_index(TENSOR)
    half = D // 2
    block = inputs.shape[1]
    count = block // 2
    hidden = fc_weight.shape[1]
    first = tensor == 0

    def features(mine, other):
        return ordered(first, mine, other, mine.ndim - 1)

    micro = lambda a, which: lax.dynamic_index_in_dim(a, which, 0, keepdims=False)
    starts = jnp.cumsum(seq_blocks, axis=1) - seq_blocks
    continuing = jnp.logical_not(jnp.any(starts == position, axis=1))
    continues = micro(continuing, tensor)
    where = jnp.stack([section, continues.astype(jnp.int32), tensor])

    own_rows = lambda a, which: part(micro(a, which), section, 2)
    here, there = own_rows(inputs, tensor), own_rows(inputs, 1 - tensor)
    count_dp = lax.axis_size("dp")
    ahead = [(2 * i + j, 2 * i + 2 + 1 - j) for i in range(count_dp - 1) for j in range(2)]
    across = swap(there, TENSOR)
    before_here = shift(here, 1)
    before_there = lax.ppermute(there, ("dp", TENSOR), ahead)
    arrived = jnp.concatenate([across, before_here, before_there], axis=0)
    mate = swap(arrived, SECTION)
    rows_one, mine = assemble(where, micro(inputs, tensor), arrived, mate)
    vectors = pack_vectors(
        [ln1_gain, ln1_shift, out_bias, ln2_gain, ln2_shift, proj_bias], qv_bias, fc_bias
    )
    vec, *biases = unpack_vectors(tensor, vectors, swap(vectors, TENSOR))
    qkv_weight = jnp.concatenate([qkv_weight[:, n] for n in range(3)], axis=0)
    fetch_qkv, fetch_out = Fetch(qkv_weight, 1), Fetch(out_weight, 1)
    fetch_fc, fetch_proj = Fetch(fc_weight, 2), Fetch(proj_weight, 2)
    weights = [
        dict(wqkv=qkv_weight, wo=out_weight, wfc=fc_weight, wp=proj_weight),
        {},
    ]
    for half_index in range(2):
        weights[half_index].update(bqv=biases[half_index], bfc=biases[2 + half_index])
    dep = fetch_qkv.start(across)
    dep = fetch_out.start(dep)
    dep = fetch_fc.start(dep)
    one = forward_part(where, vec, weights, (0,), (), rows=rows_one, dep=dep)
    dep = fetch_proj.start(one["sum"])
    dep = fetch_qkv.join(dep)
    dep = fetch_out.join(dep)
    dep = fetch_qkv.finish(dep)
    dep = fetch_out.finish(dep)
    dep = fetch_fc.join(dep)
    weights[1].update(wqkv=fetch_qkv.whole, wo=fetch_out.whole)
    one_b = forward_part(
        where, vec, weights, (1,), (0,), nrm=one["nrm"], carried=one["sum"], dep=dep
    )
    dep = fetch_proj.join(one_b["sum"])
    dep = fetch_fc.finish(dep)
    dep = fetch_proj.finish(dep)
    weights[1].update(wfc=fetch_fc.whole, wp=fetch_proj.whole)
    one_c = forward_part(
        where, vec, weights, (), (1,), nrm2=one_b["nrm2"], carried=one_b["sum"], dep=dep
    )
    one = {**one, **one_b, **one_c}
    dout = features(own_rows(out_grads, tensor), swap(own_rows(out_grads, 1 - tensor), TENSOR))
    two = last_layer(where, vec, weights, gather_rows(one["act"]), dout)
    norm_two = NormBack(one["act"], vec, two, two["dh1"])
    dep = norm_two.send(two["prior"])
    layers = [[two, two, two, dout], [one, None, None, None]]
    flat = lambda s, piece: (0, 0)
    by_piece = lambda s, piece: (0, piece)
    own_piece = lambda s, piece: (2 + s, piece)
    square, tall, narrow, thin = (count, D), (4 * count, half), (count, half), (4 * count, half)

    def proj_terms(i):
        return [[(f[f"u{i}"], square, by_piece, g, square, flat) for f, _, _, g in layers]]

    def fc_terms(i):
        return [
            [(f["nrm2"], square, flat, m[f"df{i}"], square, by_piece) for f, m, _, _ in layers]
        ]

    def attn_terms(i):
        return [
            [(f["nrm"], narrow, own_piece, a[f"dq{i}"], narrow, flat) for f, _, a, _ in layers if a],
            [(f["nrm"], tall, by_piece, a[f"dk{i}"], thin, flat) for f, _, a, _ in layers if a],
            [(f["nrm"], tall, by_piece, a[f"dv{i}"], thin, flat) for f, _, a, _ in layers if a],
            [(f[f"o{i}"], narrow, flat, m["ga"], narrow, by_piece) for f, m, a, _ in layers if a],
        ]

    proj, fc = Reduction(where, proj_terms), Reduction(where, fc_terms)
    attn = Reduction(where, attn_terms, True)
    dep = attn.first_layer(dep)
    low_two, small_two = norm_two.finish(dep)
    layers[1][3] = low_two
    dep = proj.theirs_foreign(low_two)
    dep = proj.theirs_own(dep)
    dep = proj.foreign(dep)
    mlp_one = layers[1][1] = backward_mlp(vec, weights, one, low_two, where, dep)
    dep = proj.own(mlp_one["ga"])
    dep = fc.theirs_foreign(dep)
    dep = fc.theirs_own(dep)
    dep = fc.foreign(dep)
    dep = fc.own(dep)
    dep = proj.split(dep)
    attn_one = layers[1][2] = backward_attn(where, weights, one, mlp_one["ga"], dep)
    norm_one = NormBack(mine, vec, attn_one, mlp_one["dh1"])
    sums = grads = None
    low_one, small_one = None, None
    levels = 0
    while 2 ** (levels + 1) < count_dp:
        levels += 1
    dep = attn.theirs_foreign(attn_one["own"])
    dep = attn.theirs_own(dep)
    dep = proj.split(dep)
    dep = attn.foreign(dep)
    dep = fc.split(dep)
    dep = norm_one.send(dep)
    for level in range(1, levels):
        dep = proj.split(dep)
    dep = attn.own(dep)
    dep = proj.sum(dep)
    dep = fc.split(dep)
    low_one, small_one = norm_one.finish(dep)
    norms, mlps, attns = (small_one, small_two), (mlp_one, two), (attn_one, two)
    dep = gather_small(where, norms, mlps, attns, low_one)
    sums = SmallSum(dep)
    for level in range(1, levels):
        dep = proj.join(dep)
    dep = attn.split(dep)
    dep = sums.step(dep)
    for level in range(1, levels):
        dep = fc.split(dep)
        dep = sums.step(dep)
    dep = attn.split(dep)
    dep = fc.sum(dep)
    dep = proj.join(dep)
    for level in range(1, levels):
        dep = attn.split(dep)
        dep = fc.join(dep)
        dep = sums.step(dep)
    dep = attn.sum(dep)
    dep = fc.join(dep)
    dep = proj.join(dep)
    dep = sums.step(dep)
    dep = attn.join(dep)
    acts, grads = Spread(section, tensor), Spread(section, tensor)
    dep = acts.add([one["act"], two["act"]], dep)
    dep = grads.add([low_one, low_two], dep)
    row_steps = 2
    take = lambda i, size: slice(i * size, (i + 1) * size)

    def place_proj(core):
        size = hidden // 2 // row_steps
        return [
            (take(i, size), (take(core * row_steps + i, size), slice(0, D)))
            for i in range(row_steps)
        ]

    def place_fc(core):
        size = D // row_steps
        return [(take(i, size), (take(i, size), take(core, D))) for i in range(row_steps)]

    def place_out(core):
        return [(take(3, half), (slice(0, half), take(core, half)))]

    proj_grad, dep = widen(section, proj.kept, proj.other, (hidden, D), place_proj, dep)
    for level in range(1, levels):
        dep = attn.join(dep)
    dep = sums.step(dep)
    dep = fc.join(dep)
    dep = acts.turn(dep)
    dep = grads.turn(dep)
    fc_grad, dep = widen(section, fc.kept, fc.other, (D, hidden), place_fc, dep)
    dep = acts_out = acts.finish(BF16, dep)
    dep = grads_out = grads.finish(F32, dep)
    dep = attn.join(dep)

    while sums.other is not None:
        dep = sums.step(dep)
    out_grad, _ = widen(section, attn.kept, attn.other, (half, D), place_out, dep)
    assert proj.bit == fc.bit == attn.bit == 0
    sides = lambda n: [a[n * half : (n + 1) * half] for a in (attn.kept, attn.other)]
    qkv_grad = jnp.stack([ordered(section == 0, *sides(n), 0) for n in range(3)], axis=1)
    qkv_grad = qkv_grad.astype(F32)
    rows_here = part(sums.array[:8], tensor, 2, 1)
    bfc_grad = part(sums.array[8:12], tensor, 2).reshape(hidden)
    return (
        acts_out[None],
        grads_out[None],
        rows_here[0],
        rows_here[1],
        qkv_grad,
        rows_here[6:8],
        out_grad,
        rows_here[4],
        rows_here[2],
        rows_here[3],
        fc_grad,
        bfc_grad,
        proj_grad,
        rows_here[5],
    )


def solution(mesh):
    in_specs = (
        P(None, "dp", TENSOR),
        P(None, "dp", TENSOR),
        P(),
        P(TENSOR),
        P(TENSOR),
        P(None, None, TENSOR),
        P(None, TENSOR),
        P(TENSOR, None),
        P(TENSOR),
        P(TENSOR),
        P(TENSOR),
        P(None, TENSOR),
        P(TENSOR),
        P(TENSOR, None),
        P(TENSOR),
    )
    out_specs = (
        P(SECTION, None, "dp", TENSOR),
        P(SECTION, None, "dp", TENSOR),
        P(TENSOR),
        P(TENSOR),
        P(None, None, TENSOR),
        P(None, TENSOR),
        P(TENSOR, None),
        P(TENSOR),
        P(TENSOR),
        P(TENSOR),
        P(None, TENSOR),
        P(TENSOR),
        P(TENSOR, None),
        P(TENSOR),
    )
    return jax.shard_map(local, mesh=mesh, in_specs=in_specs, out_specs=out_specs, check_vma=False)
```

```python
import math

import jax
import jax.numpy as jnp
from jax import lax
from jax.experimental import pallas as pl
from jax.experimental.pallas import tpu as pltpu
from jax.sharding import PartitionSpec as P

SECTION, TENSOR = "section", "tensor"
D = 768
HEAD = 64
NORM_EPSILON = 1e-05
MASKED = -1e30
SCALE = HEAD ** (-0.5)
F32 = jnp.float32
BF16 = jnp.bfloat16
LIMIT = 60 * 1024 * 1024
SMALL = 12 * 1024 * 1024
SPARE = 12 * 1024 * 1024


def dot(a, b, dims=((1,), (0,))):
    return lax.dot_general(a, b, (dims, ((), ())), preferred_element_type=F32)


def swap(array, axis):
    return lax.ppermute(array, axis, [(0, 1), (1, 0)])


def shift(array, by):
    count = lax.axis_size("dp")
    pairs = [(i, i + by) for i in range(count) if 0 <= i + by < count]
    return lax.ppermute(array, "dp", pairs)


def exchange(array, bit):
    count = lax.axis_size("dp")
    return lax.ppermute(array, "dp", [(i, i ^ bit) for i in range(count)])


def part(array, which, parts, axis=0):
    size = array.shape[axis] // parts
    return lax.dynamic_slice_in_dim(array, which * size, size, axis)


def ordered(first, mine, other, axis):
    return jnp.concatenate(
        [jnp.where(first, mine, other), jnp.where(first, other, mine)], axis=axis
    )


def add_low(a, b):
    return (a.astype(F32) + b.astype(F32)).astype(BF16)


def lasts(microseconds):
    return pl.CostEstimate(flops=int(microseconds * 2e7), bytes_accessed=1, transcendentals=0)


def params(limit):
    return pltpu.CompilerParams(vmem_limit_bytes=limit)


def after(dep):
    deps = [] if dep is None else list(dep) if isinstance(dep, (list, tuple)) else [dep]
    return deps, [pl.BlockSpec(memory_space=pl.ANY)] * len(deps)


def sum_split(sets, side, dep=None):
    halves = [arrays[0].shape[0] // 2 for arrays in sets]
    if any(rows % 16 for rows in halves):
        totals = [sum(a.astype(F32) for a in arrays).astype(BF16) for arrays in sets]
        pick = lambda which: jnp.concatenate([part(t, which, 2) for t in totals], axis=0)
        return pick(side), pick(1 - side)
    width = sets[0][0].shape[1]
    extra, extra_specs = after(dep)
    operands, specs = [], []
    for arrays, rows in zip(sets, halves):
        for array in arrays:
            operands += [array, array]
            specs.append(pl.BlockSpec((rows, width), lambda j, which: (which[0], 0)))
            specs.append(pl.BlockSpec((rows, width), lambda j, which: (1 - which[0], 0)))

    def kernel(which, *refs):
        at, row = 0, 0
        for arrays, rows in zip(sets, halves):
            for out, first in ((refs[-2], at), (refs[-1], at + 1)):
                total = refs[first][...].astype(F32)
                for i in range(1, len(arrays)):
                    total += refs[first + 2 * i][...].astype(F32)
                out[row : row + rows, :] = total.astype(BF16)
            at, row = at + 2 * len(arrays), row + rows

    block = (sum(halves), width)
    flat = pl.BlockSpec(block, lambda j, which: (0, 0))
    return pl.pallas_call(
        kernel,
        grid_spec=pltpu.PrefetchScalarGridSpec(
            num_scalar_prefetch=1,
            grid=(1,),
            in_specs=specs + extra_specs,
            out_specs=[flat] * 2,
        ),
        out_shape=[jax.ShapeDtypeStruct(block, BF16)] * 2,
        compiler_params=params(SMALL),
        cost_estimate=lasts(1.2),
        name="sum_split",
    )(side.reshape(1), *operands, *extra)


def sum_rows(arrays, dep=None):
    rows, width = arrays[0].shape
    kind = arrays[0].dtype
    if rows % 16:
        return add_low(*arrays)
    extra, extra_specs = after(dep)

    def kernel(a, b, *rest):
        rest[-1][...] = (a[...].astype(F32) + b[...].astype(F32)).astype(kind)

    return pl.pallas_call(
        kernel,
        in_specs=[pl.BlockSpec(memory_space=pltpu.VMEM)] * 2 + extra_specs,
        out_shape=jax.ShapeDtypeStruct((rows, width), kind),
        compiler_params=params(SMALL),
        cost_estimate=lasts(0.7),
        name="sum_rows",
    )(*arrays, *extra)


def put_rows(side, mine, other, dep=None):
    rows, width = mine.shape
    if rows % 16:
        return ordered(side == 0, mine, other, 0)
    extra, extra_specs = after(dep)

    def kernel(which, a, b, *rest):
        out = rest[-1]
        out[pl.ds(pl.multiple_of(which[0] * rows, rows), rows), :] = a[...]
        out[pl.ds(pl.multiple_of((1 - which[0]) * rows, rows), rows), :] = b[...]

    return pl.pallas_call(
        kernel,
        in_specs=[pl.BlockSpec(memory_space=pltpu.SMEM)]
        + [pl.BlockSpec(memory_space=pltpu.VMEM)] * 2
        + extra_specs,
        out_shape=jax.ShapeDtypeStruct((2 * rows, width), BF16),
        compiler_params=params(SMALL),
        cost_estimate=lasts(0.7),
        name="put_rows",
    )(side.reshape(1), mine, other, *extra)


def gradient(where, terms, which, added=(), dep=None, cuts=1):
    arrays, specs, plan = [], [], []
    for term in terms:
        plan.append(len(term))
        for a, a_block, a_index, b, b_block, b_index in term:
            for array, block, index in ((a, a_block, a_index), (b, b_block, b_index)):
                arrays.append(array)
                specs.append(
                    pl.BlockSpec(block, lambda j, w, index=index: index(w[0], w[0] ^ which))
                )
    rows, width = terms[0][0][1][1], terms[0][0][4][1]
    total = rows * len(terms)
    last = len(arrays)
    for pieces in added:
        for array in pieces:
            arrays.append(array)
            specs.append(pl.BlockSpec(array.shape, lambda j, w: (0, 0)))
    extra, extra_specs = after(dep)

    def kernel(w, *refs):
        outs, at = refs[len(refs) - cuts :], 0
        for i, layers in enumerate(plan):
            value = None
            for _ in range(layers):
                one = dot(refs[at][...], refs[at + 1][...], ((0,), (0,)))
                value = one if value is None else value + one
                at += 2
            span = slice(i * rows, (i + 1) * rows)
            place = last
            for pieces in added:
                each = total // len(pieces)
                taken = []
                for cut in range(len(pieces)):
                    low, high = max(span.start, cut * each), min(span.stop, (cut + 1) * each)
                    if low < high:
                        taken.append(refs[place + cut][low - cut * each : high - cut * each, :])
                value += jnp.concatenate([t.astype(F32) for t in taken], axis=0)
                place += len(pieces)
            each = total // cuts
            for cut in range(cuts):
                low, high = max(span.start, cut * each), min(span.stop, (cut + 1) * each)
                if low < high:
                    taken = value[low - span.start : high - span.start, :]
                    outs[cut][low - cut * each : high - cut * each, :] = taken.astype(BF16)

    outs = pl.pallas_call(
        kernel,
        grid_spec=pltpu.PrefetchScalarGridSpec(
            num_scalar_prefetch=1,
            grid=(1,),
            in_specs=specs + extra_specs,
            out_specs=[pl.BlockSpec((total // cuts, width), lambda j, w: (0, 0))] * cuts,
        ),
        out_shape=[jax.ShapeDtypeStruct((total // cuts, width), BF16)] * cuts,
        compiler_params=params(SMALL),
        cost_estimate=lasts(1 + sum(plan) * 0.35),
        name="gradient",
    )(where, *arrays, *extra)
    return outs[0] if cuts == 1 else outs


class Reduction:
    def __init__(self, where, terms_of, early=False):
        self.where, self.terms_of = where, terms_of
        self.bit = 1
        self.early = early
        self.partial = {}

    def first_layer(self, dep):
        for half in (1, 0):
            for which in (1, 0):
                terms = [term[:1] for term in self.terms_of(half)]
                dep = self.partial[half, which] = gradient(self.where, terms, which, dep=dep)
        return dep

    def piece(self, half, which, mate, dep, cuts=1):
        terms, added = self.terms_of(half), [] if mate is None else [mate]
        added = [a if isinstance(a, list) else [a] for a in added]
        if self.early:
            terms = [term[1:] for term in terms]
            added.append([self.partial[half, which]])
        return gradient(self.where, terms, which, added, dep, cuts)

    def theirs_foreign(self, dep):
        theirs = self.piece(1, 1, None, dep, 2)
        self.mate_foreign = [swap(cut, SECTION) for cut in theirs]
        return theirs[0]

    def theirs_own(self, dep):
        theirs = self.piece(0, 1, None, dep, 2)
        self.mate_own = [swap(cut, SECTION) for cut in theirs]
        return theirs[0]

    def foreign(self, dep):
        foreign = self.piece(1, 0, self.mate_foreign, dep)
        self.across = swap(foreign, TENSOR)
        return foreign

    def own(self, dep):
        own = self.piece(0, 0, self.mate_own, dep)
        self.arrays = [own, self.across]
        return own

    def side(self):
        return (lax.axis_index("dp") // self.bit) % 2

    def split(self, dep, other=None):
        sets = [self.arrays] if other is None else [self.arrays, other.arrays]
        kept, sent = sum_split(sets, self.side(), dep)
        self.arrays = [kept, exchange(sent, self.bit)]
        self.bit *= 2
        return kept

    def sum(self, dep):
        self.kept = sum_rows(self.arrays, dep)
        self.send_back()
        return self.kept

    def send_back(self):
        self.bit //= 2
        self.other = swap(self.kept, SECTION) if self.bit == 0 else exchange(self.kept, self.bit)

    def join(self, dep):
        self.kept = put_rows(self.side(), self.kept, self.other, dep)
        self.send_back()
        return self.kept


class SmallSum:
    def __init__(self, array):
        bits = []
        while 2 ** len(bits) < lax.axis_size("dp"):
            bits.append(2 ** len(bits))
        self.moves = [lambda a: swap(a, SECTION), lambda a: swap(a, TENSOR)]
        self.moves += [lambda a, bit=bit: exchange(a, bit) for bit in bits]
        self.array = array
        self.other = self.moves.pop(0)(array)

    def step(self, dep):
        if self.other is None:
            return dep
        self.array = sum_rows([self.array, self.other], dep)
        self.other = self.moves.pop(0)(self.array) if self.moves else None
        return self.array


def widen(section, kept, other, shape, place, dep):
    extra, extra_specs = after(dep)
    plan = [place(core) for core in range(2)]
    steps = len(plan[0])

    def kernel(which, a, b, *rest):
        out, token, held, sems = rest[-4:]
        token[...] = jnp.zeros_like(token)
        for value in range(2):

            @pl.when(which[0] == value)
            def _():
                copies = []
                for core, ref in ((value, a), (1 - value, b)):
                    for step, (rows, block) in enumerate(plan[core]):
                        held[block] = ref[rows, :].astype(F32)
                        copy = pltpu.make_async_copy(
                            held.at[block], out.at[block], sems.at[core * steps + step]
                        )
                        copy.start()
                        copies.append(copy)
                for copy in copies:
                    copy.wait()

    return pl.pallas_call(
        kernel,
        in_specs=[pl.BlockSpec(memory_space=pltpu.SMEM)]
        + [pl.BlockSpec(memory_space=pltpu.VMEM)] * 2
        + extra_specs,
        out_specs=[pl.BlockSpec(memory_space=pltpu.HBM), pl.BlockSpec(memory_space=pltpu.VMEM)],
        out_shape=[jax.ShapeDtypeStruct(shape, F32), jax.ShapeDtypeStruct((8, 128), F32)],
        scratch_shapes=[pltpu.VMEM(shape, F32), pltpu.SemaphoreType.DMA((2 * steps,))],
        compiler_params=params(SMALL),
        cost_estimate=lasts(2),
        name="widen",
    )(section.reshape(1), kept, other, *extra)


def take_rows(array, which, parts, dep):
    rows, width = array.shape[0] // parts, array.shape[1]
    extra, extra_specs = after(dep)

    def kernel(w, a, *rest):
        out, sem = rest[-2:]
        span = pl.ds(pl.multiple_of(w[0] * rows, rows), rows)
        copy = pltpu.make_async_copy(a.at[span, :], out, sem)
        copy.start()
        copy.wait()

    return pl.pallas_call(
        kernel,
        in_specs=[pl.BlockSpec(memory_space=pltpu.SMEM), pl.BlockSpec(memory_space=pl.ANY)]
        + extra_specs,
        out_specs=pl.BlockSpec(memory_space=pltpu.VMEM),
        out_shape=jax.ShapeDtypeStruct((rows, width), array.dtype),
        scratch_shapes=[pltpu.SemaphoreType.DMA(())],
        compiler_params=params(SMALL),
        cost_estimate=lasts(0.7),
        name="take_rows",
    )(which.reshape(1), array, *extra)


class Fetch:
    def __init__(self, array, bit, cuts=1):
        self.array, self.bit, self.cuts = array, bit, cuts
        self.section = lax.axis_index(SECTION)
        self.side = (lax.axis_index("dp") // bit) % 2

    def start(self, dep):
        piece = take_rows(self.array, self.section * 2 + self.side, 4, dep)
        self.mine = swap(piece, TENSOR)
        return piece

    def pass_on(self, dep=None):
        if dep is not None:
            self.mine = take_rows(self.mine, jnp.int32(0), 1, dep)
        self.other = exchange(self.mine, self.bit)
        return self.mine

    def join(self, dep):
        mine, other = self.mine, self.other
        dep = other = take_rows(other, jnp.int32(0), 1, dep)
        rows = mine.shape[0] // self.cuts
        cut = lambda a: [a[i * rows : (i + 1) * rows] for i in range(self.cuts)]
        self.parts = [mine, other] + [swap(a, SECTION) for a in cut(mine) + cut(other)]
        return dep

    def finish(self, dep):
        self.whole = put_parts(self.section, self.side, self.parts, dep)
        return self.whole


def put_parts(section, side, parts, dep):
    rows, width = parts[0].shape
    cuts = (len(parts) - 2) // 2
    extra, extra_specs = after(dep)

    def kernel(which, *refs):
        out = refs[-1]

        def put(ref, core, half, piece):
            size = ref.shape[0]
            start = pl.multiple_of((2 * core + half) * rows, rows) + piece * size
            out[pl.ds(pl.multiple_of(start, 16), size), :] = ref[...]

        put(refs[0], which[0], which[1], 0)
        put(refs[1], which[0], 1 - which[1], 0)
        for i in range(cuts):
            put(refs[2 + i], 1 - which[0], which[1], i)
            put(refs[2 + cuts + i], 1 - which[0], 1 - which[1], i)

    return pl.pallas_call(
        kernel,
        in_specs=[pl.BlockSpec(memory_space=pltpu.SMEM)]
        + [pl.BlockSpec(memory_space=pltpu.VMEM)] * len(parts)
        + extra_specs,
        out_shape=jax.ShapeDtypeStruct((4 * rows, width), parts[0].dtype),
        compiler_params=params(SMALL),
        cost_estimate=lasts(1),
        name="put_parts",
    )(jnp.stack([section, side]), *parts, *extra)


def standard(rows):
    center = jnp.sum(rows, axis=1, keepdims=True) / D
    spread = jnp.sum(rows * rows, axis=1, keepdims=True) / D - center * center
    factor = lax.rsqrt(spread + NORM_EPSILON)
    return (rows - center) * factor, factor


def norm(rows, gain, shift_by):
    return (standard(rows)[0] * gain + shift_by).astype(BF16)


def norm_back(grad, normed, factor, gain):
    scaled = grad * gain
    mean = jnp.sum(scaled, axis=1, keepdims=True) / D
    along = jnp.sum(scaled * normed, axis=1, keepdims=True) / D
    return factor * (scaled - mean - normed * along)


def total_rows(array):
    return jnp.sum(array.astype(F32), axis=0, keepdims=True)


def only_head(array, which):
    lane = lax.broadcasted_iota(jnp.int32, array.shape, 1)
    return jnp.where((lane >= HEAD) == (which == 1), array, jnp.zeros_like(array))


GELU_A = 0.7978845608028654
GELU_B = 0.044715
PAIR = 2 * HEAD
CHUNK = 768


class Call:
    def __init__(self):
        self.names, self.arrays, self.out_names, self.out_shape, self.scratch = [], [], [], [], []

    def take(self, name, array):
        self.names.append(name)
        self.arrays.append(array)

    def give(self, name, shape, dtype):
        self.out_names.append(name)
        self.out_shape.append(jax.ShapeDtypeStruct(shape, dtype))

    def keep(self, name, shape, dtype):
        self.scratch.append((name, pltpu.VMEM(shape, dtype)))

    def run(self, body, flags, name, time, dep=None):
        extra, extra_specs = after(dep)
        taken, given = len(self.names), len(self.out_names)
        memory = [pltpu.VMEM(a.shape, a.dtype) for a in self.arrays]
        memory += [pltpu.VMEM(o.shape, o.dtype) for o in self.out_shape]
        memory += [shape for _, shape in self.scratch]
        size = sum(math.prod(m.shape) * jnp.dtype(m.dtype).itemsize for m in memory)
        memory.append(pltpu.SemaphoreType.DMA((taken + given,)))

        def kernel(flags_ref, *refs):
            far = list(refs[:taken]) + list(refs[taken + len(extra) : taken + len(extra) + given])
            near = refs[taken + len(extra) + given :]
            names = self.names + self.out_names + [n for n, _ in self.scratch]
            held = dict(zip(names, near[: len(names)]))
            sems = near[-1]
            copies = {}
            for i, key in enumerate(self.names):
                copies[key] = pltpu.make_async_copy(far[i], held[key], sems.at[i])
                copies[key].start()
            waiting = dict(copies)
            leaving = []

            def get(key):
                if key in waiting:
                    waiting.pop(key).wait()
                return held[key]

            def send(*keys):
                for key in keys:
                    if key not in self.out_names:
                        continue
                    i = taken + self.out_names.index(key)
                    copy = pltpu.make_async_copy(held[key], far[i], sems.at[i])
                    copy.start()
                    leaving.append(copy)

            body(flags_ref, get, send)
            for key in list(waiting):
                waiting.pop(key).wait()
            for copy in leaving:
                copy.wait()

        anywhere = pl.BlockSpec(memory_space=pltpu.HBM)
        outs = pl.pallas_call(
            kernel,
            in_specs=[pl.BlockSpec(memory_space=pltpu.SMEM)] + [anywhere] * taken + extra_specs,
            out_specs=[anywhere] * given,
            out_shape=self.out_shape,
            scratch_shapes=memory,
            compiler_params=params(min(size + SPARE, LIMIT)),
            cost_estimate=lasts(time),
            name=name,
        )(flags, *self.arrays, *extra)
        return dict(zip(self.out_names, outs))


def out_part(weights):
    width = weights.shape[1]
    return jnp.concatenate([weights[3 * D : 3 * D + width, :], weights[3 * D + width :, :]], axis=1)


def each_pair(count, body):
    for i in range(count):
        body(slice(i * PAIR, (i + 1) * PAIR), i)


def forward_part(
    where, vec, weights, attn, mlp, rows=None, nrm=None, nrm2=None, carried=None, dep=None
):
    c = Call()
    c.take("vec", vec)
    if rows is not None:
        c.take("rows", rows)
    if nrm is not None:
        c.take("nrm", nrm)
    if carried is not None:
        c.take("carried", carried)
    if nrm2 is not None:
        c.take("nrm2", nrm2)
    full = rows if rows is not None else nrm
    count = carried.shape[0] if full is None else full.shape[0] // 4
    width = weights[0]["wqkv"].shape[1]
    hidden = weights[0]["wp"].shape[0]
    for half in attn:
        for name in ("bqv", "wqkv"):
            c.take(f"{name}{half}", weights[half][name])
    for half in mlp:
        for name in ("bfc", "wfc", "wp"):
            c.take(f"{name}{half}", weights[half][name])
    if rows is not None:
        c.give("nrm", (4 * count, D), BF16)
    for half in attn:
        for name, n, kind in (
            ("q", count, BF16), ("k", 4 * count, BF16), ("v", 4 * count, BF16),
            ("o", count, BF16), ("of", count, F32), ("rl", count, F32),
        ):
            c.give(f"{name}{half}", (n, width), kind)
        c.give(f"p{half}", (2 * width // PAIR, count, 4 * count), BF16)
    middle = bool(attn) and bool(mlp)
    if middle:
        c.give("h1", (count, D), F32)
        c.give("nrm2", (count, D), BF16)
    for half in mlp:
        c.give(f"f{half}", (count, hidden), F32)
        c.give(f"u{half}", (count, hidden), BF16)
    final = 1 in mlp
    if final:
        c.give("act", (count, D), BF16)
        c.keep("sum", (count, D), F32)
    else:
        c.give("sum", (count, D), F32)
    if attn:
        c.keep("mask", (count, 4 * count), F32)

    body = forward_body(attn, mlp, count, width, hidden, rows is not None)
    return c.run(body, where, "forward", 12 * len(attn) + 3 * len(mlp), dep)


def forward_body(attn, mlp, count, width, hidden, first):
    def body(flags, get, send):
        total = get("sum")
        vec = get("vec")
        span = pl.ds(pl.multiple_of(2 * count + flags[0] * count, count), count)
        if first:
            rows_ref = get("rows")
            get("nrm")[...] = norm(rows_ref[...].astype(F32), vec[0:1, :], vec[1:2, :])
            total[...] = rows_ref[span, :].astype(F32) + vec[2:3, :]
            send("nrm")
        else:
            total[...] = get("carried")[...]
        if attn:
            mask = get("mask")
            row = lax.broadcasted_iota(jnp.int32, mask.shape, 0) + flags[0] * count
            col = lax.broadcasted_iota(jnp.int32, mask.shape, 1)
            limit = jnp.where(col < 2 * count, flags[1] * (4 * count) - 1, row + 2 * count)
            mask[...] = jnp.where(col <= limit, 0.0, MASKED)
            nrm_ref = get("nrm")
        for half in attn:
            here = lambda name, half=half: get(f"{name}{half}")
            bqv, wqkv = here("bqv"), here("wqkv")

            def pair(lanes, i, here=here, bqv=bqv, wqkv=wqkv):
                wq, wk, wv = [wqkv[n * D : (n + 1) * D, lanes] for n in range(3)]
                q = (dot(nrm_ref[span, :], wq) + bqv[0:1, lanes]).astype(BF16)
                here("q")[:, lanes] = q
                kv = dot(nrm_ref[...], jnp.concatenate([wk, wv], axis=1))
                k = kv[:, :PAIR].astype(BF16)
                here("k")[:, lanes] = k
                v = (kv[:, PAIR:] + bqv[1:2, lanes]).astype(BF16)
                here("v")[:, lanes] = v
                scaled = q * jnp.asarray(SCALE, BF16)
                both = jnp.concatenate([only_head(scaled, 0), only_head(scaled, 1)], axis=0)
                scores = dot(both, k, ((1,), (1,)))
                lows, factors = [], []
                for which in range(2):
                    masked = scores[which * count : (which + 1) * count, :] + mask[...]
                    lifted = jnp.exp(masked - jnp.max(masked, axis=1, keepdims=True))
                    lows.append(lifted.astype(BF16))
                    here("p")[2 * i + which] = lows[which]
                    factors.append(1.0 / jnp.sum(lifted, axis=1, keepdims=True))
                sides = dot(jnp.concatenate(lows, axis=0), v)
                lane = lax.broadcasted_iota(jnp.int32, q.shape, 1)
                factor = jnp.where(lane < HEAD, factors[0], factors[1])
                here("rl")[:, lanes] = factor
                o = jnp.where(lane < HEAD, sides[:count], sides[count:]) * factor
                here("of")[:, lanes] = o
                here("o")[:, lanes] = o.astype(BF16)

            each_pair(width // PAIR, pair)
            send(*[f"{name}{half}" for name in ("q", "k", "v", "p", "o", "of", "rl")])
            total[...] += dot(here("o")[...], out_part(wqkv))
        if attn and mlp:
            get("h1")[...] = total[...]
            get("nrm2")[...] = norm(total[...], vec[3:4, :], vec[4:5, :])
            total[...] += vec[5:6, :]
            send("h1", "nrm2")
        for half in mlp:
            here = lambda name, half=half: get(f"{name}{half}")
            wfc, bfc = here("wfc"), here("bfc")
            for i in range(hidden // CHUNK):
                lanes = slice(i * CHUNK, (i + 1) * CHUNK)
                pre = dot(get("nrm2")[...], wfc[:, lanes]) + bfc[:, lanes]
                here("f")[:, lanes] = pre
                inner = jnp.tanh(GELU_A * (pre + GELU_B * pre * pre * pre))
                hidden_low = (0.5 * pre * (1.0 + inner)).astype(BF16)
                here("u")[:, lanes] = hidden_low
                total[...] += dot(hidden_low, here("wp")[lanes, :])
            send(f"f{half}", f"u{half}")
        if 1 in mlp:
            get("act")[...] = total[...].astype(BF16)
            send("act")
        else:
            send("sum")

    return body


def backward_mlp(vec, weights, kept, dout, where, dep=None):
    c = Call()
    count = dout.shape[0]
    hidden = weights[0]["wp"].shape[0]
    c.take("dout", dout)
    for half in range(2):
        c.take(f"wp{half}", weights[half]["wp"])
        c.take(f"f{half}", kept[f"f{half}"])
        c.take(f"wfc{half}", weights[half]["wfc"])
    c.take("h1", kept["h1"])
    c.take("vec", vec)
    for half in range(2):
        c.give(f"df{half}", (count, hidden), BF16)
        c.give(f"gfc{half}", (1, hidden), F32)
    c.give("ga", (count, D), BF16)
    c.give("dh1", (count, D), F32)
    c.give("small", (8, D), F32)
    return c.run(mlp_body(hidden), where, "backward_mlp", 7, dep)


def mlp_body(hidden):
    def body(flags, get, send):
        dout = get("dout")
        back = None
        for half in range(2):
            wp, f, wfc = get(f"wp{half}"), get(f"f{half}"), get(f"wfc{half}")
            for i in range(hidden // CHUNK):
                lanes = slice(i * CHUNK, (i + 1) * CHUNK)
                du = dot(dout[...], wp[lanes, :], ((1,), (1,)))
                pre = f[:, lanes]
                square = pre * pre
                inner = jnp.tanh(GELU_A * (pre + GELU_B * square * pre))
                slope = 0.5 * (1.0 + inner) + (0.5 * GELU_A) * pre * (1.0 - inner * inner) * (
                    1.0 + 3.0 * GELU_B * square
                )
                low = (du * slope).astype(BF16)
                get(f"df{half}")[:, lanes] = low
                get(f"gfc{half}")[:, lanes] = total_rows(low)
                one = dot(low, wfc[:, lanes], ((1,), (1,)))
                back = one if back is None else back + one
            send(f"df{half}", f"gfc{half}")
        vec = get("vec")
        normed, factor = standard(get("h1")[...])
        grad = dout[...].astype(F32) + norm_back(back, normed, factor, vec[3:4, :])
        get("dh1")[...] = grad
        low = grad.astype(BF16)
        get("ga")[...] = low
        sums = [total_rows(x) for x in (back * normed, back, low, dout[...])]
        get("small")[...] = jnp.concatenate(sums + [jnp.zeros((4, D), F32)], axis=0)
        send("ga", "dh1", "small")

    return body


def backward_attn(where, weights, kept, ga, dep=None):
    c = Call()
    count = ga.shape[0]
    width = weights[0]["wqkv"].shape[1]
    c.take("ga", ga)
    for half in range(2):
        c.take(f"wqkv{half}", weights[half]["wqkv"])
        for name in ("rl", "of", "q", "v", "p", "k"):
            c.take(f"{name}{half}", kept[f"{name}{half}"])
    for half in range(2):
        for name, n in (("dq", count), ("dk", 4 * count), ("dv", 4 * count)):
            c.give(f"{name}{half}", (n, width), BF16)
        c.give(f"gqv{half}", (8, width), F32)
    c.give("sent", (2 * count, D), BF16)
    c.give("prior", (count, D), BF16)
    c.give("own", (count, D), F32)
    c.keep("dn", (4 * count, D), F32)
    return c.run(attn_body(count, width), where, "backward_attn", 15, dep)


def attn_body(count, width):
    def body(flags, get, send):
        dn = get("dn")
        span = pl.ds(pl.multiple_of(2 * count + flags[0] * count, count), count)
        ga = get("ga")
        for half in range(2):
            here = lambda name, half=half: get(f"{name}{half}")
            wqkv = here("wqkv")
            do_all = dot(ga[...], out_part(wqkv), ((1,), (1,)))
            refs = {name: here(name) for name in ("rl", "of", "q", "v", "p", "k")}

            def pair(lanes, i, here=here, do_all=do_all, refs=refs):
                by_head = lambda a: jnp.concatenate([only_head(a, 0), only_head(a, 1)], axis=0)
                do = (do_all[:, lanes] * refs["rl"][:, lanes]).astype(BF16)
                product = do.astype(F32) * refs["of"][:, lanes]
                center = jnp.sum(by_head(product), axis=1, keepdims=True)
                do_both = by_head(do)
                scaled_q = by_head(refs["q"][:, lanes] * jnp.asarray(SCALE, BF16))
                scaled_k = refs["k"][:, lanes] * jnp.asarray(SCALE, BF16)
                lifted = refs["p"][2 * i : 2 * i + 2].reshape(2 * count, 4 * count)
                dpw = dot(do_both, refs["v"][:, lanes], ((1,), (1,)))
                ds = (lifted.astype(F32) * (dpw - center)).astype(BF16)
                dq_both = dot(ds, scaled_k)
                lane = lax.broadcasted_iota(jnp.int32, do.shape, 1)
                dq = jnp.where(lane < HEAD, dq_both[:count], dq_both[count:]).astype(BF16)
                dk = dot(scaled_q, ds, ((0,), (0,))).astype(BF16).T
                dv = dot(do_both, lifted, ((0,), (0,))).astype(BF16).T
                here("dq")[:, lanes] = dq
                here("dk")[:, lanes] = dk
                here("dv")[:, lanes] = dv
                sums = [total_rows(dq), total_rows(dv), jnp.zeros((6, PAIR), F32)]
                here("gqv")[:, lanes] = jnp.concatenate(sums, axis=0)

            each_pair(width // PAIR, pair)
            send(*[f"{name}{half}" for name in ("dq", "dk", "dv", "gqv")])
            back = dot(here("dk")[...], wqkv[D : 2 * D, :], ((1,), (1,)))
            back += dot(here("dv")[...], wqkv[2 * D : 3 * D, :], ((1,), (1,)))
            if half == 0:
                dn[...] = back
            else:
                dn[...] += back
            dn[span, :] += dot(here("dq")[...], wqkv[:D, :], ((1,), (1,)))
        at = lambda base, which: pl.ds(pl.multiple_of(base + which * count, count), count)
        mine, other = flags[0], 1 - flags[0]
        get("sent")[:count, :] = dn[at(0, other), :].astype(BF16)
        get("sent")[count:, :] = dn[at(2 * count, other), :].astype(BF16)
        send("sent")
        get("prior")[...] = dn[at(0, mine), :].astype(BF16)
        get("own")[...] = dn[at(2 * count, mine), :]
        send("prior", "own")

    return body


def last_layer(where, vec, weights, rows, dout, dep=None):
    c = Call()
    count = rows.shape[0] // 4
    width = weights[0]["wqkv"].shape[1]
    hidden = weights[0]["wp"].shape[0]
    c.take("vec", vec)
    c.take("rows", rows)
    for name in ("bqv", "wqkv"):
        for half in range(2):
            c.take(f"{name}{half}", weights[half][name])
    for half in range(2):
        for name in ("bfc", "wfc", "wp"):
            c.take(f"{name}{half}", weights[half][name])
    c.take("dout", dout)
    c.give("nrm", (4 * count, D), BF16)
    c.give("nrm2", (count, D), BF16)
    c.give("act", (count, D), BF16)
    c.give("ga", (count, D), BF16)
    c.give("dh1", (count, D), F32)
    c.give("small", (8, D), F32)
    c.give("sent", (2 * count, D), BF16)
    c.give("prior", (count, D), BF16)
    c.give("own", (count, D), F32)
    for half in range(2):
        c.give(f"o{half}", (count, width), BF16)
        c.give(f"u{half}", (count, hidden), BF16)
        c.give(f"df{half}", (count, hidden), BF16)
        c.give(f"gfc{half}", (1, hidden), F32)
        for name, n in (("dq", count), ("dk", 4 * count), ("dv", 4 * count)):
            c.give(f"{name}{half}", (n, width), BF16)
        c.give(f"gqv{half}", (8, width), F32)
    for half in range(2):
        for name, n, kind in (
            ("q", count, BF16), ("k", 4 * count, BF16), ("v", 4 * count, BF16),
            ("of", count, F32), ("rl", count, F32),
        ):
            c.keep(f"{name}{half}", (n, width), kind)
        c.keep(f"p{half}", (2 * width // PAIR, count, 4 * count), BF16)
        c.keep(f"f{half}", (count, hidden), F32)
    c.keep("h1", (count, D), F32)
    c.keep("sum", (count, D), F32)
    c.keep("mask", (count, 4 * count), F32)
    c.keep("dn", (4 * count, D), F32)

    def body(flags, get, send):
        forward_body((0, 1), (0, 1), count, width, hidden, True)(flags, get, send)
        mlp_body(hidden)(flags, get, send)
        attn_body(count, width)(flags, get, send)

    return c.run(body, where, "last_layer", 40, dep)


def norm_kernel(rows, vec, own, mate, later, dh1, low, small):
    back = own[...] + mate[...].astype(F32) + later[...].astype(F32)
    normed, factor = standard(rows[...].astype(F32))
    low[...] = (dh1[...] + norm_back(back, normed, factor, vec[0:1, :])).astype(BF16)
    small[...] = jnp.concatenate(
        [total_rows(back * normed), total_rows(back), jnp.zeros((6, D), F32)], axis=0
    )


class NormBack:
    def __init__(self, rows, vec, back, dh1):
        self.rows, self.vec, self.back, self.dh1 = rows, vec, back, dh1
        self.mate = swap(back["sent"], SECTION)

    def send(self, dep):
        count = self.rows.shape[0]
        prior = sum_rows([self.back["prior"], self.mate[:count]], dep)
        self.later = shift(prior, -1)
        return prior

    def finish(self, dep):
        shape = jax.ShapeDtypeStruct
        extra, extra_specs = after(dep)
        count = self.rows.shape[0]
        operands = [
            self.rows, self.vec, self.back["own"], self.mate[count:], self.later, self.dh1,
        ]

        def kernel(*refs):
            norm_kernel(*refs[: len(operands)], *refs[-2:])

        return pl.pallas_call(
            kernel,
            in_specs=[pl.BlockSpec(memory_space=pltpu.VMEM)] * len(operands) + extra_specs,
            out_shape=[shape(self.dh1.shape, BF16), shape((8, D), F32)],
            name="first_norm_back",
            compiler_params=params(SMALL),
            cost_estimate=lasts(1),
        )(*operands, *extra)


def gather_small(where, norms, mlps, attns, dep):
    halves = [m[f"gfc{i}"] for m in mlps for i in range(2)]
    halves += [a[f"gqv{i}"] for a in attns for i in range(2)]
    operands = list(norms) + [m["small"] for m in mlps] + halves
    extra, extra_specs = after(dep)

    def kernel(flags, norm_a, norm_b, mlp_a, mlp_b, f0, f1, g0, g1, a0, a1, b0, b1, *rest):
        out = rest[-1]
        out[...] = jnp.zeros_like(out)
        out[0:2, :] = norm_a[0:2, :] + norm_b[0:2, :]
        out[2:6, :] = mlp_a[0:4, :] + mlp_b[0:4, :]
        bqv = (a0[0:2, :] + b0[0:2, :], a1[0:2, :] + b1[0:2, :])
        bfc = (f0[...] + g0[...], f1[...] + g1[...])
        for value in range(2):

            @pl.when(flags[2] == value)
            def _():
                out[6:8, :] = jnp.concatenate([bqv[value], bqv[1 - value]], axis=1)
                for place in range(2):
                    row = 8 + 2 * (place if value == 0 else 1 - place)
                    out[row : row + 1, :] = bfc[place][:, :D]
                    out[row + 1 : row + 2, :] = bfc[place][:, D:]

    return pl.pallas_call(
        kernel,
        in_specs=[pl.BlockSpec(memory_space=pltpu.SMEM)]
        + [pl.BlockSpec(memory_space=pltpu.VMEM)] * len(operands)
        + extra_specs,
        out_shape=jax.ShapeDtypeStruct((16, D), F32),
        compiler_params=params(SMALL),
        cost_estimate=lasts(1),
        name="gather_small",
    )(where, *operands, *extra)


class Spread:
    def __init__(self, section, tensor):
        self.section, self.tensor = section, tensor

    def add(self, layers, dep):
        rows, width = layers[0].shape[0], layers[0].shape[1] // 2
        extra, extra_specs = after(dep)

        def kernel(which, a, b, *rest):
            for value in range(2):

                @pl.when(which[0] == value)
                def _():
                    for layer, ref in enumerate((a, b)):
                        rest[-2][layer] = ref[:, value * width : (value + 1) * width]
                        rest[-1][layer] = ref[:, (1 - value) * width : (2 - value) * width]

        shape = jax.ShapeDtypeStruct((2, rows, width), layers[0].dtype)
        self.mine, theirs = pl.pallas_call(
            kernel,
            in_specs=[pl.BlockSpec(memory_space=pltpu.SMEM)]
            + [pl.BlockSpec(memory_space=pltpu.VMEM)] * 2
            + extra_specs,
            out_shape=[shape, shape],
            compiler_params=params(SMALL),
            cost_estimate=lasts(0.7),
            name="spread",
        )(self.tensor.reshape(1), *layers, *extra)
        self.theirs = swap(theirs, TENSOR)
        return self.mine

    def turn(self, dep):
        extra, extra_specs = after(dep)

        def kernel(which, a, b, *rest):
            for section in range(2):
                for tensor in range(2):

                    @pl.when((which[0] == section) & (which[1] == tensor))
                    def _():
                        for out, layer in ((rest[-2], section), (rest[-1], 1 - section)):
                            out[tensor] = a[layer]
                            out[1 - tensor] = b[layer]

        shape = jax.ShapeDtypeStruct(self.mine.shape, self.mine.dtype)
        self.kept, sent = pl.pallas_call(
            kernel,
            in_specs=[pl.BlockSpec(memory_space=pltpu.SMEM)]
            + [pl.BlockSpec(memory_space=pltpu.VMEM)] * 2
            + extra_specs,
            out_shape=[shape, shape],
            compiler_params=params(SMALL),
            cost_estimate=lasts(0.7),
            name="turn",
        )(jnp.stack([self.section, self.tensor]), self.mine, self.theirs, *extra)
        self.mate = swap(sent, SECTION)
        return self.kept

    def finish(self, kind, dep):
        _, rows, width = self.kept.shape
        extra, extra_specs = after(dep)

        def kernel(which, mine, mate, *rest):
            out = rest[-1]
            for value in range(2):

                @pl.when(which[0] == value)
                def _():
                    for micro in range(2):
                        here = slice(value * rows, (value + 1) * rows)
                        there = slice((1 - value) * rows, (2 - value) * rows)
                        out[micro, here, :] = mine[micro].astype(kind)
                        out[micro, there, :] = mate[micro].astype(kind)

        return pl.pallas_call(
            kernel,
            in_specs=[pl.BlockSpec(memory_space=pltpu.SMEM)]
            + [pl.BlockSpec(memory_space=pltpu.VMEM)] * 2
            + extra_specs,
            out_shape=jax.ShapeDtypeStruct((2, 2 * rows, width), kind),
            compiler_params=params(SMALL),
            cost_estimate=lasts(1),
            name="spread_out",
        )(self.section.reshape(1), self.kept, self.mate, *extra)


def pack_vectors(vectors, qv_bias, fc_bias):
    half = vectors[0].shape[0]
    more = fc_bias.shape[0] // half

    def kernel(*refs):
        out = refs[-1]
        out[...] = jnp.zeros_like(out)
        for i in range(len(vectors)):
            out[i : i + 1, :] = refs[i][...].astype(F32)
        out[6:8, :] = refs[-3][...].astype(F32)
        for i in range(more):
            out[8 + i : 9 + i, :] = refs[-2][:, i * half : (i + 1) * half].astype(F32)

    return pl.pallas_call(
        kernel,
        out_shape=jax.ShapeDtypeStruct((16, half), F32),
        compiler_params=params(SMALL),
        cost_estimate=lasts(1),
        name="pack_vectors",
    )(*[v.reshape(1, half) for v in vectors], qv_bias, fc_bias.reshape(1, -1))


def unpack_vectors(tensor, mine, other):
    half = mine.shape[1]

    def kernel(which, a, b, vec, bqv0, bqv1, bfc0, bfc1):
        for value in range(2):

            @pl.when(which[0] == value)
            def _():
                order = (a, b) if value == 0 else (b, a)
                vec[:, :half] = order[0][0:8, :]
                vec[:, half:] = order[1][0:8, :]

        for ref, bqv, bfc in ((a, bqv0, bfc0), (b, bqv1, bfc1)):
            bqv[...] = ref[6:8, :]
            for i in range(4):
                bfc[:, i * half : (i + 1) * half] = ref[8 + i : 9 + i, :]

    shape = lambda *s: jax.ShapeDtypeStruct(s, F32)
    pair = [shape(2, half)] * 2 + [shape(1, 4 * half)] * 2
    return pl.pallas_call(
        kernel,
        in_specs=[pl.BlockSpec(memory_space=pltpu.SMEM)]
        + [pl.BlockSpec(memory_space=pltpu.VMEM)] * 2,
        out_shape=[shape(8, 2 * half)] + pair,
        compiler_params=params(SMALL),
        cost_estimate=lasts(1),
        name="unpack_vectors",
    )(tensor.reshape(1), mine, other)


def assemble(where, own, arrived, mate):
    count = arrived.shape[0] // 3
    half = own.shape[1]

    def kernel(which, own_ref, arrived_ref, mate_ref, out, mine):
        for section in range(2):
            for tensor in range(2):

                @pl.when((which[0] == section) & (which[2] == tensor))
                def _():
                    here = slice(tensor * half, (tensor + 1) * half)
                    there = slice((1 - tensor) * half, (2 - tensor) * half)
                    out[2 * count :, here] = own_ref[...]
                    for place in range(2):
                        ref = arrived_ref if place == section else mate_ref
                        rows = slice(place * count, (place + 1) * count)
                        later = slice((2 + place) * count, (3 + place) * count)
                        out[later, there] = ref[:count, :]
                        out[rows, here] = ref[count : 2 * count, :]
                        out[rows, there] = ref[2 * count :, :]
                    rows = slice((2 + section) * count, (3 + section) * count)
                    mine[...] = out[rows, :]

    return pl.pallas_call(
        kernel,
        in_specs=[pl.BlockSpec(memory_space=pltpu.SMEM)]
        + [pl.BlockSpec(memory_space=pltpu.VMEM)] * 3,
        out_shape=[
            jax.ShapeDtypeStruct((4 * count, 2 * half), BF16),
            jax.ShapeDtypeStruct((count, 2 * half), BF16),
        ],
        compiler_params=params(SMALL),
        cost_estimate=lasts(1),
        name="assemble",
    )(where, own, arrived, mate)


def gather_rows(own):
    section = lax.axis_index(SECTION)
    mate = swap(own, SECTION)
    prior_mine = shift(own, 1)
    prior_mate = swap(prior_mine, SECTION)
    first = section == 0
    pick = lambda a, b: [jnp.where(first, a, b), jnp.where(first, b, a)]
    return jnp.concatenate(pick(prior_mine, prior_mate) + pick(own, mate), axis=0)


def join_features(tensor, mine, other, dep):
    rows, half = mine.shape
    extra, extra_specs = after(dep)

    def kernel(which, a, b, *rest):
        for value in range(2):

            @pl.when(which[0] == value)
            def _():
                rest[-1][:, value * half : (value + 1) * half] = a[...]
                rest[-1][:, (1 - value) * half : (2 - value) * half] = b[...]

    return pl.pallas_call(
        kernel,
        in_specs=[pl.BlockSpec(memory_space=pltpu.SMEM)]
        + [pl.BlockSpec(memory_space=pltpu.VMEM)] * 2
        + extra_specs,
        out_shape=jax.ShapeDtypeStruct((rows, 2 * half), mine.dtype),
        compiler_params=params(SMALL),
        cost_estimate=lasts(0.7),
        name="join_features",
    )(tensor.reshape(1), mine, other, *extra)


def local(
    inputs,
    out_grads,
    seq_blocks,
    ln1_gain,
    ln1_shift,
    qkv_weight,
    qv_bias,
    out_weight,
    out_bias,
    ln2_gain,
    ln2_shift,
    fc_weight,
    fc_bias,
    proj_weight,
    proj_bias,
):
    section = lax.axis_index(SECTION)
    position = lax.axis_index("dp")
    tensor = lax.axis_index(TENSOR)
    half = D // 2
    block = inputs.shape[1]
    count = block // 2
    hidden = fc_weight.shape[1]
    first = tensor == 0

    def features(mine, other):
        return ordered(first, mine, other, mine.ndim - 1)

    micro = lambda a, which: lax.dynamic_index_in_dim(a, which, 0, keepdims=False)
    starts = jnp.cumsum(seq_blocks, axis=1) - seq_blocks
    continuing = jnp.logical_not(jnp.any(starts == position, axis=1))
    continues = micro(continuing, tensor)
    where = jnp.stack([section, continues.astype(jnp.int32), tensor])

    own_rows = lambda a, which: part(micro(a, which), section, 2)
    here, there = own_rows(inputs, tensor), own_rows(inputs, 1 - tensor)
    count_dp = lax.axis_size("dp")
    ahead = [(2 * i + j, 2 * i + 2 + 1 - j) for i in range(count_dp - 1) for j in range(2)]
    across = swap(there, TENSOR)
    before_here = shift(here, 1)
    before_there = lax.ppermute(there, ("dp", TENSOR), ahead)
    arrived = jnp.concatenate([across, before_here, before_there], axis=0)
    mate = swap(arrived, SECTION)
    rows_one, mine = assemble(where, micro(inputs, tensor), arrived, mate)
    vectors = pack_vectors(
        [ln1_gain, ln1_shift, out_bias, ln2_gain, ln2_shift, proj_bias], qv_bias, fc_bias
    )
    other_vectors = swap(vectors, TENSOR)
    vec, *biases = unpack_vectors(tensor, vectors, other_vectors)
    head_weights = [qkv_weight[:, n] for n in range(3)] + [out_weight[:, :half], out_weight[:, half:]]
    head_weights = jnp.concatenate(head_weights, axis=0)
    fetch_heads = Fetch(head_weights, 1, 2)
    fetch_fc, fetch_proj = Fetch(fc_weight, 2), Fetch(proj_weight, 1)
    weights = [
        dict(wqkv=head_weights, wfc=fc_weight, wp=proj_weight),
        {},
    ]
    for half_index in range(2):
        weights[half_index].update(bqv=biases[half_index], bfc=biases[2 + half_index])
    dep = fetch_heads.start([across, before_here, before_there, other_vectors])
    fetch_heads.pass_on()
    dep = fetch_fc.start(dep)
    dep = fetch_proj.start(dep)
    one = forward_part(where, vec, weights, (0,), (), rows=rows_one, dep=dep)
    dep = fetch_heads.join(one["sum"])
    dep = fetch_heads.finish(dep)
    dep = fetch_fc.pass_on(dep)
    dep = fetch_proj.pass_on(dep)
    weights[1].update(wqkv=fetch_heads.whole)
    one_b = forward_part(
        where, vec, weights, (1,), (0,), nrm=one["nrm"], carried=one["sum"], dep=dep
    )
    other = swap(own_rows(out_grads, 1 - tensor), TENSOR)
    dep = dout = join_features(tensor, own_rows(out_grads, tensor), other, one_b["sum"])
    dep = fetch_fc.join(dep)
    dep = fetch_proj.join(dep)
    dep = fetch_fc.finish(dep)
    dep = fetch_proj.finish(dep)
    weights[1].update(wfc=fetch_fc.whole, wp=fetch_proj.whole)
    one_c = forward_part(
        where, vec, weights, (), (1,), nrm2=one_b["nrm2"], carried=one_b["sum"], dep=dep
    )
    one = {**one, **one_b, **one_c}
    two = last_layer(where, vec, weights, gather_rows(one["act"]), dout)
    norm_two = NormBack(one["act"], vec, two, two["dh1"])
    dep = norm_two.send(two["prior"])
    layers = [[two, two, two, dout], [one, None, None, None]]
    flat = lambda s, piece: (0, 0)
    by_piece = lambda s, piece: (0, piece)
    own_piece = lambda s, piece: (2 + s, piece)
    square, tall, narrow, thin = (count, D), (4 * count, half), (count, half), (4 * count, half)

    def proj_terms(i):
        return [[(f[f"u{i}"], square, by_piece, g, square, flat) for f, _, _, g in layers]]

    def fc_terms(i):
        return [
            [(f["nrm2"], square, flat, m[f"df{i}"], square, by_piece) for f, m, _, _ in layers]
        ]

    def attn_terms(i):
        return [
            [(f["nrm"], narrow, own_piece, a[f"dq{i}"], narrow, flat) for f, _, a, _ in layers if a],
            [(f["nrm"], tall, by_piece, a[f"dk{i}"], thin, flat) for f, _, a, _ in layers if a],
            [(f["nrm"], tall, by_piece, a[f"dv{i}"], thin, flat) for f, _, a, _ in layers if a],
            [(f[f"o{i}"], narrow, flat, m["ga"], narrow, by_piece) for f, m, a, _ in layers if a],
        ]

    proj, fc = Reduction(where, proj_terms), Reduction(where, fc_terms)
    attn = Reduction(where, attn_terms, True)
    dep = attn.first_layer(dep)
    low_two, small_two = norm_two.finish(dep)
    layers[1][3] = low_two
    dep = proj.theirs_foreign(low_two)
    dep = proj.theirs_own(dep)
    dep = proj.foreign(dep)
    mlp_one = layers[1][1] = backward_mlp(vec, weights, one, low_two, where, dep)
    dep = proj.own(mlp_one["ga"])
    dep = fc.theirs_foreign(dep)
    dep = fc.theirs_own(dep)
    dep = fc.foreign(dep)
    dep = fc.own(dep)
    dep = proj.split(dep)
    attn_one = layers[1][2] = backward_attn(where, weights, one, mlp_one["ga"], dep)
    norm_one = NormBack(mine, vec, attn_one, mlp_one["dh1"])
    sums = grads = None
    low_one, small_one = None, None
    levels = 0
    while 2 ** (levels + 1) < count_dp:
        levels += 1
    dep = attn.theirs_foreign(attn_one["own"])
    dep = attn.theirs_own(dep)
    dep = proj.split(dep)
    dep = attn.foreign(dep)
    dep = fc.split(dep)
    dep = norm_one.send(dep)
    for level in range(1, levels):
        dep = proj.split(dep)
    dep = attn.own(dep)
    dep = proj.sum(dep)
    dep = fc.split(dep)
    low_one, small_one = norm_one.finish(dep)
    norms, mlps, attns = (small_one, small_two), (mlp_one, two), (attn_one, two)
    dep = gather_small(where, norms, mlps, attns, low_one)
    sums = SmallSum(dep)
    for level in range(1, levels):
        dep = proj.join(dep)
    dep = attn.split(dep)
    dep = sums.step(dep)
    for level in range(1, levels):
        dep = fc.split(dep)
        dep = sums.step(dep)
    dep = attn.split(dep)
    dep = fc.sum(dep)
    dep = proj.join(dep)
    for level in range(1, levels):
        dep = attn.split(dep)
        dep = fc.join(dep)
        dep = sums.step(dep)
    dep = attn.sum(dep)
    dep = fc.join(dep)
    dep = proj.join(dep)
    dep = sums.step(dep)
    dep = attn.join(dep)
    acts, grads = Spread(section, tensor), Spread(section, tensor)
    dep = acts.add([one["act"], two["act"]], dep)
    dep = grads.add([low_one, low_two], dep)
    row_steps = 2
    take = lambda i, size: slice(i * size, (i + 1) * size)

    def place_proj(core):
        size = hidden // 2 // row_steps
        return [
            (take(i, size), (take(core * row_steps + i, size), slice(0, D)))
            for i in range(row_steps)
        ]

    def place_fc(core):
        size = D // row_steps
        return [(take(i, size), (take(i, size), take(core, D))) for i in range(row_steps)]

    def place_out(core):
        return [(take(3, half), (slice(0, half), take(core, half)))]

    proj_grad, dep = widen(section, proj.kept, proj.other, (hidden, D), place_proj, dep)
    for level in range(1, levels):
        dep = attn.join(dep)
    dep = sums.step(dep)
    dep = fc.join(dep)
    dep = acts.turn(dep)
    dep = grads.turn(dep)
    fc_grad, dep = widen(section, fc.kept, fc.other, (D, hidden), place_fc, dep)
    dep = acts_out = acts.finish(BF16, dep)
    dep = grads_out = grads.finish(F32, dep)
    dep = attn.join(dep)

    while sums.other is not None:
        dep = sums.step(dep)
    out_grad, _ = widen(section, attn.kept, attn.other, (half, D), place_out, dep)
    assert proj.bit == fc.bit == attn.bit == 0
    sides = lambda n: [a[n * half : (n + 1) * half] for a in (attn.kept, attn.other)]
    qkv_grad = jnp.stack([ordered(section == 0, *sides(n), 0) for n in range(3)], axis=1)
    qkv_grad = qkv_grad.astype(F32)
    rows_here = part(sums.array[:8], tensor, 2, 1)
    bfc_grad = part(sums.array[8:12], tensor, 2).reshape(hidden)
    return (
        acts_out[None],
        grads_out[None],
        rows_here[0],
        rows_here[1],
        qkv_grad,
        rows_here[6:8],
        out_grad,
        rows_here[4],
        rows_here[2],
        rows_here[3],
        fc_grad,
        bfc_grad,
        proj_grad,
        rows_here[5],
    )


def solution(mesh):
    in_specs = (
        P(None, "dp", TENSOR),
        P(None, "dp", TENSOR),
        P(),
        P(TENSOR),
        P(TENSOR),
        P(None, None, TENSOR),
        P(None, TENSOR),
        P(TENSOR, None),
        P(TENSOR),
        P(TENSOR),
        P(TENSOR),
        P(None, TENSOR),
        P(TENSOR),
        P(TENSOR, None),
        P(TENSOR),
    )
    out_specs = (
        P(SECTION, None, "dp", TENSOR),
        P(SECTION, None, "dp", TENSOR),
        P(TENSOR),
        P(TENSOR),
        P(None, None, TENSOR),
        P(None, TENSOR),
        P(TENSOR, None),
        P(TENSOR),
        P(TENSOR),
        P(TENSOR),
        P(None, TENSOR),
        P(TENSOR),
        P(TENSOR, None),
        P(TENSOR),
    )
    return jax.shard_map(local, mesh=mesh, in_specs=in_specs, out_specs=out_specs, check_vma=False)
```

```python
import math

import jax
import jax.numpy as jnp
from jax import lax
from jax.experimental import pallas as pl
from jax.experimental.pallas import tpu as pltpu
from jax.sharding import PartitionSpec as P

SECTION, TENSOR = "section", "tensor"
D = 768
HEAD = 64
NORM_EPSILON = 1e-05
MASKED = -1e30
SCALE = HEAD ** (-0.5)
F32 = jnp.float32
BF16 = jnp.bfloat16
LIMIT = 60 * 1024 * 1024
SMALL = 12 * 1024 * 1024
SPARE = 12 * 1024 * 1024


def dot(a, b, dims=((1,), (0,))):
    return lax.dot_general(a, b, (dims, ((), ())), preferred_element_type=F32)


def swap(array, axis):
    return lax.ppermute(array, axis, [(0, 1), (1, 0)])


def shift(array, by):
    count = lax.axis_size("dp")
    pairs = [(i, i + by) for i in range(count) if 0 <= i + by < count]
    return lax.ppermute(array, "dp", pairs)


def exchange(array, bit):
    count = lax.axis_size("dp")
    return lax.ppermute(array, "dp", [(i, i ^ bit) for i in range(count)])


def part(array, which, parts, axis=0):
    size = array.shape[axis] // parts
    return lax.dynamic_slice_in_dim(array, which * size, size, axis)


def ordered(first, mine, other, axis):
    return jnp.concatenate(
        [jnp.where(first, mine, other), jnp.where(first, other, mine)], axis=axis
    )


def add_low(a, b):
    return (a.astype(F32) + b.astype(F32)).astype(BF16)


def lasts(microseconds):
    return pl.CostEstimate(flops=int(microseconds * 2e7), bytes_accessed=1, transcendentals=0)


def params(limit):
    return pltpu.CompilerParams(vmem_limit_bytes=limit)


def after(dep):
    deps = [] if dep is None else list(dep) if isinstance(dep, (list, tuple)) else [dep]
    return deps, [pl.BlockSpec(memory_space=pl.ANY)] * len(deps)


def sum_split(sets, side, dep=None):
    halves = [arrays[0].shape[0] // 2 for arrays in sets]
    if any(rows % 16 for rows in halves):
        totals = [sum(a.astype(F32) for a in arrays).astype(BF16) for arrays in sets]
        pick = lambda which: jnp.concatenate([part(t, which, 2) for t in totals], axis=0)
        return pick(side), pick(1 - side)
    width = sets[0][0].shape[1]
    extra, extra_specs = after(dep)
    operands, specs = [], []
    for arrays, rows in zip(sets, halves):
        for array in arrays:
            operands += [array, array]
            specs.append(pl.BlockSpec((rows, width), lambda j, which: (which[0], 0)))
            specs.append(pl.BlockSpec((rows, width), lambda j, which: (1 - which[0], 0)))

    def kernel(which, *refs):
        at, row = 0, 0
        for arrays, rows in zip(sets, halves):
            for out, first in ((refs[-2], at), (refs[-1], at + 1)):
                total = refs[first][...].astype(F32)
                for i in range(1, len(arrays)):
                    total += refs[first + 2 * i][...].astype(F32)
                out[row : row + rows, :] = total.astype(BF16)
            at, row = at + 2 * len(arrays), row + rows

    block = (sum(halves), width)
    flat = pl.BlockSpec(block, lambda j, which: (0, 0))
    return pl.pallas_call(
        kernel,
        grid_spec=pltpu.PrefetchScalarGridSpec(
            num_scalar_prefetch=1,
            grid=(1,),
            in_specs=specs + extra_specs,
            out_specs=[flat] * 2,
        ),
        out_shape=[jax.ShapeDtypeStruct(block, BF16)] * 2,
        compiler_params=params(SMALL),
        cost_estimate=lasts(1.2),
        name="sum_split",
    )(side.reshape(1), *operands, *extra)


def sum_rows(arrays, dep=None):
    rows, width = arrays[0].shape
    kind = arrays[0].dtype
    if rows % 16:
        return add_low(*arrays)
    extra, extra_specs = after(dep)

    def kernel(a, b, *rest):
        rest[-1][...] = (a[...].astype(F32) + b[...].astype(F32)).astype(kind)

    return pl.pallas_call(
        kernel,
        in_specs=[pl.BlockSpec(memory_space=pltpu.VMEM)] * 2 + extra_specs,
        out_shape=jax.ShapeDtypeStruct((rows, width), kind),
        compiler_params=params(SMALL),
        cost_estimate=lasts(0.7),
        name="sum_rows",
    )(*arrays, *extra)


def put_rows(side, mine, other, dep=None):
    rows, width = mine.shape
    if rows % 16:
        return ordered(side == 0, mine, other, 0)
    extra, extra_specs = after(dep)

    def kernel(which, a, b, *rest):
        out = rest[-1]
        out[pl.ds(pl.multiple_of(which[0] * rows, rows), rows), :] = a[...]
        out[pl.ds(pl.multiple_of((1 - which[0]) * rows, rows), rows), :] = b[...]

    return pl.pallas_call(
        kernel,
        in_specs=[pl.BlockSpec(memory_space=pltpu.SMEM)]
        + [pl.BlockSpec(memory_space=pltpu.VMEM)] * 2
        + extra_specs,
        out_shape=jax.ShapeDtypeStruct((2 * rows, width), BF16),
        compiler_params=params(SMALL),
        cost_estimate=lasts(0.7),
        name="put_rows",
    )(side.reshape(1), mine, other, *extra)


def gradient(where, terms, which, added=(), dep=None, cuts=1):
    arrays, specs, plan = [], [], []
    for term in terms:
        plan.append(len(term))
        for a, a_block, a_index, b, b_block, b_index in term:
            for array, block, index in ((a, a_block, a_index), (b, b_block, b_index)):
                arrays.append(array)
                specs.append(
                    pl.BlockSpec(block, lambda j, w, index=index: index(w[0], w[0] ^ which))
                )
    rows, width = terms[0][0][1][1], terms[0][0][4][1]
    total = rows * len(terms)
    last = len(arrays)
    for pieces in added:
        for array in pieces:
            arrays.append(array)
            specs.append(pl.BlockSpec(array.shape, lambda j, w: (0, 0)))
    extra, extra_specs = after(dep)

    def kernel(w, *refs):
        outs, at = refs[len(refs) - cuts :], 0
        for i, layers in enumerate(plan):
            value = None
            for _ in range(layers):
                one = dot(refs[at][...], refs[at + 1][...], ((0,), (0,)))
                value = one if value is None else value + one
                at += 2
            span = slice(i * rows, (i + 1) * rows)
            place = last
            for pieces in added:
                each = total // len(pieces)
                taken = []
                for cut in range(len(pieces)):
                    low, high = max(span.start, cut * each), min(span.stop, (cut + 1) * each)
                    if low < high:
                        taken.append(refs[place + cut][low - cut * each : high - cut * each, :])
                value += jnp.concatenate([t.astype(F32) for t in taken], axis=0)
                place += len(pieces)
            each = total // cuts
            for cut in range(cuts):
                low, high = max(span.start, cut * each), min(span.stop, (cut + 1) * each)
                if low < high:
                    taken = value[low - span.start : high - span.start, :]
                    outs[cut][low - cut * each : high - cut * each, :] = taken.astype(BF16)

    outs = pl.pallas_call(
        kernel,
        grid_spec=pltpu.PrefetchScalarGridSpec(
            num_scalar_prefetch=1,
            grid=(1,),
            in_specs=specs + extra_specs,
            out_specs=[pl.BlockSpec((total // cuts, width), lambda j, w: (0, 0))] * cuts,
        ),
        out_shape=[jax.ShapeDtypeStruct((total // cuts, width), BF16)] * cuts,
        compiler_params=params(SMALL),
        cost_estimate=lasts(1 + sum(plan) * 0.35),
        name="gradient",
    )(where, *arrays, *extra)
    return outs[0] if cuts == 1 else outs


class Reduction:
    def __init__(self, where, terms_of, early=False):
        self.where, self.terms_of = where, terms_of
        self.bit = 1
        self.early = early
        self.partial = {}

    def first_layer(self, dep):
        for half in (1, 0):
            for which in (1, 0):
                terms = [term[:1] for term in self.terms_of(half)]
                dep = self.partial[half, which] = gradient(self.where, terms, which, dep=dep)
        return dep

    def piece(self, half, which, mate, dep, cuts=1):
        terms, added = self.terms_of(half), [] if mate is None else [mate]
        added = [a if isinstance(a, list) else [a] for a in added]
        if self.early:
            terms = [term[1:] for term in terms]
            added.append([self.partial[half, which]])
        return gradient(self.where, terms, which, added, dep, cuts)

    def theirs_foreign(self, dep):
        theirs = self.piece(1, 1, None, dep, 2)
        self.mate_foreign = [swap(cut, SECTION) for cut in theirs]
        return theirs[0]

    def theirs_own(self, dep):
        theirs = self.piece(0, 1, None, dep, 2)
        self.mate_own = [swap(cut, SECTION) for cut in theirs]
        return theirs[0]

    def foreign(self, dep):
        foreign = self.piece(1, 0, self.mate_foreign, dep)
        self.across = swap(foreign, TENSOR)
        return foreign

    def own(self, dep):
        own = self.piece(0, 0, self.mate_own, dep)
        self.arrays = [own, self.across]
        return own

    def side(self):
        return (lax.axis_index("dp") // self.bit) % 2

    def split(self, dep, other=None):
        sets = [self.arrays] if other is None else [self.arrays, other.arrays]
        kept, sent = sum_split(sets, self.side(), dep)
        self.arrays = [kept, exchange(sent, self.bit)]
        self.bit *= 2
        return kept

    def sum(self, dep):
        self.kept = sum_rows(self.arrays, dep)
        self.send_back()
        return self.kept

    def send_back(self):
        self.bit //= 2
        self.other = swap(self.kept, SECTION) if self.bit == 0 else exchange(self.kept, self.bit)

    def join(self, dep):
        self.kept = put_rows(self.side(), self.kept, self.other, dep)
        self.send_back()
        return self.kept


class SmallSum:
    def __init__(self, array):
        bits = []
        while 2 ** len(bits) < lax.axis_size("dp"):
            bits.append(2 ** len(bits))
        self.moves = [lambda a: swap(a, SECTION), lambda a: swap(a, TENSOR)]
        self.moves += [lambda a, bit=bit: exchange(a, bit) for bit in bits]
        self.array = array
        self.other = self.moves.pop(0)(array)

    def step(self, dep):
        if self.other is None:
            return dep
        self.array = sum_rows([self.array, self.other], dep)
        self.other = self.moves.pop(0)(self.array) if self.moves else None
        return self.array


def widen(section, kept, other, shape, place, dep):
    extra, extra_specs = after(dep)
    plan = [place(core) for core in range(2)]
    steps = len(plan[0])

    def kernel(which, a, b, *rest):
        out, token, held, sems = rest[-4:]
        token[...] = jnp.zeros_like(token)
        for value in range(2):

            @pl.when(which[0] == value)
            def _():
                copies = []
                for core, ref in ((value, a), (1 - value, b)):
                    for step, (rows, block) in enumerate(plan[core]):
                        held[block] = ref[rows, :].astype(F32)
                        copy = pltpu.make_async_copy(
                            held.at[block], out.at[block], sems.at[core * steps + step]
                        )
                        copy.start()
                        copies.append(copy)
                for copy in copies:
                    copy.wait()

    return pl.pallas_call(
        kernel,
        in_specs=[pl.BlockSpec(memory_space=pltpu.SMEM)]
        + [pl.BlockSpec(memory_space=pltpu.VMEM)] * 2
        + extra_specs,
        out_specs=[pl.BlockSpec(memory_space=pltpu.HBM), pl.BlockSpec(memory_space=pltpu.VMEM)],
        out_shape=[jax.ShapeDtypeStruct(shape, F32), jax.ShapeDtypeStruct((8, 128), F32)],
        scratch_shapes=[pltpu.VMEM(shape, F32), pltpu.SemaphoreType.DMA((2 * steps,))],
        compiler_params=params(SMALL),
        cost_estimate=lasts(2),
        name="widen",
    )(section.reshape(1), kept, other, *extra)


def take_rows(array, which, parts, dep):
    rows, width = array.shape[0] // parts, array.shape[1]
    extra, extra_specs = after(dep)

    def kernel(w, a, *rest):
        out, sem = rest[-2:]
        span = pl.ds(pl.multiple_of(w[0] * rows, rows), rows)
        copy = pltpu.make_async_copy(a.at[span, :], out, sem)
        copy.start()
        copy.wait()

    return pl.pallas_call(
        kernel,
        in_specs=[pl.BlockSpec(memory_space=pltpu.SMEM), pl.BlockSpec(memory_space=pl.ANY)]
        + extra_specs,
        out_specs=pl.BlockSpec(memory_space=pltpu.VMEM),
        out_shape=jax.ShapeDtypeStruct((rows, width), array.dtype),
        scratch_shapes=[pltpu.SemaphoreType.DMA(())],
        compiler_params=params(SMALL),
        cost_estimate=lasts(0.7),
        name="take_rows",
    )(which.reshape(1), array, *extra)


class Fetch:
    def __init__(self, array, bit, cuts=1):
        self.array, self.bit, self.cuts = array, bit, cuts
        self.section = lax.axis_index(SECTION)
        self.side = (lax.axis_index("dp") // bit) % 2

    def start(self, dep):
        piece = take_rows(self.array, self.section * 2 + self.side, 4, dep)
        self.mine = swap(piece, TENSOR)
        return piece

    def pass_on(self, dep=None):
        if dep is not None:
            self.mine = take_rows(self.mine, jnp.int32(0), 1, dep)
        self.other = exchange(self.mine, self.bit)
        return self.mine

    def join(self, dep):
        mine, other = self.mine, self.other
        dep = other = take_rows(other, jnp.int32(0), 1, dep)
        rows = mine.shape[0] // self.cuts
        cut = lambda a: [a[i * rows : (i + 1) * rows] for i in range(self.cuts)]
        self.parts = [mine, other] + [swap(a, SECTION) for a in cut(mine) + cut(other)]
        return dep

    def finish(self, dep):
        self.whole = put_parts(self.section, self.side, self.parts, dep)
        return self.whole


def put_parts(section, side, parts, dep):
    rows, width = parts[0].shape
    cuts = (len(parts) - 2) // 2
    extra, extra_specs = after(dep)

    def kernel(which, *refs):
        out = refs[-1]

        def put(ref, core, half, piece):
            size = ref.shape[0]
            start = pl.multiple_of((2 * core + half) * rows, rows) + piece * size
            out[pl.ds(pl.multiple_of(start, 16), size), :] = ref[...]

        put(refs[0], which[0], which[1], 0)
        put(refs[1], which[0], 1 - which[1], 0)
        for i in range(cuts):
            put(refs[2 + i], 1 - which[0], which[1], i)
            put(refs[2 + cuts + i], 1 - which[0], 1 - which[1], i)

    return pl.pallas_call(
        kernel,
        in_specs=[pl.BlockSpec(memory_space=pltpu.SMEM)]
        + [pl.BlockSpec(memory_space=pltpu.VMEM)] * len(parts)
        + extra_specs,
        out_shape=jax.ShapeDtypeStruct((4 * rows, width), parts[0].dtype),
        compiler_params=params(SMALL),
        cost_estimate=lasts(1),
        name="put_parts",
    )(jnp.stack([section, side]), *parts, *extra)


def standard(rows):
    center = jnp.sum(rows, axis=1, keepdims=True) / D
    spread = jnp.sum(rows * rows, axis=1, keepdims=True) / D - center * center
    factor = lax.rsqrt(spread + NORM_EPSILON)
    return (rows - center) * factor, factor


def norm(rows, gain, shift_by):
    return (standard(rows)[0] * gain + shift_by).astype(BF16)


def norm_back(grad, normed, factor, gain):
    scaled = grad * gain
    mean = jnp.sum(scaled, axis=1, keepdims=True) / D
    along = jnp.sum(scaled * normed, axis=1, keepdims=True) / D
    return factor * (scaled - mean - normed * along)


def total_rows(array):
    return jnp.sum(array.astype(F32), axis=0, keepdims=True)


def only_head(array, which):
    lane = lax.broadcasted_iota(jnp.int32, array.shape, 1)
    return jnp.where((lane >= HEAD) == (which == 1), array, jnp.zeros_like(array))


GELU_A = 0.7978845608028654
GELU_B = 0.044715
PAIR = 2 * HEAD
CHUNK = 768


class Call:
    def __init__(self):
        self.names, self.arrays, self.out_names, self.out_shape, self.scratch = [], [], [], [], []

    def take(self, name, array):
        self.names.append(name)
        self.arrays.append(array)

    def give(self, name, shape, dtype):
        self.out_names.append(name)
        self.out_shape.append(jax.ShapeDtypeStruct(shape, dtype))

    def keep(self, name, shape, dtype):
        self.scratch.append((name, pltpu.VMEM(shape, dtype)))

    def run(self, body, flags, name, time, dep=None):
        extra, extra_specs = after(dep)
        taken, given = len(self.names), len(self.out_names)
        memory = [pltpu.VMEM(a.shape, a.dtype) for a in self.arrays]
        memory += [pltpu.VMEM(o.shape, o.dtype) for o in self.out_shape]
        memory += [shape for _, shape in self.scratch]
        size = sum(math.prod(m.shape) * jnp.dtype(m.dtype).itemsize for m in memory)
        memory.append(pltpu.SemaphoreType.DMA((taken + given,)))

        def kernel(flags_ref, *refs):
            far = list(refs[:taken]) + list(refs[taken + len(extra) : taken + len(extra) + given])
            near = refs[taken + len(extra) + given :]
            names = self.names + self.out_names + [n for n, _ in self.scratch]
            held = dict(zip(names, near[: len(names)]))
            sems = near[-1]
            copies = {}
            for i, key in enumerate(self.names):
                copies[key] = pltpu.make_async_copy(far[i], held[key], sems.at[i])
                copies[key].start()
            waiting = dict(copies)
            leaving = []

            def get(key):
                if key in waiting:
                    waiting.pop(key).wait()
                return held[key]

            def send(*keys):
                for key in keys:
                    if key not in self.out_names:
                        continue
                    i = taken + self.out_names.index(key)
                    copy = pltpu.make_async_copy(held[key], far[i], sems.at[i])
                    copy.start()
                    leaving.append(copy)

            body(flags_ref, get, send)
            for key in list(waiting):
                waiting.pop(key).wait()
            for copy in leaving:
                copy.wait()

        anywhere = pl.BlockSpec(memory_space=pltpu.HBM)
        outs = pl.pallas_call(
            kernel,
            in_specs=[pl.BlockSpec(memory_space=pltpu.SMEM)] + [anywhere] * taken + extra_specs,
            out_specs=[anywhere] * given,
            out_shape=self.out_shape,
            scratch_shapes=memory,
            compiler_params=params(min(size + SPARE, LIMIT)),
            cost_estimate=lasts(time),
            name=name,
        )(flags, *self.arrays, *extra)
        return dict(zip(self.out_names, outs))


def out_part(weights):
    width = weights.shape[1]
    return jnp.concatenate([weights[3 * D : 3 * D + width, :], weights[3 * D + width :, :]], axis=1)


def each_pair(count, body):
    for i in range(count):
        body(slice(i * PAIR, (i + 1) * PAIR), i)


def forward_part(
    where, vec, weights, attn, mlp, rows=None, nrm=None, nrm2=None, carried=None, dep=None
):
    c = Call()
    c.take("vec", vec)
    if rows is not None:
        c.take("rows", rows)
    if nrm is not None:
        c.take("nrm", nrm)
    if carried is not None:
        c.take("carried", carried)
    if nrm2 is not None:
        c.take("nrm2", nrm2)
    full = rows if rows is not None else nrm
    count = carried.shape[0] if full is None else full.shape[0] // 4
    width = weights[0]["wqkv"].shape[1]
    hidden = weights[0]["wp"].shape[0]
    for half in attn:
        for name in ("bqv", "wqkv"):
            c.take(f"{name}{half}", weights[half][name])
    for half in mlp:
        for name in ("bfc", "wfc", "wp"):
            c.take(f"{name}{half}", weights[half][name])
    if rows is not None:
        c.give("nrm", (4 * count, D), BF16)
    for half in attn:
        for name, n, kind in (
            ("q", count, BF16), ("k", 4 * count, BF16), ("v", 4 * count, BF16),
            ("o", count, BF16), ("of", count, F32), ("rl", count, F32),
        ):
            c.give(f"{name}{half}", (n, width), kind)
        c.give(f"p{half}", (2 * width // PAIR, count, 4 * count), BF16)
    middle = bool(attn) and bool(mlp)
    if middle:
        c.give("h1", (count, D), F32)
        c.give("nrm2", (count, D), BF16)
    for half in mlp:
        c.give(f"f{half}", (count, hidden), F32)
        c.give(f"u{half}", (count, hidden), BF16)
    final = 1 in mlp
    if final:
        c.give("act", (count, D), BF16)
        c.keep("sum", (count, D), F32)
    else:
        c.give("sum", (count, D), F32)
    if attn:
        c.keep("mask", (count, 4 * count), F32)

    body = forward_body(attn, mlp, count, width, hidden, rows is not None)
    return c.run(body, where, "forward", 12 * len(attn) + 3 * len(mlp), dep)


def forward_body(attn, mlp, count, width, hidden, first):
    def body(flags, get, send):
        total = get("sum")
        vec = get("vec")
        span = pl.ds(pl.multiple_of(2 * count + flags[0] * count, count), count)
        if first:
            rows_ref = get("rows")
            get("nrm")[...] = norm(rows_ref[...].astype(F32), vec[0:1, :], vec[1:2, :])
            total[...] = rows_ref[span, :].astype(F32) + vec[2:3, :]
            send("nrm")
        else:
            total[...] = get("carried")[...]
        if attn:
            mask = get("mask")
            row = lax.broadcasted_iota(jnp.int32, mask.shape, 0) + flags[0] * count
            col = lax.broadcasted_iota(jnp.int32, mask.shape, 1)
            limit = jnp.where(col < 2 * count, flags[1] * (4 * count) - 1, row + 2 * count)
            mask[...] = jnp.where(col <= limit, 0.0, MASKED)
            nrm_ref = get("nrm")
        for half in attn:
            here = lambda name, half=half: get(f"{name}{half}")
            bqv, wqkv = here("bqv"), here("wqkv")

            def pair(lanes, i, here=here, bqv=bqv, wqkv=wqkv):
                wq, wk, wv = [wqkv[n * D : (n + 1) * D, lanes] for n in range(3)]
                q = (dot(nrm_ref[span, :], wq) + bqv[0:1, lanes]).astype(BF16)
                here("q")[:, lanes] = q
                kv = dot(nrm_ref[...], jnp.concatenate([wk, wv], axis=1))
                k = kv[:, :PAIR].astype(BF16)
                here("k")[:, lanes] = k
                v = (kv[:, PAIR:] + bqv[1:2, lanes]).astype(BF16)
                here("v")[:, lanes] = v
                scaled = q * jnp.asarray(SCALE, BF16)
                both = jnp.concatenate([only_head(scaled, 0), only_head(scaled, 1)], axis=0)
                scores = dot(both, k, ((1,), (1,)))
                lows, factors = [], []
                for which in range(2):
                    masked = scores[which * count : (which + 1) * count, :] + mask[...]
                    lifted = jnp.exp(masked - jnp.max(masked, axis=1, keepdims=True))
                    lows.append(lifted.astype(BF16))
                    here("p")[2 * i + which] = lows[which]
                    factors.append(1.0 / jnp.sum(lifted, axis=1, keepdims=True))
                sides = dot(jnp.concatenate(lows, axis=0), v)
                lane = lax.broadcasted_iota(jnp.int32, q.shape, 1)
                factor = jnp.where(lane < HEAD, factors[0], factors[1])
                here("rl")[:, lanes] = factor
                o = jnp.where(lane < HEAD, sides[:count], sides[count:]) * factor
                here("of")[:, lanes] = o
                here("o")[:, lanes] = o.astype(BF16)

            each_pair(width // PAIR, pair)
            send(*[f"{name}{half}" for name in ("q", "k", "v", "p", "o", "of", "rl")])
            total[...] += dot(here("o")[...], out_part(wqkv))
        if attn and mlp:
            get("h1")[...] = total[...]
            get("nrm2")[...] = norm(total[...], vec[3:4, :], vec[4:5, :])
            total[...] += vec[5:6, :]
            send("h1", "nrm2")
        for half in mlp:
            here = lambda name, half=half: get(f"{name}{half}")
            wfc, bfc = here("wfc"), here("bfc")
            for i in range(hidden // CHUNK):
                lanes = slice(i * CHUNK, (i + 1) * CHUNK)
                pre = dot(get("nrm2")[...], wfc[:, lanes]) + bfc[:, lanes]
                here("f")[:, lanes] = pre
                inner = jnp.tanh(GELU_A * (pre + GELU_B * pre * pre * pre))
                hidden_low = (0.5 * pre * (1.0 + inner)).astype(BF16)
                here("u")[:, lanes] = hidden_low
                total[...] += dot(hidden_low, here("wp")[lanes, :])
            send(f"f{half}", f"u{half}")
        if 1 in mlp:
            get("act")[...] = total[...].astype(BF16)
            send("act")
        else:
            send("sum")

    return body


def backward_mlp(vec, weights, kept, dout, where, dep=None):
    c = Call()
    count = dout.shape[0]
    hidden = weights[0]["wp"].shape[0]
    c.take("dout", dout)
    for half in range(2):
        c.take(f"wp{half}", weights[half]["wp"])
        c.take(f"f{half}", kept[f"f{half}"])
        c.take(f"wfc{half}", weights[half]["wfc"])
    c.take("h1", kept["h1"])
    c.take("vec", vec)
    for half in range(2):
        c.give(f"df{half}", (count, hidden), BF16)
        c.give(f"gfc{half}", (1, hidden), F32)
    c.give("ga", (count, D), BF16)
    c.give("dh1", (count, D), F32)
    c.give("small", (8, D), F32)
    return c.run(mlp_body(hidden), where, "backward_mlp", 7, dep)


def mlp_body(hidden):
    def body(flags, get, send):
        dout = get("dout")
        back = None
        for half in range(2):
            wp, f, wfc = get(f"wp{half}"), get(f"f{half}"), get(f"wfc{half}")
            for i in range(hidden // CHUNK):
                lanes = slice(i * CHUNK, (i + 1) * CHUNK)
                du = dot(dout[...], wp[lanes, :], ((1,), (1,)))
                pre = f[:, lanes]
                square = pre * pre
                inner = jnp.tanh(GELU_A * (pre + GELU_B * square * pre))
                slope = 0.5 * (1.0 + inner) + (0.5 * GELU_A) * pre * (1.0 - inner * inner) * (
                    1.0 + 3.0 * GELU_B * square
                )
                low = (du * slope).astype(BF16)
                get(f"df{half}")[:, lanes] = low
                get(f"gfc{half}")[:, lanes] = total_rows(low)
                one = dot(low, wfc[:, lanes], ((1,), (1,)))
                back = one if back is None else back + one
            send(f"df{half}", f"gfc{half}")
        vec = get("vec")
        normed, factor = standard(get("h1")[...])
        grad = dout[...].astype(F32) + norm_back(back, normed, factor, vec[3:4, :])
        get("dh1")[...] = grad
        low = grad.astype(BF16)
        get("ga")[...] = low
        sums = [total_rows(x) for x in (back * normed, back, low, dout[...])]
        get("small")[...] = jnp.concatenate(sums + [jnp.zeros((4, D), F32)], axis=0)
        send("ga", "dh1", "small")

    return body


def backward_attn(where, weights, kept, ga, dep=None):
    c = Call()
    count = ga.shape[0]
    width = weights[0]["wqkv"].shape[1]
    c.take("ga", ga)
    for half in range(2):
        c.take(f"wqkv{half}", weights[half]["wqkv"])
        for name in ("rl", "of", "q", "v", "p", "k"):
            c.take(f"{name}{half}", kept[f"{name}{half}"])
    for half in range(2):
        for name, n in (("dq", count), ("dk", 4 * count), ("dv", 4 * count)):
            c.give(f"{name}{half}", (n, width), BF16)
        c.give(f"gqv{half}", (8, width), F32)
    c.give("sent", (2 * count, D), BF16)
    c.give("prior", (count, D), BF16)
    c.give("own", (count, D), F32)
    c.keep("dn", (4 * count, D), F32)
    return c.run(attn_body(count, width), where, "backward_attn", 15, dep)


def attn_body(count, width):
    def body(flags, get, send):
        dn = get("dn")
        span = pl.ds(pl.multiple_of(2 * count + flags[0] * count, count), count)
        ga = get("ga")
        for half in range(2):
            here = lambda name, half=half: get(f"{name}{half}")
            wqkv = here("wqkv")
            do_all = dot(ga[...], out_part(wqkv), ((1,), (1,)))
            refs = {name: here(name) for name in ("rl", "of", "q", "v", "p", "k")}

            def pair(lanes, i, here=here, do_all=do_all, refs=refs):
                by_head = lambda a: jnp.concatenate([only_head(a, 0), only_head(a, 1)], axis=0)
                do = (do_all[:, lanes] * refs["rl"][:, lanes]).astype(BF16)
                product = do.astype(F32) * refs["of"][:, lanes]
                center = jnp.sum(by_head(product), axis=1, keepdims=True)
                do_both = by_head(do)
                scaled_q = by_head(refs["q"][:, lanes] * jnp.asarray(SCALE, BF16))
                scaled_k = refs["k"][:, lanes] * jnp.asarray(SCALE, BF16)
                lifted = refs["p"][2 * i : 2 * i + 2].reshape(2 * count, 4 * count)
                dpw = dot(do_both, refs["v"][:, lanes], ((1,), (1,)))
                ds = (lifted.astype(F32) * (dpw - center)).astype(BF16)
                dq_both = dot(ds, scaled_k)
                lane = lax.broadcasted_iota(jnp.int32, do.shape, 1)
                dq = jnp.where(lane < HEAD, dq_both[:count], dq_both[count:]).astype(BF16)
                dk = dot(scaled_q, ds, ((0,), (0,))).astype(BF16).T
                dv = dot(do_both, lifted, ((0,), (0,))).astype(BF16).T
                here("dq")[:, lanes] = dq
                here("dk")[:, lanes] = dk
                here("dv")[:, lanes] = dv
                sums = [total_rows(dq), total_rows(dv), jnp.zeros((6, PAIR), F32)]
                here("gqv")[:, lanes] = jnp.concatenate(sums, axis=0)

            each_pair(width // PAIR, pair)
            send(*[f"{name}{half}" for name in ("dq", "dk", "dv", "gqv")])
            back = dot(here("dk")[...], wqkv[D : 2 * D, :], ((1,), (1,)))
            back += dot(here("dv")[...], wqkv[2 * D : 3 * D, :], ((1,), (1,)))
            if half == 0:
                dn[...] = back
            else:
                dn[...] += back
            dn[span, :] += dot(here("dq")[...], wqkv[:D, :], ((1,), (1,)))
        at = lambda base, which: pl.ds(pl.multiple_of(base + which * count, count), count)
        mine, other = flags[0], 1 - flags[0]
        get("sent")[:count, :] = dn[at(0, other), :].astype(BF16)
        get("sent")[count:, :] = dn[at(2 * count, other), :].astype(BF16)
        send("sent")
        get("prior")[...] = dn[at(0, mine), :].astype(BF16)
        get("own")[...] = dn[at(2 * count, mine), :]
        send("prior", "own")

    return body


def last_layer(where, vec, weights, rows, dout, dep=None):
    c = Call()
    count = rows.shape[0] // 4
    width = weights[0]["wqkv"].shape[1]
    hidden = weights[0]["wp"].shape[0]
    c.take("vec", vec)
    c.take("rows", rows)
    for name in ("bqv", "wqkv"):
        for half in range(2):
            c.take(f"{name}{half}", weights[half][name])
    for half in range(2):
        for name in ("bfc", "wfc", "wp"):
            c.take(f"{name}{half}", weights[half][name])
    c.take("dout", dout)
    c.give("nrm", (4 * count, D), BF16)
    c.give("nrm2", (count, D), BF16)
    c.give("act", (count, D), BF16)
    c.give("ga", (count, D), BF16)
    c.give("dh1", (count, D), F32)
    c.give("small", (8, D), F32)
    c.give("sent", (2 * count, D), BF16)
    c.give("prior", (count, D), BF16)
    c.give("own", (count, D), F32)
    for half in range(2):
        c.give(f"o{half}", (count, width), BF16)
        c.give(f"u{half}", (count, hidden), BF16)
        c.give(f"df{half}", (count, hidden), BF16)
        c.give(f"gfc{half}", (1, hidden), F32)
        for name, n in (("dq", count), ("dk", 4 * count), ("dv", 4 * count)):
            c.give(f"{name}{half}", (n, width), BF16)
        c.give(f"gqv{half}", (8, width), F32)
    for half in range(2):
        for name, n, kind in (
            ("q", count, BF16), ("k", 4 * count, BF16), ("v", 4 * count, BF16),
            ("of", count, F32), ("rl", count, F32),
        ):
            c.keep(f"{name}{half}", (n, width), kind)
        c.keep(f"p{half}", (2 * width // PAIR, count, 4 * count), BF16)
        c.keep(f"f{half}", (count, hidden), F32)
    c.keep("h1", (count, D), F32)
    c.keep("sum", (count, D), F32)
    c.keep("mask", (count, 4 * count), F32)
    c.keep("dn", (4 * count, D), F32)

    def body(flags, get, send):
        forward_body((0, 1), (0, 1), count, width, hidden, True)(flags, get, send)
        mlp_body(hidden)(flags, get, send)
        attn_body(count, width)(flags, get, send)

    return c.run(body, where, "last_layer", 40, dep)


def norm_kernel(rows, vec, own, mate, later, dh1, low, small):
    back = own[...] + mate[...].astype(F32) + later[...].astype(F32)
    normed, factor = standard(rows[...].astype(F32))
    low[...] = (dh1[...] + norm_back(back, normed, factor, vec[0:1, :])).astype(BF16)
    small[...] = jnp.concatenate(
        [total_rows(back * normed), total_rows(back), jnp.zeros((6, D), F32)], axis=0
    )


class NormBack:
    def __init__(self, rows, vec, back, dh1):
        self.rows, self.vec, self.back, self.dh1 = rows, vec, back, dh1
        self.mate = swap(back["sent"], SECTION)

    def send(self, dep):
        count = self.rows.shape[0]
        prior = sum_rows([self.back["prior"], self.mate[:count]], dep)
        self.later = shift(prior, -1)
        return prior

    def finish(self, dep):
        shape = jax.ShapeDtypeStruct
        extra, extra_specs = after(dep)
        count = self.rows.shape[0]
        operands = [
            self.rows, self.vec, self.back["own"], self.mate[count:], self.later, self.dh1,
        ]

        def kernel(*refs):
            norm_kernel(*refs[: len(operands)], *refs[-2:])

        return pl.pallas_call(
            kernel,
            in_specs=[pl.BlockSpec(memory_space=pltpu.VMEM)] * len(operands) + extra_specs,
            out_shape=[shape(self.dh1.shape, BF16), shape((8, D), F32)],
            name="first_norm_back",
            compiler_params=params(SMALL),
            cost_estimate=lasts(1),
        )(*operands, *extra)


def gather_small(where, norms, mlps, attns, dep):
    halves = [m[f"gfc{i}"] for m in mlps for i in range(2)]
    halves += [a[f"gqv{i}"] for a in attns for i in range(2)]
    operands = list(norms) + [m["small"] for m in mlps] + halves
    extra, extra_specs = after(dep)

    def kernel(flags, norm_a, norm_b, mlp_a, mlp_b, f0, f1, g0, g1, a0, a1, b0, b1, *rest):
        out = rest[-1]
        out[...] = jnp.zeros_like(out)
        out[0:2, :] = norm_a[0:2, :] + norm_b[0:2, :]
        out[2:6, :] = mlp_a[0:4, :] + mlp_b[0:4, :]
        bqv = (a0[0:2, :] + b0[0:2, :], a1[0:2, :] + b1[0:2, :])
        bfc = (f0[...] + g0[...], f1[...] + g1[...])
        for value in range(2):

            @pl.when(flags[2] == value)
            def _():
                out[6:8, :] = jnp.concatenate([bqv[value], bqv[1 - value]], axis=1)
                for place in range(2):
                    row = 8 + 2 * (place if value == 0 else 1 - place)
                    out[row : row + 1, :] = bfc[place][:, :D]
                    out[row + 1 : row + 2, :] = bfc[place][:, D:]

    return pl.pallas_call(
        kernel,
        in_specs=[pl.BlockSpec(memory_space=pltpu.SMEM)]
        + [pl.BlockSpec(memory_space=pltpu.VMEM)] * len(operands)
        + extra_specs,
        out_shape=jax.ShapeDtypeStruct((16, D), F32),
        compiler_params=params(SMALL),
        cost_estimate=lasts(1),
        name="gather_small",
    )(where, *operands, *extra)


class Spread:
    def __init__(self, section, tensor):
        self.section, self.tensor = section, tensor

    def add(self, layers, dep):
        rows, width = layers[0].shape[0], layers[0].shape[1] // 2
        extra, extra_specs = after(dep)

        def kernel(which, a, b, *rest):
            for value in range(2):

                @pl.when(which[0] == value)
                def _():
                    for layer, ref in enumerate((a, b)):
                        rest[-2][layer] = ref[:, value * width : (value + 1) * width]
                        rest[-1][layer] = ref[:, (1 - value) * width : (2 - value) * width]

        shape = jax.ShapeDtypeStruct((2, rows, width), layers[0].dtype)
        self.mine, theirs = pl.pallas_call(
            kernel,
            in_specs=[pl.BlockSpec(memory_space=pltpu.SMEM)]
            + [pl.BlockSpec(memory_space=pltpu.VMEM)] * 2
            + extra_specs,
            out_shape=[shape, shape],
            compiler_params=params(SMALL),
            cost_estimate=lasts(0.7),
            name="spread",
        )(self.tensor.reshape(1), *layers, *extra)
        self.theirs = swap(theirs, TENSOR)
        return self.mine

    def turn(self, dep):
        extra, extra_specs = after(dep)

        def kernel(which, a, b, *rest):
            for section in range(2):
                for tensor in range(2):

                    @pl.when((which[0] == section) & (which[1] == tensor))
                    def _():
                        for out, layer in ((rest[-2], section), (rest[-1], 1 - section)):
                            out[tensor] = a[layer]
                            out[1 - tensor] = b[layer]

        shape = jax.ShapeDtypeStruct(self.mine.shape, self.mine.dtype)
        self.kept, sent = pl.pallas_call(
            kernel,
            in_specs=[pl.BlockSpec(memory_space=pltpu.SMEM)]
            + [pl.BlockSpec(memory_space=pltpu.VMEM)] * 2
            + extra_specs,
            out_shape=[shape, shape],
            compiler_params=params(SMALL),
            cost_estimate=lasts(0.7),
            name="turn",
        )(jnp.stack([self.section, self.tensor]), self.mine, self.theirs, *extra)
        self.mate = swap(sent, SECTION)
        return self.kept

    def finish(self, kind, dep):
        _, rows, width = self.kept.shape
        extra, extra_specs = after(dep)

        def kernel(which, mine, mate, *rest):
            out = rest[-1]
            for value in range(2):

                @pl.when(which[0] == value)
                def _():
                    for micro in range(2):
                        here = slice(value * rows, (value + 1) * rows)
                        there = slice((1 - value) * rows, (2 - value) * rows)
                        out[micro, here, :] = mine[micro].astype(kind)
                        out[micro, there, :] = mate[micro].astype(kind)

        return pl.pallas_call(
            kernel,
            in_specs=[pl.BlockSpec(memory_space=pltpu.SMEM)]
            + [pl.BlockSpec(memory_space=pltpu.VMEM)] * 2
            + extra_specs,
            out_shape=jax.ShapeDtypeStruct((2, 2 * rows, width), kind),
            compiler_params=params(SMALL),
            cost_estimate=lasts(1),
            name="spread_out",
        )(self.section.reshape(1), self.kept, self.mate, *extra)


def pack_vectors(vectors, qv_bias, fc_bias):
    half = vectors[0].shape[0]
    more = fc_bias.shape[0] // half

    def kernel(*refs):
        out = refs[-1]
        out[...] = jnp.zeros_like(out)
        for i in range(len(vectors)):
            out[i : i + 1, :] = refs[i][...].astype(F32)
        out[6:8, :] = refs[-3][...].astype(F32)
        for i in range(more):
            out[8 + i : 9 + i, :] = refs[-2][:, i * half : (i + 1) * half].astype(F32)

    return pl.pallas_call(
        kernel,
        out_shape=jax.ShapeDtypeStruct((16, half), F32),
        compiler_params=params(SMALL),
        cost_estimate=lasts(1),
        name="pack_vectors",
    )(*[v.reshape(1, half) for v in vectors], qv_bias, fc_bias.reshape(1, -1))


def unpack_vectors(tensor, mine, other):
    half = mine.shape[1]

    def kernel(which, a, b, vec, bqv0, bqv1, bfc0, bfc1):
        for value in range(2):

            @pl.when(which[0] == value)
            def _():
                order = (a, b) if value == 0 else (b, a)
                vec[:, :half] = order[0][0:8, :]
                vec[:, half:] = order[1][0:8, :]

        for ref, bqv, bfc in ((a, bqv0, bfc0), (b, bqv1, bfc1)):
            bqv[...] = ref[6:8, :]
            for i in range(4):
                bfc[:, i * half : (i + 1) * half] = ref[8 + i : 9 + i, :]

    shape = lambda *s: jax.ShapeDtypeStruct(s, F32)
    pair = [shape(2, half)] * 2 + [shape(1, 4 * half)] * 2
    return pl.pallas_call(
        kernel,
        in_specs=[pl.BlockSpec(memory_space=pltpu.SMEM)]
        + [pl.BlockSpec(memory_space=pltpu.VMEM)] * 2,
        out_shape=[shape(8, 2 * half)] + pair,
        compiler_params=params(SMALL),
        cost_estimate=lasts(1),
        name="unpack_vectors",
    )(tensor.reshape(1), mine, other)


def assemble(where, own, arrived, mate):
    count = arrived.shape[0] // 3
    half = own.shape[1]

    def kernel(which, own_ref, arrived_ref, mate_ref, out, mine):
        for section in range(2):
            for tensor in range(2):

                @pl.when((which[0] == section) & (which[2] == tensor))
                def _():
                    here = slice(tensor * half, (tensor + 1) * half)
                    there = slice((1 - tensor) * half, (2 - tensor) * half)
                    out[2 * count :, here] = own_ref[...]
                    for place in range(2):
                        ref = arrived_ref if place == section else mate_ref
                        rows = slice(place * count, (place + 1) * count)
                        later = slice((2 + place) * count, (3 + place) * count)
                        out[later, there] = ref[:count, :]
                        out[rows, here] = ref[count : 2 * count, :]
                        out[rows, there] = ref[2 * count :, :]
                    rows = slice((2 + section) * count, (3 + section) * count)
                    mine[...] = out[rows, :]

    return pl.pallas_call(
        kernel,
        in_specs=[pl.BlockSpec(memory_space=pltpu.SMEM)]
        + [pl.BlockSpec(memory_space=pltpu.VMEM)] * 3,
        out_shape=[
            jax.ShapeDtypeStruct((4 * count, 2 * half), BF16),
            jax.ShapeDtypeStruct((count, 2 * half), BF16),
        ],
        compiler_params=params(SMALL),
        cost_estimate=lasts(1),
        name="assemble",
    )(where, own, arrived, mate)


def gather_rows(own):
    section = lax.axis_index(SECTION)
    mate = swap(own, SECTION)
    prior_mine = shift(own, 1)
    prior_mate = swap(prior_mine, SECTION)
    first = section == 0
    pick = lambda a, b: [jnp.where(first, a, b), jnp.where(first, b, a)]
    return jnp.concatenate(pick(prior_mine, prior_mate) + pick(own, mate), axis=0)


def join_features(tensor, mine, other, dep):
    rows, half = mine.shape
    extra, extra_specs = after(dep)

    def kernel(which, a, b, *rest):
        for value in range(2):

            @pl.when(which[0] == value)
            def _():
                rest[-1][:, value * half : (value + 1) * half] = a[...]
                rest[-1][:, (1 - value) * half : (2 - value) * half] = b[...]

    return pl.pallas_call(
        kernel,
        in_specs=[pl.BlockSpec(memory_space=pltpu.SMEM)]
        + [pl.BlockSpec(memory_space=pltpu.VMEM)] * 2
        + extra_specs,
        out_shape=jax.ShapeDtypeStruct((rows, 2 * half), mine.dtype),
        compiler_params=params(SMALL),
        cost_estimate=lasts(0.7),
        name="join_features",
    )(tensor.reshape(1), mine, other, *extra)


def local(
    inputs,
    out_grads,
    seq_blocks,
    ln1_gain,
    ln1_shift,
    qkv_weight,
    qv_bias,
    out_weight,
    out_bias,
    ln2_gain,
    ln2_shift,
    fc_weight,
    fc_bias,
    proj_weight,
    proj_bias,
):
    section = lax.axis_index(SECTION)
    position = lax.axis_index("dp")
    tensor = lax.axis_index(TENSOR)
    half = D // 2
    block = inputs.shape[1]
    count = block // 2
    hidden = fc_weight.shape[1]
    first = tensor == 0

    def features(mine, other):
        return ordered(first, mine, other, mine.ndim - 1)

    micro = lambda a, which: lax.dynamic_index_in_dim(a, which, 0, keepdims=False)
    starts = jnp.cumsum(seq_blocks, axis=1) - seq_blocks
    continuing = jnp.logical_not(jnp.any(starts == position, axis=1))
    continues = micro(continuing, tensor)
    where = jnp.stack([section, continues.astype(jnp.int32), tensor])

    own_rows = lambda a, which: part(micro(a, which), section, 2)
    here, there = own_rows(inputs, tensor), own_rows(inputs, 1 - tensor)
    count_dp = lax.axis_size("dp")
    ahead = [(2 * i + j, 2 * i + 2 + 1 - j) for i in range(count_dp - 1) for j in range(2)]
    across = swap(there, TENSOR)
    before_here = shift(here, 1)
    before_there = lax.ppermute(there, ("dp", TENSOR), ahead)
    arrived = jnp.concatenate([across, before_here, before_there], axis=0)
    mate = swap(arrived, SECTION)
    rows_one, mine = assemble(where, micro(inputs, tensor), arrived, mate)
    vectors = pack_vectors(
        [ln1_gain, ln1_shift, out_bias, ln2_gain, ln2_shift, proj_bias], qv_bias, fc_bias
    )
    other_vectors = swap(vectors, TENSOR)
    vec, *biases = unpack_vectors(tensor, vectors, other_vectors)
    head_weights = [qkv_weight[:, n] for n in range(3)] + [out_weight[:, :half], out_weight[:, half:]]
    head_weights = jnp.concatenate(head_weights, axis=0)
    fetch_heads = Fetch(head_weights, 1, 2)
    fetch_fc, fetch_proj = Fetch(fc_weight, 2), Fetch(proj_weight, 1)
    weights = [
        dict(wqkv=head_weights, wfc=fc_weight, wp=proj_weight),
        {},
    ]
    for half_index in range(2):
        weights[half_index].update(bqv=biases[half_index], bfc=biases[2 + half_index])
    dep = fetch_heads.start([across, before_here, before_there, other_vectors])
    fetch_heads.pass_on()
    dep = fetch_fc.start(dep)
    dep = fetch_proj.start(dep)
    one = forward_part(where, vec, weights, (0,), (), rows=rows_one, dep=dep)
    dep = fetch_heads.join(one["sum"])
    dep = fetch_heads.finish(dep)
    dep = fetch_fc.pass_on(dep)
    dep = fetch_proj.pass_on(dep)
    weights[1].update(wqkv=fetch_heads.whole)
    one_b = forward_part(
        where, vec, weights, (1,), (0,), nrm=one["nrm"], carried=one["sum"], dep=dep
    )
    other = swap(own_rows(out_grads, 1 - tensor), TENSOR)
    dep = dout = join_features(tensor, own_rows(out_grads, tensor), other, one_b["sum"])
    dep = fetch_fc.join(dep)
    dep = fetch_proj.join(dep)
    dep = fetch_fc.finish(dep)
    dep = fetch_proj.finish(dep)
    weights[1].update(wfc=fetch_fc.whole, wp=fetch_proj.whole)
    one_c = forward_part(
        where, vec, weights, (), (1,), nrm2=one_b["nrm2"], carried=one_b["sum"], dep=dep
    )
    one = {**one, **one_b, **one_c}
    two = last_layer(where, vec, weights, gather_rows(one["act"]), dout)
    norm_two = NormBack(one["act"], vec, two, two["dh1"])
    dep = norm_two.send(two["prior"])
    layers = [[two, two, two, dout], [one, None, None, None]]
    flat = lambda s, piece: (0, 0)
    by_piece = lambda s, piece: (0, piece)
    own_piece = lambda s, piece: (2 + s, piece)
    square, tall, narrow, thin = (count, D), (4 * count, half), (count, half), (4 * count, half)

    def proj_terms(i):
        return [[(f[f"u{i}"], square, by_piece, g, square, flat) for f, _, _, g in layers]]

    def fc_terms(i):
        return [
            [(f["nrm2"], square, flat, m[f"df{i}"], square, by_piece) for f, m, _, _ in layers]
        ]

    def attn_terms(i):
        return [
            [(f["nrm"], narrow, own_piece, a[f"dq{i}"], narrow, flat) for f, _, a, _ in layers if a],
            [(f["nrm"], tall, by_piece, a[f"dk{i}"], thin, flat) for f, _, a, _ in layers if a],
            [(f["nrm"], tall, by_piece, a[f"dv{i}"], thin, flat) for f, _, a, _ in layers if a],
            [(f[f"o{i}"], narrow, flat, m["ga"], narrow, by_piece) for f, m, a, _ in layers if a],
        ]

    proj, fc = Reduction(where, proj_terms), Reduction(where, fc_terms)
    attn = Reduction(where, attn_terms, True)
    dep = attn.first_layer(dep)
    low_two, small_two = norm_two.finish(dep)
    layers[1][3] = low_two
    dep = proj.theirs_foreign(low_two)
    dep = proj.theirs_own(dep)
    dep = proj.foreign(dep)
    mlp_one = layers[1][1] = backward_mlp(vec, weights, one, low_two, where, dep)
    dep = proj.own(mlp_one["ga"])
    dep = fc.theirs_foreign(dep)
    dep = fc.theirs_own(dep)
    dep = fc.foreign(dep)
    dep = fc.own(dep)
    dep = proj.split(dep)
    attn_one = layers[1][2] = backward_attn(where, weights, one, mlp_one["ga"], dep)
    norm_one = NormBack(mine, vec, attn_one, mlp_one["dh1"])
    sums = grads = None
    low_one, small_one = None, None
    levels = 0
    while 2 ** (levels + 1) < count_dp:
        levels += 1
    dep = attn.theirs_foreign(attn_one["own"])
    dep = attn.theirs_own(dep)
    dep = proj.split(dep)
    dep = attn.foreign(dep)
    dep = fc.split(dep)
    dep = norm_one.send(dep)
    for level in range(1, levels):
        dep = proj.split(dep)
    dep = attn.own(dep)
    dep = proj.sum(dep)
    dep = fc.split(dep)
    low_one, small_one = norm_one.finish(dep)
    norms, mlps, attns = (small_one, small_two), (mlp_one, two), (attn_one, two)
    dep = gather_small(where, norms, mlps, attns, low_one)
    sums = SmallSum(dep)
    for level in range(1, levels):
        dep = proj.join(dep)
    dep = attn.split(dep)
    acts, grads = Spread(section, tensor), Spread(section, tensor)
    dep = acts.add([one["act"], two["act"]], dep)
    dep = grads.add([low_one, low_two], dep)
    dep = sums.step(dep)
    for level in range(1, levels):
        dep = fc.split(dep)
        dep = sums.step(dep)
    dep = attn.split(dep)
    dep = fc.sum(dep)
    dep = proj.join(dep)
    for level in range(1, levels):
        dep = attn.split(dep)
        dep = fc.join(dep)
        dep = sums.step(dep)
    dep = attn.sum(dep)
    dep = fc.join(dep)
    dep = proj.join(dep)
    dep = sums.step(dep)
    dep = attn.join(dep)
    dep = acts.turn(dep)
    dep = grads.turn(dep)
    row_steps = 2
    take = lambda i, size: slice(i * size, (i + 1) * size)

    def place_proj(core):
        size = hidden // 2 // row_steps
        return [
            (take(i, size), (take(core * row_steps + i, size), slice(0, D)))
            for i in range(row_steps)
        ]

    def place_fc(core):
        size = D // row_steps
        return [(take(i, size), (take(i, size), take(core, D))) for i in range(row_steps)]

    def place_out(core):
        return [(take(3, half), (slice(0, half), take(core, half)))]

    proj_grad, dep = widen(section, proj.kept, proj.other, (hidden, D), place_proj, dep)
    for level in range(1, levels):
        dep = attn.join(dep)
    dep = sums.step(dep)
    dep = fc.join(dep)
    fc_grad, dep = widen(section, fc.kept, fc.other, (D, hidden), place_fc, dep)
    dep = acts_out = acts.finish(BF16, dep)
    dep = grads_out = grads.finish(F32, dep)
    dep = attn.join(dep)

    while sums.other is not None:
        dep = sums.step(dep)
    out_grad, _ = widen(section, attn.kept, attn.other, (half, D), place_out, dep)
    assert proj.bit == fc.bit == attn.bit == 0
    sides = lambda n: [a[n * half : (n + 1) * half] for a in (attn.kept, attn.other)]
    qkv_grad = jnp.stack([ordered(section == 0, *sides(n), 0) for n in range(3)], axis=1)
    qkv_grad = qkv_grad.astype(F32)
    rows_here = part(sums.array[:8], tensor, 2, 1)
    bfc_grad = part(sums.array[8:12], tensor, 2).reshape(hidden)
    return (
        acts_out[None],
        grads_out[None],
        rows_here[0],
        rows_here[1],
        qkv_grad,
        rows_here[6:8],
        out_grad,
        rows_here[4],
        rows_here[2],
        rows_here[3],
        fc_grad,
        bfc_grad,
        proj_grad,
        rows_here[5],
    )


def solution(mesh):
    in_specs = (
        P(None, "dp", TENSOR),
        P(None, "dp", TENSOR),
        P(),
        P(TENSOR),
        P(TENSOR),
        P(None, None, TENSOR),
        P(None, TENSOR),
        P(TENSOR, None),
        P(TENSOR),
        P(TENSOR),
        P(TENSOR),
        P(None, TENSOR),
        P(TENSOR),
        P(TENSOR, None),
        P(TENSOR),
    )
    out_specs = (
        P(SECTION, None, "dp", TENSOR),
        P(SECTION, None, "dp", TENSOR),
        P(TENSOR),
        P(TENSOR),
        P(None, None, TENSOR),
        P(None, TENSOR),
        P(TENSOR, None),
        P(TENSOR),
        P(TENSOR),
        P(TENSOR),
        P(None, TENSOR),
        P(TENSOR),
        P(TENSOR, None),
        P(TENSOR),
    )
    return jax.shard_map(local, mesh=mesh, in_specs=in_specs, out_specs=out_specs, check_vma=False)
```
